32 devices in a mesh: seq: 4 (over y, core), batch: 8 (over z, x).
Axes of the slice: x: 2, y: 2, z: 4, core: 2. Of those that a mesh axis runs over, the one named last changes fastest.
Arguments:
- inputs: bfloat16 [24, 512, 768], P('batch', 'seq'), may hold values from -6 to 6
- cotangent: bfloat16 [24, 512, 768], P('batch', 'seq'), may hold values from -6 to 6
- segment_ids: int32 [24, 512], P('batch', 'seq'), may hold values from 0 to 2, as said below
- bucket_table: int32 [1023], replicated, may hold values from 0 to 31
- position_bias: float32 [32, 12], replicated, may hold values from -4 to 4
- query_weight: bfloat16 [768, 768], replicated, may hold values from -0.109375 to 0.109375
- key_weight: bfloat16 [768, 768], replicated, may hold values from -0.109375 to 0.109375
- value_weight: bfloat16 [768, 768], replicated, may hold values from -0.21875 to 0.21875
- out_weight: bfloat16 [768, 768], replicated, may hold values from -0.875 to 0.875
- hidden_in: bfloat16 [768, 3072], replicated, may hold values from -0.21875 to 0.21875
- hidden_out: bfloat16 [3072, 768], replicated, may hold values from -0.109375 to 0.109375
- gain_first: float32 [768], replicated, may hold values from 0.1 to 1.9
- gain_second: float32 [768], replicated, may hold values from 0.1 to 1.9
- shared: float32 [4, 4, 4], replicated, may hold values from -4 to 4
- down_left: float32 [4, 192], replicated, may hold values from -0.4 to 0.4
- down_right: float32 [4, 12], replicated, may hold values from -2.5 to 2.5
- up_left_vectors: float32 [4, 12], replicated, may hold values from -1.5 to 1.5
- up_right: float32 [4, 192], replicated, may hold values from -0.8 to 0.8
- bias_down: float32 [48], replicated, may hold values from -2.5 to 2.5
- bias_up: float32 [768], replicated, may hold values from -2.5 to 2.5
Outputs:
- output: bfloat16 [24, 512, 768], P('batch', 'seq')
- grad_input: bfloat16 [24, 512, 768], P('batch', 'seq')
- grad_gain_first: float32 [768], replicated
- grad_gain_second: float32 [768], replicated
- grad_shared: float32 [4, 4, 4], replicated
- grad_down_left: float32 [4, 192], replicated
- grad_down_right: float32 [4, 12], replicated
- grad_up_left: float32 [4, 12], replicated
- up_right_gradient: float32 [4, 192], replicated
- grad_bias_down: float32 [48], replicated
- grad_bias_up: float32 [768], replicated
The draws below stay inside these ranges and needn't reach their ends.
Inputs may be any that keep to these rules, and one draw needn't show every extreme that they name: `segment_ids`: in each row the ids never fall; id 1 runs from a position under 512 // 8 past position 448, ids 0 and 2 fill the two ends, both present.
All inputs are finite; a program needn't handle non-finite values.
Results may differ from the reference program's by a relative error of at most 0.04.
Values may be sent and summed in bfloat16 or wider, within the bound.
No kernel may reach another device: no remote copies, remote signals or barrier semaphores. Data moves between devices by JAX's collectives and lax.ppermute only.
A program may use at most 128 MiB of HBM per device.

```python
import jax
import jax.numpy as jnp
from jax import lax

D = 768
H = 12
FF = 3072
NB = 32
AD = 48
PN = 4
LEN = 512
ROWS = 24


def draw_segment_ids(key, part):
    key = jax.random.fold_in(key, 7)
    begin_key, finish_key = jax.random.split(key)
    opening = jax.random.randint(begin_key, (ROWS, 1), 1, LEN // 8)
    closing = jax.random.randint(finish_key, (ROWS, 1), LEN - LEN // 8 + 1, LEN)
    places = jnp.arange(LEN, dtype=jnp.int32)[None, :]
    return (places >= opening).astype(jnp.int32) + (places >= closing).astype(jnp.int32)


def place_ends(entries, rng, least, largest):
    place = [jax.random.randint(jax.random.fold_in(rng, axis), (), 0, length) for axis, length in enumerate(entries.shape)]
    widest = entries.shape.index(max(entries.shape))
    neighbour = place[:widest] + [(place[widest] + 1) % entries.shape[widest]] + place[widest + 1:]
    return entries.at[tuple(place)].set(least).at[tuple(neighbour)].set(largest)


def block_scale(rng, extent, cuts, least, largest):
    loudness = 1.0
    for axis_at, parts in cuts:
        heights = jax.random.uniform(jax.random.fold_in(jax.random.fold_in(rng, 6), axis_at), (parts,), jnp.float32, least / len(cuts), largest / len(cuts))
        loudness = loudness * jnp.repeat(jnp.exp(heights), extent[axis_at] // parts).reshape((-1,) + (1,) * (len(extent) - 1 - axis_at))
    return loudness


def noise(stream_key, extent, deviation, most, cuts=(), kind=jnp.bfloat16):
    drawn = deviation * jax.random.normal(stream_key, extent, jnp.float32)
    if cuts:
        drawn = drawn * block_scale(stream_key, extent, cuts, -0.22, 0.18)
    return jnp.clip(drawn, -most, most).astype(kind)


def setup_inputs(seed: int = 0) -> dict:
    arg_keys = jax.random.split(jax.random.key(seed), 21)
    return {
        "inputs": noise(arg_keys[0], (ROWS, LEN, D), 1.0, 6.0, ((0, 8), (1, 4))),
        "cotangent": noise(arg_keys[1], (ROWS, LEN, D), 1.0, 6.0, ((0, 8), (1, 4))),
        "segment_ids": draw_segment_ids(jax.random.fold_in(arg_keys[20], 71), 0),
        "bucket_table": place_ends(jax.random.randint(arg_keys[3], (2 * LEN - 1,), 0, NB), jax.random.fold_in(arg_keys[3], 1), 0, NB - 1).astype(jnp.int32),
        "position_bias": noise(arg_keys[4], (NB, H), 1.0, 4.0, (), jnp.float32),
        "query_weight": noise(arg_keys[5], (D, D), (4 * D) ** -0.5, 0.109375),
        "key_weight": noise(arg_keys[6], (D, D), (4 * D) ** -0.5, 0.109375),
        "value_weight": noise(arg_keys[7], (D, D), D ** -0.5, 0.21875),
        "out_weight": noise(arg_keys[8], (D, D), (D // 16) ** -0.5, 0.875),
        "hidden_in": noise(arg_keys[9], (D, FF), D ** -0.5, 0.21875),
        "hidden_out": noise(arg_keys[10], (FF, D), FF ** -0.5, 0.109375),
        "gain_first": jnp.clip(1.0 + 0.18 * jax.random.normal(arg_keys[11], (D,), jnp.float32), 0.1, 1.9),
        "gain_second": jnp.clip(1.0 + 0.18 * jax.random.normal(arg_keys[12], (D,), jnp.float32), 0.1, 1.9),
        "shared": noise(arg_keys[13], (PN, PN, PN), 1.0, 4.0, (), jnp.float32),
        "down_left": noise(arg_keys[14], (PN, D // PN), 0.072, 0.4, (), jnp.float32),
        "down_right": noise(arg_keys[15], (PN, AD // PN), 0.5, 2.5, (), jnp.float32),
        "up_left_vectors": noise(arg_keys[16], (PN, AD // PN), 0.3, 1.5, (), jnp.float32),
        "up_right": noise(arg_keys[17], (PN, D // PN), 0.15, 0.8, (), jnp.float32),
        "bias_down": noise(arg_keys[18], (AD,), 0.5, 2.5, (), jnp.float32),
        "bias_up": noise(arg_keys[19], (D,), 0.5, 2.5, (), jnp.float32),
    }


@jax.custom_vjp
def low(v):
    return lax.optimization_barrier(v.astype(jnp.bfloat16)).astype(jnp.float32)

@jax.custom_vjp
def low_back(v):
    return v

def low_keep(v):
    return (low(v), None)

def low_pass(kept, grad):
    return (grad,)

def back_keep(v):
    return (v, None)

def back_low(kept, grad):
    return (low(grad),)
low.defvjp(low_keep, low_pass)
low_back.defvjp(back_keep, back_low)
epsilon = 1e-06
masked_score = -1e+30
highest_precision = lax.Precision.HIGHEST

def matmul_high(left, right):
    return jnp.dot(left, right, precision=highest_precision, preferred_element_type=jnp.float32)

def rms_scale(values, gain):
    return values * lax.rsqrt(lax.optimization_barrier(jnp.mean(values * values, -1, keepdims=True)) + epsilon) * gain

def adapter(branch, shared, down_left, down_right, up_left_vectors, up_right, bias_down, bias_up):
    count_rows = branch.shape[0]
    factors = shared.shape[0]
    blocks = branch.reshape(count_rows, factors, down_left.shape[1])
    projected = jnp.einsum('tab,ib->tia', blocks, down_left, precision=highest_precision)
    mixed = jnp.einsum('tia,iac->tic', projected, shared, precision=highest_precision)
    lowered = jnp.einsum('tic,ij->tcj', mixed, down_right, precision=highest_precision)
    bottleneck = jax.nn.gelu(lowered.reshape(count_rows, -1) + bias_down)
    folded_together = bottleneck.reshape(count_rows, factors, up_left_vectors.shape[1])
    backward_projection = jnp.einsum('orj,gj->ogr', folded_together, up_left_vectors, precision=highest_precision)
    remixed = jnp.einsum('tia,iab->tib', backward_projection, shared, precision=highest_precision)
    raised = jnp.einsum('tib,ij->tbj', remixed, up_right, precision=highest_precision)
    return raised.reshape(count_rows, -1) + bias_up

def layer(values, segments, frozen, trainable):
    query_weight, key_weight, value_weight, out_weight, hidden_in, hidden_out, position_table = frozen
    gain_first, gain_second, shared, down_left, down_right, up_left_vectors, up_right, bias_down, bias_up = trainable
    rows_per_group, length, model_dim = values.shape
    head_count = position_table.shape[0]
    flat_rows = values.reshape(rows_per_group * length, model_dim)
    normed = low(rms_scale(flat_rows, gain_first))
    queries = low_back(low(matmul_high(normed, query_weight))).reshape(rows_per_group, length, head_count, -1)
    key_heads = low_back(low(matmul_high(normed, key_weight))).reshape(rows_per_group, length, head_count, -1)
    value_heads = low_back(low(matmul_high(normed, value_weight))).reshape(rows_per_group, length, head_count, -1)
    scores = jnp.einsum('gqhe,gkhe->ghqk', queries, key_heads, precision=highest_precision) + position_table[None]
    scores = low_back(scores)
    same_doc = (segments[:, :, None] == segments[:, None, :])[:, None]
    scores = jnp.where(same_doc, scores, masked_score)
    row_peak = lax.optimization_barrier(jnp.max(scores, -1, keepdims=True))
    log_total = row_peak + jnp.log(lax.optimization_barrier(jnp.sum(jnp.exp(scores - row_peak), -1, keepdims=True)))
    weights = low(jnp.exp(scores - log_total))
    context = jnp.einsum('ghqk,gkhe->gqhe', weights, value_heads, precision=highest_precision)
    context = low_back(low(context.reshape(rows_per_group * length, model_dim)))
    hidden_state = flat_rows + low_back(matmul_high(context, out_weight))
    normed_two = low(rms_scale(hidden_state, gain_second))
    pre_gelu = low_back(matmul_high(normed_two, hidden_in))
    activated = low(jax.nn.gelu(pre_gelu))
    branch = low_back(matmul_high(activated, hidden_out))
    result = hidden_state + branch + adapter(branch, shared, down_left, down_right, up_left_vectors, up_right, bias_down, bias_up)
    return result.reshape(rows_per_group, length, model_dim)

def reference(inputs, cotangent, segment_ids, bucket_table, position_bias, query_weight, key_weight, value_weight, out_weight, hidden_in, hidden_out, gain_first, gain_second, shared, down_left, down_right, up_left_vectors, up_right, bias_down, bias_up):
    positions = jnp.arange(LEN, dtype=jnp.int32)
    offsets = positions[None, :] - positions[:, None] + LEN - 1
    position_table = jnp.transpose(position_bias[bucket_table[offsets]], (2, 0, 1))
    frozen = (query_weight.astype(jnp.float32), key_weight.astype(jnp.float32), value_weight.astype(jnp.float32), out_weight.astype(jnp.float32), hidden_in.astype(jnp.float32), hidden_out.astype(jnp.float32), position_table)
    trainable = (gain_first, gain_second, shared, down_left, down_right, up_left_vectors, up_right, bias_down, bias_up)
    group_count = ROWS // 4
    stacked_in = inputs.astype(jnp.float32).reshape(group_count, 4, LEN, D)
    stacked_cotangent = cotangent.astype(jnp.float32).reshape(group_count, 4, LEN, D)
    stacked_seg = segment_ids.reshape(group_count, 4, LEN)

    def one_group(totals, group_item):
        block_in, block_cot, block_seg = group_item

        def apply_layer(block_values, params):
            return layer(block_values, block_seg, frozen, params)
        result, pullback = jax.vjp(apply_layer, block_in, trainable)
        input_grad, param_grads = pullback(block_cot)
        totals = jax.tree.map(jnp.add, totals, param_grads)
        return (totals, (result.astype(jnp.bfloat16), input_grad.astype(jnp.bfloat16)))
    zero_grads = jax.tree.map(jnp.zeros_like, trainable)
    totals, (outputs, input_grads) = lax.scan(one_group, zero_grads, (stacked_in, stacked_cotangent, stacked_seg))
    return (outputs.reshape(ROWS, LEN, D), input_grads.reshape(ROWS, LEN, D), totals[0], totals[1], totals[2], totals[3], totals[4], totals[5], totals[6], totals[7], totals[8])
```

```python
import functools

import jax
import jax.numpy as jnp
from jax import lax
from jax.experimental import pallas as pl
from jax.experimental.pallas import tpu as pltpu
from jax.sharding import PartitionSpec as P

F32 = jnp.float32
BF16 = jnp.bfloat16
epsilon = 1e-06
masked = -1e30
gelu_a = 0.7978845608028654
gelu_b = 0.044715
MIB = 1024 * 1024


def dot(a, b, precision=None):
    return lax.dot_general(a, b, (((1,), (0,)), ((), ())), precision=precision, preferred_element_type=F32)


def dot_nt(a, b, precision=None):
    return lax.dot_general(a, b, (((1,), (1,)), ((), ())), precision=precision, preferred_element_type=F32)


def dot_tn(a, b, precision=None):
    return lax.dot_general(a, b, (((0,), (0,)), ((), ())), precision=precision, preferred_element_type=F32)


HI = lax.Precision.HIGHEST


def iota(shape, axis):
    return lax.broadcasted_iota(jnp.int32, shape, axis)


def block_of(index, size, count):
    total = jnp.zeros_like(index)
    for k in range(1, count):
        total = total + (index >= k * size).astype(jnp.int32)
    return total


def gelu_pair(v):
    square = v * v
    h = 0.5 + 0.5 * jnp.tanh(v * (gelu_a + gelu_a * gelu_b * square))
    g = v * h
    slope = h + (g - g * h) * (2.0 * gelu_a + 6.0 * gelu_a * gelu_b * square)
    return g, slope


def inverse_rms(x):
    return lax.rsqrt(jnp.mean(x * x, -1, keepdims=True) + epsilon)


def main_kernel(dims, *refs):
    rows, shard, width, heads, hidden, parts, ranks, mid = dims
    names = (
        "own", "sib", "rown", "rsib", "cot", "seg_own", "seg_sib", "seg_rown", "seg_rsib", "table", "bias", "wq",
        "wk", "wv", "wo", "win", "wout", "gain1", "gain2", "shared", "dl", "dr", "ul", "ur", "bd", "bu", "out",
        "own_part", "sib_part", "rsib_part", "rown_part", "hidden_grad", "pack", "xs", "xn", "ks", "vs", "kf", "q", "qt", "e",
        "bias_rows", "ctx", "ctx_low", "rinv", "hid", "hid_low", "gslope", "dctx", "dq", "dkt", "dvt", "cots", "wqv",
        "wkv", "wvv", "wov", "winv", "woutv", "tab", "sh16", "sh16t", "work", "act", "sems",
    )
    n = dict(zip(names, refs, strict=True))
    (own, sib, rown, rsib, cot) = (n[k] for k in ("own", "sib", "rown", "rsib", "cot"))
    xs, xn, ks, vs, kf, q, qt, e = (n[k] for k in ("xs", "xn", "ks", "vs", "kf", "q", "qt", "e"))
    bias_rows, ctx, ctx_low, rinv = (n[k] for k in ("bias_rows", "ctx", "ctx_low", "rinv"))
    hid, hid_low, gslope, dctx, dq, dkt, dvt = (n[k] for k in ("hid", "hid_low", "gslope", "dctx", "dq", "dkt", "dvt"))
    sems, pack, act = n["sems"], n["pack"], n["act"]
    pairs = heads // 2
    lanes = width // pairs
    half = lanes // 2
    keys = shard * parts
    tokens = rows * shard
    place = lax.axis_index("seq")

    copies = []

    def fetch(source, target):
        c = pltpu.make_async_copy(source, target, sems.at[len(copies)])
        c.start()
        copies.append(c)
        return c

    x_copies = [
        fetch(block, xs.at[:, pl.ds(k * shard, shard), :]) for k, block in enumerate((own, sib, rown, rsib))
    ]
    w_copies = {
        k: fetch(n[k], n[k + "v"]) for k in ("wq", "wk", "wv", "wo", "win", "wout")
    }
    cot_copy = fetch(cot, n["cots"])

    hits = (n["table"][...][None, :] == iota((n["bias"].shape[0], n["table"].shape[0]), 0)).astype(F32)
    n["tab"][0:heads, 0 : n["table"].shape[0]] = dot_tn(n["bias"][...], hits, HI)
    for k in range(parts):
        other = jnp.bitwise_xor(place, k)
        start = pl.multiple_of((other - place + parts - 1) * shard, shard)
        for h in range(heads):
            line = n["tab"][h : h + 1, pl.ds(start, 2 * shard)]
            turned = pltpu.roll(
                jnp.broadcast_to(line, (shard, 2 * shard)), shard + 1, 1, stride=1, stride_axis=0
            )
            bias_rows[h // 2, (h % 2) * shard : (h % 2 + 1) * shard, k * shard : (k + 1) * shard] = turned[:, :shard]

    lane = iota((shard, lanes), 1)
    query_feature = []
    for r in range(rows):
        for k, ids in enumerate((n["seg_own"], n["seg_sib"], n["seg_rown"], n["seg_rsib"])):
            line = jnp.broadcast_to(ids[r : r + 1, :].astype(F32), (lanes, shard))
            seg = jnp.transpose(line)
            same = lane.astype(F32) == seg
            kf[r, k * shard : (k + 1) * shard, :] = same.astype(F32).astype(BF16)
            if k == 0:
                n["work"][r, :, :] = jnp.where((lane < 3) & jnp.logical_not(same), masked, 0.0).astype(BF16)

    mixes = adapter_setup(n, ranks, mid, width)

    for k, c in enumerate(x_copies):
        c.wait()
        for r in range(rows):
            x = xs[r, k * shard : (k + 1) * shard, :].astype(F32)
            xn[r, k * shard : (k + 1) * shard, :] = (x * inverse_rms(x) * n["gain1"][...][None, :]).astype(BF16)

    step = 2 * lanes
    for key in ("wq", "wk", "wv"):
        w_copies[key].wait()

    for t in range(width // step):
        cols = slice(t * step, (t + 1) * step)
        for r in range(rows):
            block = xn[r]
            kk = dot(block, n["wkv"][:, cols]).astype(BF16)
            vv = dot(block, n["wvv"][:, cols]).astype(BF16)
            qq = dot(block[:shard], n["wqv"][:, cols]).astype(BF16)
            for s in range(2):
                part = slice(s * lanes, (s + 1) * lanes)
                ks[2 * t + s, r] = kk[:, part]
                vs[2 * t + s, r] = vv[:, part]
                q[2 * t + s, r] = qq[:, part]
                qt[2 * t + s, r] = jnp.transpose(qq[:, part])

    low_half = iota((1, lanes), 1) < half
    low_lane = low_half.astype(F32).astype(BF16)
    high_lane = 1.0 - low_lane
    low_row = (iota((lanes, 1), 0) < half).astype(F32).astype(BF16)
    high_row = 1.0 - low_row
    ones = jnp.ones((keys, lanes), BF16)

    def forward(index):
        r, p = index // pairs, index % pairs
        qq = q[p, r]
        feature = n["work"][r]
        left = jnp.concatenate(
            [
                jnp.concatenate([qq * low_lane, feature], 1),
                jnp.concatenate([qq * high_lane, feature], 1),
            ],
            0,
        )
        right = jnp.concatenate([ks[p, r], kf[r]], 1)
        scores = dot_nt(left, right) + bias_rows[p]
        peak = jnp.max(scores, 1, keepdims=True)
        weights = jnp.exp(scores - peak).astype(BF16)
        e[index] = weights
        both = dot(weights, jnp.concatenate([vs[p, r], ones], 1))
        scale = 1.0 / both[:, lanes:]
        mixed = both[:, :lanes] * scale
        kept = jnp.where(low_half, mixed[:shard], mixed[shard:])
        ctx[p, r] = kept
        ctx_low[p, r] = kept.astype(BF16)
        rinv[p, r] = jnp.where(low_half, scale[:shard], scale[shard:])

    for index in range(rows * pairs):
        forward(index)

    w_copies["wo"].wait()
    for r in range(rows):
        context = jnp.concatenate([ctx_low[p, r] for p in range(pairs)], 1)
        hid[r * shard : (r + 1) * shard, :] = xs[r, :shard, :].astype(F32) + dot(context, n["wov"][...])
    state = hid[...]
    inv2 = inverse_rms(state)
    hat2 = state * inv2
    hid_low[...] = (hat2 * n["gain2"][...][None, :]).astype(BF16)

    w_copies["win"].wait()
    w_copies["wout"].wait()
    chunk = 2 * lanes
    for j in range(hidden // chunk):
        cols = slice(j * chunk, (j + 1) * chunk)
        g, slope = gelu_pair(dot(hid_low[...], n["winv"][:, cols]))
        gslope[:, cols] = slope.astype(BF16)
        act[:, cols] = g.astype(BF16)

    cot_copy.wait()
    branch = dot(act[...], n["woutv"][...])
    branch_low = branch.astype(BF16)
    down_t, up = mixes["down_t"], mixes["up"]
    g, slope = gelu_pair(dot_nt(branch_low, down_t) + n["bd"][...][None, :])
    g_low = g.astype(BF16)
    adapted = dot(g_low, up) + n["bu"][...][None, :]
    result = hid[...] + branch + adapted
    for r in range(rows):
        n["out"][r] = result[r * shard : (r + 1) * shard].astype(BF16)
    up_low = jnp.concatenate([n["cots"][r] for r in range(rows)], 0)
    upstream = up_low.astype(F32)
    gb = dot_nt(up_low, up) * slope
    gb_low = gb.astype(BF16)
    branch_grad = (upstream + dot(gb_low, down_t)).astype(BF16)
    grad_up = dot_tn(g_low, up_low)
    grad_down_t = dot_tn(gb_low, branch_low)
    adapter_grads(n, mixes, grad_up, grad_down_t, ranks, mid, width)
    pack[2:3, :] = jnp.sum(upstream, 0, keepdims=True)
    pack[7:8, 0 : gb.shape[1]] = jnp.sum(gb, 0, keepdims=True)

    n["hid_low"][...] = branch_grad
    for j in range(hidden // chunk):
        cols = slice(j * chunk, (j + 1) * chunk)
        act[:, cols] = (dot_nt(hid_low[...], n["woutv"][cols, :]) * gslope[:, cols].astype(F32)).astype(BF16)
    grad2 = dot_nt(act[...], n["winv"][...])
    state = hid[...]
    inv2 = inverse_rms(state)
    hat2 = state * inv2
    pack[1:2, :] = jnp.sum(grad2 * hat2, 0, keepdims=True)
    c = grad2 * n["gain2"][...][None, :]
    hidden_grad = upstream + inv2 * (c - hat2 * jnp.mean(hat2 * c, -1, keepdims=True))
    n["hidden_grad"][...] = hidden_grad
    hid_low[...] = hidden_grad.astype(BF16)

    for t in range(width // step):
        part = dot_nt(hid_low[...], n["wov"][t * step : (t + 1) * step, :]).astype(BF16)
        for r in range(rows):
            for s in range(2):
                dctx[2 * t + s, r] = part[r * shard : (r + 1) * shard, s * lanes : (s + 1) * lanes]

    def backward(index):
        r, p = index // pairs, index % pairs
        scale = rinv[p, r]
        slope_in = dctx[p, r].astype(F32) * scale
        product = slope_in * ctx[p, r]
        first = jnp.sum(jnp.where(low_half, product, 0.0), 1, keepdims=True)
        second = jnp.sum(jnp.where(low_half, 0.0, product), 1, keepdims=True)
        delta = jnp.concatenate([first, second], 0)
        slope_low = slope_in.astype(BF16)
        slope_t = jnp.transpose(slope_low)
        left = jnp.concatenate([slope_low * low_lane, slope_low * high_lane], 0)
        weights = e[index]
        steep = weights * (dot_nt(left, vs[p, r]) - delta).astype(BF16)
        grad_q = dot(steep, ks[p, r])
        dq[r, p] = jnp.where(low_half, grad_q[:shard], grad_q[shard:]).astype(BF16)
        qq_t = qt[p, r]
        turned_q = jnp.concatenate([qq_t * low_row, qq_t * high_row], 1)
        turned_s = jnp.concatenate([slope_t * low_row, slope_t * high_row], 1)
        dkt[r, p] = dot(turned_q, steep).astype(BF16)
        dvt[r, p] = dot(turned_s, weights).astype(BF16)

    for index in range(rows * pairs):
        backward(index)

    gain_total = jnp.zeros((1, width), F32)
    for r in range(rows):
        key_t = dkt[r].reshape(width, keys)
        value_t = dvt[r].reshape(width, keys)
        part = jnp.transpose(dot(n["wkv"][...], key_t) + dot(n["wvv"][...], value_t))
        grad_q = jnp.concatenate([dq[r, p] for p in range(pairs)], 1)
        own_grad = part[:shard] + dot_nt(grad_q, n["wqv"][...])
        x = xs[r].astype(F32)
        hat = x * inverse_rms(x)
        gain_total = gain_total + jnp.sum(own_grad * hat[:shard], 0, keepdims=True)
        gain_total = gain_total + jnp.sum(part[shard:] * hat[shard:], 0, keepdims=True)
        n["own_part"][r * shard : (r + 1) * shard, :] = own_grad
        n["sib_part"][r] = part[shard : 2 * shard].astype(BF16)
        n["rown_part"][r] = part[2 * shard : 3 * shard].astype(BF16)
        n["rsib_part"][r] = part[3 * shard :].astype(BF16)
    pack[0:1, :] = gain_total


def adapter_setup(n, ranks, mid, width):
    inner, outer = mid // ranks, width // ranks
    square = ranks * ranks
    for i in range(ranks):
        block = n["shared"][i]
        n["sh16"][i * ranks : (i + 1) * ranks, :] = block
        eye = (iota((ranks, ranks), 0) == iota((ranks, ranks), 1)).astype(F32)
        n["sh16t"][i * ranks : (i + 1) * ranks, :] = dot_tn(block, eye, HI)
    spread = (block_of(iota((square, ranks), 0), ranks, ranks) == iota((square, ranks), 1)).astype(F32)
    by_c = (block_of(iota((ranks, mid), 1), inner, ranks) == iota((ranks, mid), 0)).astype(F32)
    column = iota((inner, mid), 1)
    by_j = (column - inner * block_of(column, inner, ranks) == iota((inner, mid), 0)).astype(F32)
    column = iota((outer, width), 1)
    by_b = (column - outer * block_of(column, outer, ranks) == iota((outer, width), 0)).astype(F32)
    line = iota((square, width), 0)
    own_block = (
        line - ranks * block_of(line, ranks, ranks) == block_of(iota((square, width), 1), outer, ranks)
    ).astype(F32)
    shx = dot(n["sh16"][...], by_c, HI)
    shtx = dot(n["sh16t"][...], by_c, HI)
    drx = dot(dot(spread, n["dr"][...], HI), by_j, HI)
    ulx = dot(dot(spread, n["ul"][...], HI), by_j, HI)
    dlx = dot(dot(spread, n["dl"][...], HI), by_b, HI) * own_block
    urx = dot(dot(spread, n["ur"][...], HI), by_b, HI) * own_block
    mx = shx * drx
    nx = shtx * ulx
    return dict(
        spread=spread, by_c=by_c, by_j=by_j, by_b=by_b, own_block=own_block, shx=shx, shtx=shtx, drx=drx, ulx=ulx,
        dlx=dlx, urx=urx, mx=mx, nx=nx,
        down_t=dot_tn(mx, dlx, HI).astype(BF16), up=dot_tn(nx, urx, HI).astype(BF16),
    )


def adapter_grads(n, m, grad_up, grad_down_t, ranks, mid, width):
    inner, outer = mid // ranks, width // ranks
    square = ranks * ranks
    pack = n["pack"]
    pack[3:16, :] = jnp.zeros((13, width), F32)
    p_down = dot_nt(m["dlx"], grad_down_t, HI)
    p_up = dot_nt(m["urx"], grad_up, HI)
    pack[3 : 3 + ranks, 0:outer] = dot_nt(
        dot_tn(m["spread"], dot(m["mx"], grad_down_t, HI) * m["own_block"], HI), m["by_b"], HI
    )
    pack[3 : 3 + ranks, 256 : 256 + outer] = dot_nt(
        dot_tn(m["spread"], dot(m["nx"], grad_up, HI) * m["own_block"], HI), m["by_b"], HI
    )
    pack[3 : 3 + ranks, 512 : 512 + inner] = dot_nt(dot_tn(m["spread"], p_down * m["shx"], HI), m["by_j"], HI)
    pack[3 : 3 + ranks, 640 : 640 + inner] = dot_nt(dot_tn(m["spread"], p_up * m["shtx"], HI), m["by_j"], HI)
    shared_down = dot_nt(p_down * m["drx"], m["by_c"], HI)
    shared_up = dot_nt(p_up * m["ulx"], m["by_c"], HI)
    for i in range(ranks):
        rows = slice(i * ranks, (i + 1) * ranks)
        eye = (iota((ranks, ranks), 0) == iota((ranks, ranks), 1)).astype(F32)
        total = shared_down[rows] + dot_tn(shared_up[rows], eye, HI)
        pack[8 : 8 + ranks, i * 128 : i * 128 + ranks] = total


def last_kernel(dims, own, sib, far, x_ref, gain1, hidden_grad, grad_input):
    rows, shard = dims[0], dims[1]
    for r in range(rows):
        lines = slice(r * shard, (r + 1) * shard)
        grad = own[lines, :] + sib[r].astype(F32) + far[r].astype(F32)
        x = x_ref[r].astype(F32)
        inv = inverse_rms(x)
        hat = x * inv
        c = grad * gain1[...][None, :]
        total = hidden_grad[lines, :] + inv * (c - hat * jnp.mean(hat * c, -1, keepdims=True))
        grad_input[r] = total.astype(BF16)


def unpack_kernel(dims, pack, g1, g2, shared, dl, dr, ul, ur, bd, bu):
    rows, shard, width, heads, hidden, parts, ranks, mid = dims
    inner, outer = mid // ranks, width // ranks
    g1[...] = pack[0]
    g2[...] = pack[1]
    bu[...] = pack[2]
    bd[...] = pack[7, 0:mid]
    dl[...] = pack[3 : 3 + ranks, 0:outer]
    ur[...] = pack[3 : 3 + ranks, 256 : 256 + outer]
    dr[...] = pack[3 : 3 + ranks, 512 : 512 + inner]
    ul[...] = pack[3 : 3 + ranks, 640 : 640 + inner]
    for i in range(ranks):
        shared[i] = pack[8 : 8 + ranks, i * 128 : i * 128 + ranks]


def exchange(value, axis, bit):
    count = lax.axis_size(axis)
    return lax.ppermute(value, axis, [(k, k ^ bit) for k in range(count)])


def shards(
    inputs, cotangent, segment_ids, bucket_table, position_bias, query_weight, key_weight, value_weight, out_weight,
    hidden_in, hidden_out, gain_first, gain_second, shared, down_left, down_right, up_left_vectors, up_right,
    bias_down, bias_up,
):
    rows, shard, width = inputs.shape
    heads = position_bias.shape[1]
    hidden = hidden_in.shape[1]
    parts = lax.axis_size("seq")
    ranks, mid = shared.shape[0], bias_down.shape[0]
    dims = (rows, shard, width, heads, hidden, parts, ranks, mid)
    pairs, tokens, keys = heads // 2, rows * shard, shard * parts
    lanes = width // pairs

    x_far = exchange(inputs, "seq", 2)
    seg_far = exchange(segment_ids, "seq", 2)
    x_sib = exchange(inputs, "seq", 1)
    seg_sib = exchange(segment_ids, "seq", 1)
    x_farsib = exchange(x_far, "seq", 1)
    seg_farsib = exchange(seg_far, "seq", 1)

    any_spec = pl.BlockSpec(memory_space=pl.ANY)
    vmem = pl.BlockSpec(memory_space=pltpu.VMEM)
    scratch = [
        pltpu.VMEM((rows, keys, width), BF16),
        pltpu.VMEM((rows, keys, width), BF16),
        pltpu.VMEM((pairs, rows, keys, lanes), BF16),
        pltpu.VMEM((pairs, rows, keys, lanes), BF16),
        pltpu.VMEM((rows, keys, lanes), BF16),
        pltpu.VMEM((pairs, rows, shard, lanes), BF16),
        pltpu.VMEM((pairs, rows, lanes, shard), BF16),
        pltpu.VMEM((rows * pairs, 2 * shard, keys), BF16),
        pltpu.VMEM((pairs, 2 * shard, keys), F32),
        pltpu.VMEM((pairs, rows, shard, lanes), F32),
        pltpu.VMEM((pairs, rows, shard, lanes), BF16),
        pltpu.VMEM((pairs, rows, shard, lanes), F32),
        pltpu.VMEM((tokens, width), F32),
        pltpu.VMEM((tokens, width), BF16),
        pltpu.VMEM((tokens, hidden), BF16),
        pltpu.VMEM((pairs, rows, shard, lanes), BF16),
        pltpu.VMEM((rows, pairs, shard, lanes), BF16),
        pltpu.VMEM((rows, pairs, lanes, keys), BF16),
        pltpu.VMEM((rows, pairs, lanes, keys), BF16),
        pltpu.VMEM((rows, shard, width), BF16),
        pltpu.VMEM((width, width), BF16),
        pltpu.VMEM((width, width), BF16),
        pltpu.VMEM((width, width), BF16),
        pltpu.VMEM((width, width), BF16),
        pltpu.VMEM((width, hidden), BF16),
        pltpu.VMEM((hidden, width), BF16),
        pltpu.VMEM((16, 2 * keys), F32),
        pltpu.VMEM((ranks * ranks, ranks), F32),
        pltpu.VMEM((ranks * ranks, ranks), F32),
        pltpu.VMEM((rows, shard, lanes), BF16),
        pltpu.VMEM((tokens, hidden), BF16),
        pltpu.SemaphoreType.DMA((11,)),
    ]
    out, own_part, sib_part, rsib_part, rown_part, hidden_grad, pack = pl.pallas_call(
        functools.partial(main_kernel, dims),
        out_shape=[
            jax.ShapeDtypeStruct((rows, shard, width), BF16),
            jax.ShapeDtypeStruct((tokens, width), F32),
            jax.ShapeDtypeStruct((rows, shard, width), BF16),
            jax.ShapeDtypeStruct((rows, shard, width), BF16),
            jax.ShapeDtypeStruct((rows, shard, width), BF16),
            jax.ShapeDtypeStruct((tokens, width), F32),
            jax.ShapeDtypeStruct((16, width), F32),
        ],
        in_specs=[any_spec] * 5 + [vmem] * 6 + [any_spec] * 6 + [vmem] * 9,
        out_specs=[vmem] * 7,
        scratch_shapes=scratch,
        compiler_params=pltpu.CompilerParams(vmem_limit_bytes=60 * MIB),
    )(
        inputs, x_sib, x_far, x_farsib, cotangent, segment_ids, seg_sib, seg_far, seg_farsib,
        bucket_table, position_bias,
        query_weight, key_weight, value_weight, out_weight, hidden_in, hidden_out,
        gain_first, gain_second, shared, down_left, down_right, up_left_vectors, up_right,
        bias_down, bias_up,
    )

    far = exchange(rown_part + exchange(rsib_part, "seq", 1), "seq", 2)
    from_sib = exchange(sib_part, "seq", 1)
    for axis in ("seq", "batch"):
        bit = 1
        while bit < lax.axis_size(axis):
            pack = pack + exchange(pack, axis, bit)
            bit *= 2

    (grad_input,) = pl.pallas_call(
        functools.partial(last_kernel, dims),
        out_shape=[jax.ShapeDtypeStruct((rows, shard, width), BF16)],
        in_specs=[vmem] * 6,
        out_specs=[vmem],
        compiler_params=pltpu.CompilerParams(vmem_limit_bytes=30 * MIB),
    )(own_part, from_sib, far, inputs, gain_first, hidden_grad)

    inner, outer = mid // ranks, width // ranks
    grads = pl.pallas_call(
        functools.partial(unpack_kernel, dims),
        out_shape=[
            jax.ShapeDtypeStruct((width,), F32),
            jax.ShapeDtypeStruct((width,), F32),
            jax.ShapeDtypeStruct((ranks, ranks, ranks), F32),
            jax.ShapeDtypeStruct((ranks, outer), F32),
            jax.ShapeDtypeStruct((ranks, inner), F32),
            jax.ShapeDtypeStruct((ranks, inner), F32),
            jax.ShapeDtypeStruct((ranks, outer), F32),
            jax.ShapeDtypeStruct((mid,), F32),
            jax.ShapeDtypeStruct((width,), F32),
        ],
        in_specs=[vmem],
        out_specs=[vmem] * 9,
    )(pack)
    return (out, grad_input, *grads)


def solution(mesh):
    rows = P("batch", "seq", None)
    in_specs = (rows, rows, P("batch", "seq")) + (P(),) * 17
    out_specs = (rows, rows) + (P(),) * 9
    return jax.shard_map(shards, mesh=mesh, in_specs=in_specs, out_specs=out_specs, check_vma=False)
```

```python
import functools

import jax
import jax.numpy as jnp
from jax import lax
from jax.experimental import pallas as pl
from jax.experimental.pallas import tpu as pltpu
from jax.sharding import PartitionSpec as P

F32 = jnp.float32
BF16 = jnp.bfloat16
HI = lax.Precision.HIGHEST
epsilon = 1e-06
masked = -1e30
gelu_a = 0.7978845608028654
gelu_b = 0.044715
MIB = 1024 * 1024
shared_slots = (192, 448, 576, 704)
VM = pl.BlockSpec(memory_space=pltpu.VMEM)


def dot(a, b, precision=None):
    return lax.dot_general(a, b, (((1,), (0,)), ((), ())), precision=precision, preferred_element_type=F32)


def dot_nt(a, b, precision=None):
    return lax.dot_general(a, b, (((1,), (1,)), ((), ())), precision=precision, preferred_element_type=F32)


def dot_tn(a, b, precision=None):
    return lax.dot_general(a, b, (((0,), (0,)), ((), ())), precision=precision, preferred_element_type=F32)


def iota(shape, axis):
    return lax.broadcasted_iota(jnp.int32, shape, axis)


def block_of(index, size, count):
    total = jnp.zeros_like(index)
    for k in range(1, count):
        total = total + (index >= k * size).astype(jnp.int32)
    return total


def gelu_pair(v):
    square = v * v
    h = 0.5 + 0.5 * jnp.tanh(v * (gelu_a + gelu_a * gelu_b * square))
    g = v * h
    slope = h + (g - g * h) * (2.0 * gelu_a + 6.0 * gelu_a * gelu_b * square)
    return g, slope


def inverse_rms(x):
    return lax.rsqrt(jnp.mean(x * x, -1, keepdims=True) + epsilon)


class Far:
    def __init__(self, value):
        self.value = value


def near(value):
    return pltpu.with_memory_space_constraint(value, pltpu.VMEM)


def call(kernel, outs, args, limit, micros, scratch=(), copies=0, last=False):
    specs = [pl.BlockSpec(memory_space=pl.ANY) if isinstance(a, Far) else VM for a in args]
    args = [pltpu.with_memory_space_constraint(a.value, pltpu.HBM) if isinstance(a, Far) else near(a) for a in args]
    scratch = [pltpu.VMEM(shape, kind) for shape, kind in scratch]
    if copies:
        scratch.append(pltpu.SemaphoreType.DMA((copies,)))
    made = jax.ShapeDtypeStruct if last else pltpu.VMEM
    return pl.pallas_call(
        kernel,
        out_shape=[made(shape, kind) for shape, kind in outs],
        in_specs=specs,
        out_specs=[VM] * len(outs),
        scratch_shapes=scratch,
        compiler_params=pltpu.CompilerParams(vmem_limit_bytes=limit * MIB),
        cost_estimate=pl.CostEstimate(flops=int(micros * 1.1e9), bytes_accessed=0, transcendentals=0),
    )(*args)


def start_copies(pairs, sems):
    started = [pltpu.make_async_copy(source, target, sems.at[k]) for k, (source, target) in enumerate(pairs)]
    for one in started:
        one.start()
    return started


def pick_kernel(inputs, cotangent, segment_ids, own, a_send, b_send, cot_send, ids, sems):
    rows, shard, width = inputs.shape
    extra = own.shape[1] - shard
    row = moved_row(rows)
    other = rows - 1 - row
    body = pl.ds(0, shard)
    started = start_copies(
        [
            (segment_ids, ids),
            (inputs.at[other], a_send.at[0, body]),
            (inputs.at[1], b_send.at[0, body]),
            (inputs.at[row], own.at[0, body]),
            (inputs.at[1], own.at[1, body]),
            (cotangent.at[other], cot_send.at[0]),
        ],
        sems,
    )
    started[0].wait()
    for target, k, source in ((own, 0, row), (own, 1, 1), (a_send, 0, other), (b_send, 0, 1)):
        line = jnp.broadcast_to(ids[pl.ds(source, 1), :].astype(F32).astype(BF16), (extra, shard))
        target[k, shard:, :] = jnp.zeros((extra, width), BF16)
        target[k, shard:, 0:shard] = line
    for one in started[1:]:
        one.wait()


def setup_kernel(
    shard, parts, table_far, position_far, shared_far, dl_far, dr_far, ul_far, ur_far, bd_far, bu_far, g1_far, g2_far,
    wq_far, wk_far, wv_far, wo_far, win_far, wout_far,
    tiles, down_t, up, shx, shtx, drx, ulx, dlx, urx, bd, bu, g1, g2, wq, wk, wv, wo, win, wout,
    tab, sh16, sh16t, table, position_bias, shared, dl, dr, ul, ur, sems,
):
    started = start_copies(
        [
            (table_far, table), (position_far, position_bias), (shared_far, shared), (dl_far, dl), (dr_far, dr),
            (ul_far, ul), (ur_far, ur), (bd_far, bd), (bu_far, bu), (g1_far, g1), (g2_far, g2),
            (wq_far, wq), (wk_far, wk), (wv_far, wv), (wo_far, wo), (win_far, win), (wout_far, wout),
        ],
        sems,
    )
    for one in started[:11]:
        one.wait()
    heads = position_bias.shape[0]
    ranks, (mid, width) = shared.shape[0], down_t.shape
    inner, outer = mid // ranks, width // ranks
    square = ranks * ranks
    hits = (table[...][None, :] == iota((position_bias.shape[1], table.shape[0]), 0)).astype(F32)
    tab[0:heads, 0 : table.shape[0]] = dot(position_bias[...], hits, HI)
    for k in range(2 * parts - 1):
        for h in range(heads):
            line = tab[h : h + 1, k * shard : (k + 2) * shard]
            turned = pltpu.roll(jnp.broadcast_to(line, (shard, 2 * shard)), shard + 1, 1, stride=1, stride_axis=0)
            tiles[k, h // 2, (h % 2) * shard : (h % 2 + 1) * shard, :] = turned[:, :shard]
    eye = (iota((ranks, ranks), 0) == iota((ranks, ranks), 1)).astype(F32)
    for i in range(ranks):
        block = shared[i]
        sh16[i * ranks : (i + 1) * ranks, :] = block
        sh16t[i * ranks : (i + 1) * ranks, :] = dot_tn(block, eye, HI)
    spread, by_c, by_j, by_b, own_block = selectors(ranks, mid, width)
    shx[...] = dot(sh16[...], by_c, HI)
    shtx[...] = dot(sh16t[...], by_c, HI)
    drx[...] = dot(dot(spread, dr[...], HI), by_j, HI)
    ulx[...] = dot(dot(spread, ul[...], HI), by_j, HI)
    dlx[...] = dot(dot(spread, dl[...], HI), by_b, HI) * own_block
    urx[...] = dot(dot(spread, ur[...], HI), by_b, HI) * own_block
    down_t[...] = dot_tn(shx[...] * drx[...], dlx[...], HI).astype(BF16)
    up[...] = dot_tn(shtx[...] * ulx[...], urx[...], HI).astype(BF16)
    for one in started[11:]:
        one.wait()


def selectors(ranks, mid, width):
    inner, outer, square = mid // ranks, width // ranks, ranks * ranks
    spread = (block_of(iota((square, ranks), 0), ranks, ranks) == iota((square, ranks), 1)).astype(F32)
    by_c = (block_of(iota((ranks, mid), 1), inner, ranks) == iota((ranks, mid), 0)).astype(F32)
    column = iota((inner, mid), 1)
    by_j = (column - inner * block_of(column, inner, ranks) == iota((inner, mid), 0)).astype(F32)
    column = iota((outer, width), 1)
    by_b = (column - outer * block_of(column, outer, ranks) == iota((outer, width), 0)).astype(F32)
    line = iota((square, width), 0)
    own_block = (
        line - ranks * block_of(line, ranks, ranks) == block_of(iota((square, width), 1), outer, ranks)
    ).astype(F32)
    return spread, by_c, by_j, by_b, own_block


def moved_row(rows):
    half = lax.axis_size("seq") // 2
    return jnp.where(lax.axis_index("seq") < half, 0, rows - 1)


def normed(x, gain):
    x = x.astype(F32)
    return (x * inverse_rms(x) * gain[...][None, :]).astype(BF16)


def project(x, weight, target, at):
    pairs, _, lanes = target.shape
    count = x.shape[0]
    for t in range(pairs // 2):
        result = dot(x, weight[:, 2 * t * lanes : (2 * t + 2) * lanes]).astype(BF16)
        target[2 * t, at : at + count, :] = result[:, :lanes]
        target[2 * t + 1, at : at + count, :] = result[:, lanes:]


def local_kernel(own, sib, wq, wk, wv, gain, k_loc, v_loc, q_loc):
    shard = q_loc.shape[1] // 2
    blocks = [normed(x, gain) for x in (own[0, :shard], sib[0, :shard], own[1, :shard], sib[1, :shard])]
    x = jnp.concatenate(blocks, 0)
    project(x, wk, k_loc, 0)
    project(x, wv, v_loc, 0)
    project(jnp.concatenate([blocks[0], blocks[2]], 0), wq, q_loc, 0)


def segment_features(blocks, shard, lanes):
    lane = iota((shard, lanes), 1)
    keys, queries = [], []
    for block in blocks:
        line = block[shard : shard + 1, 0:shard].astype(F32)
        same = lane.astype(F32) == jnp.transpose(jnp.broadcast_to(line, (lanes, shard)))
        keys.append(same.astype(F32).astype(BF16))
        queries.append(jnp.where((lane < 3) & jnp.logical_not(same), masked, 0.0).astype(BF16))
    return jnp.concatenate(keys, 0), queries


def halves(lanes):
    low = iota((1, lanes), 1) < lanes // 2
    low_lane = low.astype(F32).astype(BF16)
    return low, low_lane, 1.0 - low_lane


def attend(p, q, feature, keys, key_feature, values, bias):
    shard, lanes = q.shape
    low, low_lane, high_lane = halves(lanes)
    left = jnp.concatenate(
        [jnp.concatenate([q * low_lane, feature], 1), jnp.concatenate([q * high_lane, feature], 1)], 0
    )
    scores = dot_nt(left, jnp.concatenate([keys, key_feature], 1)) + bias
    weights = jnp.exp(scores - jnp.max(scores, 1, keepdims=True)).astype(BF16)
    both = dot(weights, jnp.concatenate([values, jnp.ones(values.shape, BF16)], 1))
    scale = 1.0 / both[:, lanes:]
    mixed = both[:, :lanes] * scale
    return weights, jnp.where(low, mixed[:shard], mixed[shard:]), jnp.where(low, scale[:shard], scale[shard:])


def attention_kernel(
    is_moved, own, sib, far, far_sib, k_loc, v_loc, q_loc, tiles,
    wq, wk, wv, wo, gain, k_rem, v_rem, *rest,
):
    pairs, _, lanes = k_rem.shape
    shard = q_loc.shape[1] // 2
    if is_moved:
        q_rem, e, ctx, rinv, hid = rest
        first, queries = 0, [0, 2]
    else:
        e, ctx, rinv, hid = rest
        first, queries = 1, [0]
    place = lax.axis_index("seq")
    parts = lax.axis_size("seq")
    far_low = normed(far[0, :shard], gain)
    x = jnp.concatenate([far_low, normed(far_sib[0, :shard], gain)], 0)
    project(x, wk, k_rem, 0)
    project(x, wv, v_rem, 0)
    if is_moved:
        project(far_low, wq, q_rem, 0)
    key_feature, query_feature = segment_features(
        (own.at[first], sib.at[first], far.at[0], far_sib.at[0]), shard, lanes
    )
    local = slice(2 * first * shard, 2 * (first + 1) * shard)
    contexts = [[] for _ in queries]
    for p in range(pairs):
        keys = jnp.concatenate([k_loc[p, local, :], k_rem[p]], 0)
        values = jnp.concatenate([v_loc[p, local, :], v_rem[p]], 0)
        for b, block in enumerate(queries):
            q = q_rem[p] if block == 2 else q_loc[p, first * shard : (first + 1) * shard, :]
            at = jnp.bitwise_xor(place, block)
            bias = jnp.concatenate(
                [tiles[jnp.bitwise_xor(place, k) - at + parts - 1, p] for k in range(parts)], 1
            )
            weights, kept, scale = attend(p, q, query_feature[block], keys, key_feature, values, bias)
            e[b * pairs + p] = weights
            span = slice(b * shard, (b + 1) * shard)
            ctx[p, span, :] = kept
            rinv[p, span, :] = scale
            contexts[b].append(kept.astype(BF16))
    context = jnp.concatenate([jnp.concatenate(c, 1) for c in contexts], 0)
    x = jnp.concatenate([own[first, :shard]] + ([far[0, :shard]] if is_moved else []), 0).astype(F32)
    hid[...] = x + dot(context, wo[...])


def middle_kernel(
    hid_a, hid_b, cot, cot_far, win, wout, wo, gain2, bd, bu, down_t, up,
    out, hidden_grad, dctx, grad_up, grad_down_t, lines, low, act, gslope,
):
    rows, shard, width = cot.shape
    hidden = win.shape[1]
    pairs, _, lanes = dctx.shape
    state = jnp.concatenate([hid_a[...], hid_b[...]], 0)
    inv2 = inverse_rms(state)
    low[...] = (state * inv2 * gain2[...][None, :]).astype(BF16)
    chunk = 2 * lanes
    for j in range(hidden // chunk):
        cols = slice(j * chunk, (j + 1) * chunk)
        g, slope = gelu_pair(dot(low[...], win[:, cols]))
        gslope[:, cols] = slope.astype(BF16)
        act[:, cols] = g.astype(BF16)
    branch = dot(act[...], wout[...])
    row = moved_row(rows)
    branch_low = branch.astype(BF16)
    g, slope = gelu_pair(dot_nt(branch_low, down_t[...]) + bd[...][None, :])
    g_low = g.astype(BF16)
    up_low = jnp.concatenate([cot[row], cot_far[0], cot[1]], 0)
    upstream = up_low.astype(F32)
    gb = dot_nt(up_low, up[...]) * slope
    gb_low = gb.astype(BF16)
    low[...] = (upstream + dot(gb_low, down_t[...])).astype(BF16)
    result = state + branch + dot(g_low, up[...]) + bu[...][None, :]
    for b in range(rows):
        out[b] = result[b * shard : (b + 1) * shard].astype(BF16)
    grad_up[...] = dot_tn(g_low, up_low)
    grad_down_t[...] = dot_tn(gb_low, branch_low)
    for j in range(hidden // chunk):
        cols = slice(j * chunk, (j + 1) * chunk)
        act[:, cols] = (dot_nt(low[...], wout[cols, :]) * gslope[:, cols].astype(F32)).astype(BF16)
    grad2 = dot_nt(act[...], win[...])
    state = jnp.concatenate([hid_a[...], hid_b[...]], 0)
    inv2 = inverse_rms(state)
    hat2 = state * inv2
    c = grad2 * gain2[...][None, :]
    total = upstream + inv2 * (c - hat2 * jnp.mean(hat2 * c, -1, keepdims=True))
    hidden_grad[...] = total
    low[...] = total.astype(BF16)
    lines[...] = jnp.zeros(lines.shape, F32)
    lines[0:1, :] = jnp.sum(grad2 * hat2, 0, keepdims=True)
    lines[1:2, :] = jnp.sum(upstream, 0, keepdims=True)
    lines[2:3, 0 : gb.shape[1]] = jnp.sum(gb, 0, keepdims=True)
    for t in range(pairs // 2):
        part = dot_nt(low[...], wo[2 * t * lanes : (2 * t + 2) * lanes, :]).astype(BF16)
        dctx[2 * t] = part[:, :lanes]
        dctx[2 * t + 1] = part[:, lanes:]


def backward_kernel(
    is_moved, ranks, own, sib, far, far_sib, dctx, ctx, rinv, e, k_loc, v_loc, q_loc, k_rem, v_rem, *rest,
):
    pairs, _, lanes = dctx.shape
    shard, width = q_loc.shape[1] // 2, pairs * lanes
    if is_moved:
        q_rem, wq, wk, wv, *rest = rest
        *small, own_part, sib_part, pack, dkt, dvt = rest
        first, blocks, start = 0, 2, 0
    else:
        wq, wk, wv, pack_a, own_part, far_part, sib_part, pack, dkt, dvt = rest
        first, blocks, start = 1, 1, 2
    low, low_lane, high_lane = halves(lanes)
    low_row = (iota((lanes, 1), 0) < lanes // 2).astype(F32).astype(BF16)
    high_row = 1.0 - low_row
    local = slice(2 * first * shard, 2 * (first + 1) * shard)
    query_grads = [[] for _ in range(blocks)]
    for p in range(pairs):
        keys = jnp.concatenate([k_loc[p, local, :], k_rem[p]], 0)
        values = jnp.concatenate([v_loc[p, local, :], v_rem[p]], 0)
        turned_q, turned_s, steeps, weight_list = [], [], [], []
        for b in range(blocks):
            span = slice(b * shard, (b + 1) * shard)
            scaled = dctx[p, (start + b) * shard : (start + b + 1) * shard, :].astype(F32) * rinv[p, span, :]
            product = scaled * ctx[p, span, :]
            delta = jnp.concatenate(
                [
                    jnp.sum(jnp.where(low, product, 0.0), 1, keepdims=True),
                    jnp.sum(jnp.where(low, 0.0, product), 1, keepdims=True),
                ],
                0,
            )
            scaled = scaled.astype(BF16)
            left = jnp.concatenate([scaled * low_lane, scaled * high_lane], 0)
            weights = e[b * pairs + p]
            steep = weights * (dot_nt(left, values) - delta).astype(BF16)
            grad_q = dot(steep, keys)
            query_grads[b].append(jnp.where(low, grad_q[:shard], grad_q[shard:]).astype(BF16))
            q = q_rem[p] if b == 1 else q_loc[p, first * shard : (first + 1) * shard, :]
            q_t, s_t = jnp.transpose(q), jnp.transpose(scaled)
            turned_q += [q_t * low_row, q_t * high_row]
            turned_s += [s_t * low_row, s_t * high_row]
            steeps.append(steep)
            weight_list.append(weights)
        dkt[p] = dot(jnp.concatenate(turned_q, 1), jnp.concatenate(steeps, 0)).astype(BF16)
        dvt[p] = dot(jnp.concatenate(turned_s, 1), jnp.concatenate(weight_list, 0)).astype(BF16)
    keys = dkt.shape[2]
    key_t = dkt[...].reshape(width, keys)
    value_t = dvt[...].reshape(width, keys)
    part = jnp.transpose(dot(wk[...], key_t) + dot(wv[...], value_t))
    from_q = dot_nt(jnp.concatenate([jnp.concatenate(g, 1) for g in query_grads], 0), wq[...])
    pieces = [part[k * shard : (k + 1) * shard] for k in range(4)]
    pieces[0] = pieces[0] + from_q[:shard]
    if is_moved:
        pieces[2] = pieces[2] + from_q[shard:]
    gain = jnp.zeros((1, width), F32)
    for piece, x in zip(pieces, (own[first], sib[first], far[0], far_sib[0])):
        x = x[:shard].astype(F32)
        gain = gain + jnp.sum(piece * (x * inverse_rms(x)), 0, keepdims=True)
    if is_moved:
        pack_small(ranks, *small, pack)
        pack[0:1, :] = gain
        own_part[0] = pieces[0]
        own_part[1] = pieces[2]
    else:
        pack[...] = pack_a[...]
        pack[0:1, :] = pack_a[0:1, :] + gain
        sib_part[0, shard:, :] = jnp.zeros((16, width), BF16)
        sib_part[1, shard:, :] = jnp.concatenate(two_parts(pack[...]), 0)
        own_part[0] = pieces[0]
        far_part[0] = pieces[2].astype(BF16)
    sib_part[0, :shard] = pieces[1].astype(BF16)
    sib_part[1, :shard] = pieces[3].astype(BF16)


def pack_small(ranks, grad_up, grad_down_t, lines, shx, shtx, drx, ulx, dlx, urx, pack):
    mid, width = grad_up.shape
    inner, outer = mid // ranks, width // ranks
    spread, by_c, by_j, by_b, own_block = selectors(ranks, mid, width)
    pack[...] = jnp.zeros(pack.shape, F32)
    pack[1:4, :] = lines[0:3, :]
    down_t, up = grad_down_t[...], grad_up[...]
    p_down = dot_nt(dlx[...], down_t)
    p_up = dot_nt(urx[...], up)
    left = dot_tn(spread, dot(shx[...] * drx[...], down_t) * own_block)
    right = dot_tn(spread, dot(shtx[...] * ulx[...], up) * own_block)
    pack[4:8, 0:outer] = dot_nt(left, by_b)
    pack[4:8, 256 : 256 + outer] = dot_nt(right, by_b)
    pack[4:8, 512 : 512 + inner] = dot_nt(dot_tn(spread, p_down * shx[...]), by_j)
    pack[4:8, 640 : 640 + inner] = dot_nt(dot_tn(spread, p_up * shtx[...]), by_j)
    shared_down = dot_nt(p_down * drx[...], by_c)
    shared_up = dot_nt(p_up * ulx[...], by_c)
    eye = (iota((ranks, ranks), 0) == iota((ranks, ranks), 1)).astype(F32)
    for i, at in enumerate(shared_slots):
        one = slice(i * ranks, (i + 1) * ranks)
        pack[4:8, at : at + ranks] = shared_down[one] + dot_tn(shared_up[one], eye)


def norm_back(x, grad, hidden_grad, gain):
    x = x.astype(F32)
    inv = inverse_rms(x)
    hat = x * inv
    c = grad * gain[...][None, :]
    return hidden_grad + inv * (c - hat * jnp.mean(hat * c, -1, keepdims=True))


def return_kernel(_, far, own_part, from_sib, far_part, from_sib_b, out, hidden_grad, gain, result):
    shard = out.shape[1]
    result[0] = (far_part[0].astype(F32) + from_sib_b[1, :shard].astype(F32)).astype(BF16)
    result[1] = out[1]
    grad = own_part[1] + from_sib[1].astype(F32)
    result[2] = norm_back(far[0, :shard], grad, hidden_grad[shard : 2 * shard, :], gain).astype(BF16)


def last_kernel(
    own, part_a, sib_a, part_b, sib_b, returned, hidden_grad, gain, out, output, grad_input
):
    rows, shard, width = out.shape
    row = moved_row(rows)
    other = rows - 1 - row
    output[row] = out[0]
    output[1] = out[2]
    output[other] = returned[1]
    grad_input[other] = returned[2]
    grad = part_a[0] + sib_a[0].astype(F32)
    grad_input[row] = norm_back(own[0, :shard], grad, hidden_grad[0:shard, :], gain).astype(BF16)
    grad = part_b[0] + sib_b[0, :shard].astype(F32) + returned[0].astype(F32)
    grad_input[1] = norm_back(own[1, :shard], grad, hidden_grad[2 * shard :, :], gain).astype(BF16)


def unpack_kernel(ranks, mid, near_pack, far_pack, _, g1, g2, shared, dl, dr, ul, ur, bd, bu):
    width = near_pack.shape[1]
    pack = near_pack[...] + far_pack[...]
    inner, outer = mid // ranks, width // ranks
    g1[...] = pack[0]
    g2[...] = pack[1]
    bu[...] = pack[2]
    bd[...] = pack[3, 0:mid]
    dl[...] = pack[4:8, 0:outer]
    ur[...] = pack[4:8, 256 : 256 + outer]
    dr[...] = pack[4:8, 512 : 512 + inner]
    ul[...] = pack[4:8, 640 : 640 + inner]
    for i, at in enumerate(shared_slots):
        shared[i] = pack[4:8, at : at + ranks]


def two_parts(value):
    high = value.astype(BF16)
    return high, (value - high.astype(F32)).astype(BF16)


def sum_kernel(pack, from_sib, total):
    shard = from_sib.shape[1] - 16
    high, low = two_parts(pack[...])
    theirs = from_sib[1, shard:, :].astype(F32)
    total[...] = (high.astype(F32) + low.astype(F32)) + (theirs[0:8] + theirs[8:16])


def exchange(value, axis, bit):
    count = lax.axis_size(axis)
    return lax.ppermute(value, axis, [(k, k ^ bit) for k in range(count)])


def shards(
    inputs, cotangent, segment_ids, bucket_table, position_bias, query_weight, key_weight, value_weight, out_weight,
    hidden_in, hidden_out, gain_first, gain_second, shared, down_left, down_right, up_left_vectors, up_right,
    bias_down, bias_up,
):
    rows, shard, width = inputs.shape
    heads = position_bias.shape[1]
    hidden = hidden_in.shape[1]
    parts = lax.axis_size("seq")
    ranks, mid = shared.shape[0], bias_down.shape[0]
    pairs, tokens, keys = heads // 2, rows * shard, shard * parts
    lanes = width // pairs
    inner, outer, square = mid // ranks, width // ranks, ranks * ranks
    padded = shard + 16

    own, a_send, b_send, cot_send = call(
        pick_kernel,
        [((2, padded, width), BF16), ((1, padded, width), BF16), ((1, padded, width), BF16), ((1, shard, width), BF16)],
        (Far(inputs), Far(cotangent), Far(segment_ids)),
        8,
        1.0,
        [((rows, shard), jnp.int32)],
        6,
    )
    a_far = exchange(a_send, "seq", 2)
    b_far = exchange(b_send, "seq", 2)
    cot_far = exchange(cot_send, "seq", 2)
    sib = exchange(own, "seq", 1)

    small = (
        bucket_table, jnp.transpose(position_bias), shared, down_left, down_right, up_left_vectors, up_right,
        bias_down, bias_up, gain_first, gain_second,
    )
    large = (query_weight, key_weight, value_weight, out_weight, hidden_in, hidden_out)
    tiles, down_t, up, *expanded = call(
        functools.partial(setup_kernel, shard, parts),
        [((2 * parts - 1, pairs, 2 * shard, shard), F32), ((mid, width), BF16), ((mid, width), BF16)]
        + [((square, mid), F32)] * 4 + [((square, width), F32)] * 2
        + [(x.shape, x.dtype) for x in small[7:] + large],
        [Far(x) for x in small + large],
        8,
        4.0,
        [((16, 2 * keys), F32), ((square, ranks), F32), ((square, ranks), F32)]
        + [(x.shape, x.dtype) for x in small[:7]],
        len(small) + len(large),
    )
    bd, bu, gain1, gain2, wq, wk, wv, wo, win, wout = expanded[6:]
    expanded = expanded[:6]
    k_loc, v_loc, q_loc = call(
        local_kernel,
        [((pairs, 4 * shard, lanes), BF16), ((pairs, 4 * shard, lanes), BF16), ((pairs, 2 * shard, lanes), BF16)],
        (own, sib, wq, wk, wv, gain1),
        8,
        2.0,
    )
    a_far, k_loc = lax.optimization_barrier((a_far, k_loc))
    a_far_sib = exchange(a_far, "seq", 1)
    a_far_sib, b_far = lax.optimization_barrier((a_far_sib, b_far))
    b_far_sib = exchange(b_far, "seq", 1)
    proj = ((pairs, 2 * shard, lanes), BF16)
    weights = (wq, wk, wv, wo, gain1)
    ka, va, qa, ea, ctx_a, rinv_a, hid_a = call(
        functools.partial(attention_kernel, True),
        [
            proj, proj, ((pairs, shard, lanes), BF16), ((2 * pairs, 2 * shard, keys), BF16),
            ((pairs, 2 * shard, lanes), F32), ((pairs, 2 * shard, lanes), F32), ((2 * shard, width), F32),
        ],
        (own, sib, a_far, a_far_sib, k_loc, v_loc, q_loc, tiles, *weights),
        12,
        3.0,
    )
    kb, vb, eb, ctx_b, rinv_b, hid_b = call(
        functools.partial(attention_kernel, False),
        [
            proj, proj, ((pairs, 2 * shard, keys), BF16),
            ((pairs, shard, lanes), F32), ((pairs, shard, lanes), F32), ((shard, width), F32),
        ],
        (own, sib, b_far, b_far_sib, k_loc, v_loc, q_loc, tiles, *weights),
        12,
        3.0,
    )
    out, hidden_grad, dctx, grad_up, grad_down_t, lines = call(
        middle_kernel,
        [
            ((rows, shard, width), BF16), ((tokens, width), F32), ((pairs, tokens, lanes), BF16),
            ((mid, width), F32), ((mid, width), F32), ((8, width), F32),
        ],
        (
            hid_a, hid_b, cotangent, cot_far, win, wout, wo, gain2, bd, bu, down_t, up,
        ),
        20,
        12.0,
        [((tokens, width), BF16), ((tokens, hidden), BF16), ((tokens, hidden), BF16)],
    )
    turned = [((pairs, lanes, keys), BF16)] * 2
    part_a, sib_part_a, pack_a = call(
        functools.partial(backward_kernel, True, ranks),
        [((2, shard, width), F32), ((2, shard, width), BF16), ((8, width), F32)],
        (
            own, sib, a_far, a_far_sib, dctx, ctx_a, rinv_a, ea, k_loc, v_loc, q_loc, ka, va, qa,
            wq, wk, wv, grad_up, grad_down_t, lines, *expanded,
        ),
        14,
        6.0,
        turned,
    )
    sib_a = exchange(sib_part_a, "seq", 1)
    part_b, far_part, sib_part_b, pack = call(
        functools.partial(backward_kernel, False, ranks),
        [((1, shard, width), F32), ((1, shard, width), BF16), ((2, padded, width), BF16), ((8, width), F32)],
        (
            own, sib, b_far, b_far_sib, dctx, ctx_b, rinv_b, eb, k_loc, v_loc, q_loc, kb, vb,
            wq, wk, wv, pack_a,
        ),
        14,
        3.6,
        turned,
    )
    sib_part_b, sib_a = lax.optimization_barrier((sib_part_b, sib_a))
    sib_b = exchange(sib_part_b, "seq", 1)
    (pack,) = call(sum_kernel, [((8, width), F32)], (pack, sib_b), 8, 0.1)
    (back,) = call(
        return_kernel,
        [((rows, shard, width), BF16)],
        (pack, a_far, part_a, sib_a, far_part, sib_b, out, hidden_grad, gain1),
        16,
        0.5,
    )
    returned = exchange(back, "seq", 2)
    bit = 1
    while bit < lax.axis_size("batch"):
        pack = pack + exchange(pack, "batch", bit)
        bit *= 2
    far_pack = exchange(pack, "seq", 2)
    output, grad_input = call(
        last_kernel,
        [((rows, shard, width), BF16), ((rows, shard, width), BF16)],
        (own, part_a, sib_a, part_b, sib_b, returned, hidden_grad, gain1, out),
        16,
        1.0,
        last=True,
    )
    grads = call(
        functools.partial(unpack_kernel, ranks, mid),
        [
            ((width,), F32), ((width,), F32), ((ranks, ranks, ranks), F32), ((ranks, outer), F32),
            ((ranks, inner), F32), ((ranks, inner), F32), ((ranks, outer), F32), ((mid,), F32), ((width,), F32),
        ],
        (pack, far_pack, Far(grad_input)),
        8,
        0.5,
        last=True,
    )
    return (output, grad_input, *grads)


def solution(mesh):
    rows = P("batch", "seq", None)
    in_specs = (rows, rows, P("batch", "seq")) + (P(),) * 17
    out_specs = (rows, rows) + (P(),) * 9
    return jax.shard_map(shards, mesh=mesh, in_specs=in_specs, out_specs=out_specs, check_vma=False)
```

```python
import functools

import jax
import jax.numpy as jnp
from jax import lax
from jax.experimental import pallas as pl
from jax.experimental.pallas import tpu as pltpu
from jax.sharding import PartitionSpec as P

F32 = jnp.float32
BF16 = jnp.bfloat16
HI = lax.Precision.HIGHEST
epsilon = 1e-06
masked = -1e30
gelu_a = 0.7978845608028654
gelu_b = 0.044715
MIB = 1024 * 1024
VM = pl.BlockSpec(memory_space=pltpu.VMEM)


def dot(a, b, precision=None):
    return lax.dot_general(a, b, (((1,), (0,)), ((), ())), precision=precision, preferred_element_type=F32)


def dot_nt(a, b, precision=None):
    return lax.dot_general(a, b, (((1,), (1,)), ((), ())), precision=precision, preferred_element_type=F32)


def dot_tn(a, b, precision=None):
    return lax.dot_general(a, b, (((0,), (0,)), ((), ())), precision=precision, preferred_element_type=F32)


def iota(shape, axis):
    return lax.broadcasted_iota(jnp.int32, shape, axis)


def block_of(index, size, count):
    total = jnp.zeros_like(index)
    for k in range(1, count):
        total = total + (index >= k * size).astype(jnp.int32)
    return total


def gelu_pair(v):
    square = v * v
    h = 0.5 + 0.5 * jnp.tanh(v * (gelu_a + gelu_a * gelu_b * square))
    g = v * h
    slope = h + (g - g * h) * (2.0 * gelu_a + 6.0 * gelu_a * gelu_b * square)
    return g, slope


def inverse_rms(x):
    return lax.rsqrt(jnp.mean(x * x, -1, keepdims=True) + epsilon)


class Far:
    def __init__(self, value):
        self.value = value


def near(value):
    return pltpu.with_memory_space_constraint(value, pltpu.VMEM)


def call(kernel, outs, args, limit, micros, scratch=(), copies=0, last=False):
    specs = [pl.BlockSpec(memory_space=pl.ANY) if isinstance(a, Far) else VM for a in args]
    args = [pltpu.with_memory_space_constraint(a.value, pltpu.HBM) if isinstance(a, Far) else near(a) for a in args]
    scratch = [pltpu.VMEM(shape, kind) for shape, kind in scratch]
    if copies:
        scratch.append(pltpu.SemaphoreType.DMA((copies,)))
    made = jax.ShapeDtypeStruct if last else pltpu.VMEM
    return pl.pallas_call(
        kernel,
        out_shape=[made(shape, kind) for shape, kind in outs],
        in_specs=specs,
        out_specs=[VM] * len(outs),
        scratch_shapes=scratch,
        compiler_params=pltpu.CompilerParams(vmem_limit_bytes=limit * MIB),
        cost_estimate=pl.CostEstimate(flops=int(micros * 1.1e9), bytes_accessed=0, transcendentals=0),
    )(*args)


def start_copies(pairs, sems):
    started = [pltpu.make_async_copy(source, target, sems.at[k]) for k, (source, target) in enumerate(pairs)]
    for one in started:
        one.start()
    return started


def pick_kernel(inputs, cotangent, segment_ids, own, a_send, b_send, cot_send, ids, sems):
    rows, shard, width = inputs.shape
    extra = own.shape[1] - shard
    row = moved_row(rows)
    other = rows - 1 - row
    body = pl.ds(0, shard)
    started = start_copies(
        [
            (segment_ids, ids),
            (inputs.at[other], a_send.at[0, body]),
            (inputs.at[1], b_send.at[0, body]),
            (inputs.at[row], own.at[0, body]),
            (inputs.at[1], own.at[1, body]),
            (cotangent.at[other], cot_send.at[0]),
        ],
        sems,
    )
    started[0].wait()
    for target, k, source in ((own, 0, row), (own, 1, 1), (a_send, 0, other), (b_send, 0, 1)):
        line = jnp.broadcast_to(ids[pl.ds(source, 1), :].astype(F32).astype(BF16), (extra, shard))
        target[k, shard:, :] = jnp.zeros((extra, width), BF16)
        target[k, shard:, 0:shard] = line
    for one in started[1:]:
        one.wait()


def setup_kernel(
    shard, parts, table_far, position_far, shared_far, dl_far, dr_far, ul_far, ur_far, bd_far, bu_far, g1_far, g2_far,
    wq_far, wk_far, wv_far, wo_far, win_far, wout_far,
    tiles, down_t, up, mix, side, left, bd, bu, g1, g2, wq, wk, wv, wo, win, wout,
    tab, sh16, sh16t, table, position_bias, shared, dl, dr, ul, ur, sems,
):
    started = start_copies(
        [
            (table_far, table), (position_far, position_bias), (shared_far, shared), (dl_far, dl), (dr_far, dr),
            (ul_far, ul), (ur_far, ur), (bd_far, bd), (bu_far, bu), (g1_far, g1), (g2_far, g2),
            (wq_far, wq), (wk_far, wk), (wv_far, wv), (wo_far, wo), (win_far, win), (wout_far, wout),
        ],
        sems,
    )
    for one in started[:11]:
        one.wait()
    heads = position_bias.shape[0]
    ranks, (mid, width) = shared.shape[0], down_t.shape
    inner, outer = mid // ranks, width // ranks
    square = ranks * ranks
    hits = (table[...][None, :] == iota((position_bias.shape[1], table.shape[0]), 0)).astype(F32)
    tab[0:heads, 0 : table.shape[0]] = dot(position_bias[...], hits, HI)
    for k in range(2 * parts - 1):
        for h in range(heads):
            line = tab[h : h + 1, k * shard : (k + 2) * shard]
            turned = pltpu.roll(jnp.broadcast_to(line, (shard, 2 * shard)), shard + 1, 1, stride=1, stride_axis=0)
            tiles[k, h // 2, (h % 2) * shard : (h % 2 + 1) * shard, :] = turned[:, :shard]
    eye = (iota((ranks, ranks), 0) == iota((ranks, ranks), 1)).astype(F32)
    for i in range(ranks):
        block = shared[i]
        sh16[i * ranks : (i + 1) * ranks, :] = block
        sh16t[i * ranks : (i + 1) * ranks, :] = dot_tn(block, eye, HI)
    spread, by_c, by_j, by_b, own_block = selectors(ranks, mid, width)
    mix[...] = jnp.zeros(mix.shape, F32)
    side[...] = jnp.zeros(side.shape, F32)
    shx, shtx = dot(sh16[...], by_c, HI), dot(sh16t[...], by_c, HI)
    drx, ulx = dot(dot(spread, dr[...], HI), by_j, HI), dot(dot(spread, ul[...], HI), by_j, HI)
    dlx = dot(dot(spread, dl[...], HI), by_b, HI) * own_block
    urx = dot(dot(spread, ur[...], HI), by_b, HI) * own_block
    mix[:square, :mid] = shx
    mix[square:, mid:] = shtx
    side[:square, :mid] = drx
    side[square:, mid:] = ulx
    left[:square, :] = dlx
    left[square:, :] = urx
    down_t[...] = dot_tn(shx * drx, dlx, HI).astype(BF16)
    up[...] = dot_tn(shtx * ulx, urx, HI).astype(BF16)
    for one in started[11:]:
        one.wait()


def selectors(ranks, mid, width):
    inner, outer, square = mid // ranks, width // ranks, ranks * ranks
    spread = (block_of(iota((square, ranks), 0), ranks, ranks) == iota((square, ranks), 1)).astype(F32)
    by_c = (block_of(iota((ranks, mid), 1), inner, ranks) == iota((ranks, mid), 0)).astype(F32)
    column = iota((inner, mid), 1)
    by_j = (column - inner * block_of(column, inner, ranks) == iota((inner, mid), 0)).astype(F32)
    column = iota((outer, width), 1)
    by_b = (column - outer * block_of(column, outer, ranks) == iota((outer, width), 0)).astype(F32)
    line = iota((square, width), 0)
    own_block = (
        line - ranks * block_of(line, ranks, ranks) == block_of(iota((square, width), 1), outer, ranks)
    ).astype(F32)
    return spread, by_c, by_j, by_b, own_block


def moved_row(rows):
    half = lax.axis_size("seq") // 2
    return jnp.where(lax.axis_index("seq") < half, 0, rows - 1)


def normed(x, gain):
    x = x.astype(F32)
    return (x * inverse_rms(x) * gain[...][None, :]).astype(BF16)


def project(x, weight, target, at):
    pairs, _, lanes = target.shape
    count = x.shape[0]
    for t in range(pairs // 2):
        result = dot(x, weight[:, 2 * t * lanes : (2 * t + 2) * lanes]).astype(BF16)
        target[2 * t, at : at + count, :] = result[:, :lanes]
        target[2 * t + 1, at : at + count, :] = result[:, lanes:]


def local_kernel(own, sib, wq, wk, wv, gain, k_loc, v_loc, q_loc):
    shard = q_loc.shape[1] // 2
    blocks = [normed(x, gain) for x in (own[0, :shard], sib[0, :shard], own[1, :shard], sib[1, :shard])]
    x = jnp.concatenate(blocks, 0)
    project(x, wk, k_loc, 0)
    project(x, wv, v_loc, 0)
    project(jnp.concatenate([blocks[0], blocks[2]], 0), wq, q_loc, 0)


def segment_features(blocks, shard, lanes):
    lane = iota((shard, lanes), 1)
    keys, queries = [], []
    for block in blocks:
        line = block[shard : shard + 1, 0:shard].astype(F32)
        same = lane.astype(F32) == jnp.transpose(jnp.broadcast_to(line, (lanes, shard)))
        keys.append(same.astype(F32).astype(BF16))
        queries.append(jnp.where((lane < 3) & jnp.logical_not(same), masked, 0.0).astype(BF16))
    return jnp.concatenate(keys, 0), queries


def halves(lanes):
    low = iota((1, lanes), 1) < lanes // 2
    low_lane = low.astype(F32).astype(BF16)
    return low, low_lane, 1.0 - low_lane


def attention_kernel(
    is_moved, own, sib, far, far_sib, k_loc, v_loc, q_loc, tiles,
    wq, wk, wv, wo, gain, k_rem, v_rem, *rest,
):
    pairs, _, lanes = k_rem.shape
    shard = q_loc.shape[1] // 2
    if is_moved:
        q_rem, e, ctx, rinv, hid = rest
        first, queries = 0, [0, 2]
    else:
        e, ctx, rinv, hid = rest
        first, queries = 1, [0]
    place = lax.axis_index("seq")
    parts = lax.axis_size("seq")
    far_low = normed(far[0, :shard], gain)
    x = jnp.concatenate([far_low, normed(far_sib[0, :shard], gain)], 0)
    project(x, wk, k_rem, 0)
    project(x, wv, v_rem, 0)
    if is_moved:
        project(far_low, wq, q_rem, 0)
    key_feature, query_feature = segment_features(
        (own.at[first], sib.at[first], far.at[0], far_sib.at[0]), shard, lanes
    )
    local = slice(2 * first * shard, 2 * (first + 1) * shard)
    contexts = [[] for _ in queries]
    low, low_lane, high_lane = halves(lanes)
    for p in range(pairs):
        keys = jnp.concatenate([k_loc[p, local, :], k_rem[p]], 0)
        values = jnp.concatenate([v_loc[p, local, :], v_rem[p]], 0)
        lefts, biases = [], []
        for block in queries:
            q = q_rem[p] if block == 2 else q_loc[p, first * shard : (first + 1) * shard, :]
            feature = query_feature[block]
            lefts.append(jnp.concatenate([q * low_lane, feature], 1))
            lefts.append(jnp.concatenate([q * high_lane, feature], 1))
            at = jnp.bitwise_xor(place, block)
            biases.append(
                jnp.concatenate([tiles[jnp.bitwise_xor(place, k) - at + parts - 1, p] for k in range(parts)], 1)
            )
        scores = dot_nt(jnp.concatenate(lefts, 0), jnp.concatenate([keys, key_feature], 1))
        scores = scores + jnp.concatenate(biases, 0)
        weights = jnp.exp(scores - jnp.max(scores, 1, keepdims=True)).astype(BF16)
        both = dot(weights, jnp.concatenate([values, jnp.ones(values.shape, BF16)], 1))
        scale = 1.0 / both[:, lanes:]
        mixed = both[:, :lanes] * scale
        for b in range(len(queries)):
            one = slice(2 * b * shard, (2 * b + 1) * shard)
            two = slice((2 * b + 1) * shard, (2 * b + 2) * shard)
            span = slice(b * shard, (b + 1) * shard)
            e[b * pairs + p] = weights[2 * b * shard : 2 * (b + 1) * shard]
            kept = jnp.where(low, mixed[one], mixed[two])
            ctx[p, span, :] = kept
            rinv[p, span, :] = jnp.where(low, scale[one], scale[two])
            contexts[b].append(kept.astype(BF16))
    context = jnp.concatenate([jnp.concatenate(c, 1) for c in contexts], 0)
    x = jnp.concatenate([own[first, :shard]] + ([far[0, :shard]] if is_moved else []), 0).astype(F32)
    hid[...] = x + dot(context, wo[...])


def middle_kernel(
    hid_a, hid_b, cot, cot_far, win, wout, wo, gain2, bd, bu, down_t, up,
    out, hidden_grad, dctx, adapter_grad, lines, low, act, gslope,
):
    rows, shard, width = cot.shape
    hidden = win.shape[1]
    pairs, _, lanes = dctx.shape
    state = jnp.concatenate([hid_a[...], hid_b[...]], 0)
    inv2 = inverse_rms(state)
    low[...] = (state * inv2 * gain2[...][None, :]).astype(BF16)
    chunk = 2 * lanes
    for j in range(hidden // chunk):
        cols = slice(j * chunk, (j + 1) * chunk)
        g, slope = gelu_pair(dot(low[...], win[:, cols]))
        gslope[:, cols] = slope.astype(BF16)
        act[:, cols] = g.astype(BF16)
    branch = dot(act[...], wout[...])
    row = moved_row(rows)
    branch_low = branch.astype(BF16)
    g, slope = gelu_pair(dot_nt(branch_low, down_t[...]) + bd[...][None, :])
    g_low = g.astype(BF16)
    up_low = jnp.concatenate([cot[row], cot_far[0], cot[1]], 0)
    upstream = up_low.astype(F32)
    gb = dot_nt(up_low, up[...]) * slope
    gb_low = gb.astype(BF16)
    low[...] = (upstream + dot(gb_low, down_t[...])).astype(BF16)
    result = state + branch + dot(g_low, up[...]) + bu[...][None, :]
    for b in range(rows):
        out[b] = result[b * shard : (b + 1) * shard].astype(BF16)
    mid = g.shape[1]
    adapter_grad[:mid, :] = dot_tn(gb_low, branch_low)
    adapter_grad[mid:, :] = dot_tn(g_low, up_low)
    grad2 = jnp.zeros((rows * shard, width), F32)
    chunk = 6 * lanes
    for j in range(hidden // chunk):
        cols = slice(j * chunk, (j + 1) * chunk)
        pre = (dot_nt(low[...], wout[cols, :]) * gslope[:, cols].astype(F32)).astype(BF16)
        grad2 = grad2 + dot_nt(pre, win[:, cols])
    state = jnp.concatenate([hid_a[...], hid_b[...]], 0)
    inv2 = inverse_rms(state)
    hat2 = state * inv2
    c = grad2 * gain2[...][None, :]
    total = upstream + inv2 * (c - hat2 * jnp.mean(hat2 * c, -1, keepdims=True))
    hidden_grad[...] = total
    low[...] = total.astype(BF16)
    lines[...] = jnp.zeros(lines.shape, F32)
    lines[0:1, :] = jnp.sum(grad2 * hat2, 0, keepdims=True)
    lines[1:2, :] = jnp.sum(upstream, 0, keepdims=True)
    lines[2:3, 0 : gb.shape[1]] = jnp.sum(gb, 0, keepdims=True)
    for t in range(pairs // 2):
        part = dot_nt(low[...], wo[2 * t * lanes : (2 * t + 2) * lanes, :]).astype(BF16)
        dctx[2 * t] = part[:, :lanes]
        dctx[2 * t + 1] = part[:, lanes:]


def backward_kernel(
    is_moved, ranks, own, sib, far, far_sib, dctx, ctx, rinv, e, k_loc, v_loc, q_loc, k_rem, v_rem, *rest,
):
    pairs, _, lanes = dctx.shape
    shard, width = q_loc.shape[1] // 2, pairs * lanes
    if is_moved:
        q_rem, wq, wk, wv, *rest = rest
        *small, own_part, sib_part, pack, dkt, dvt = rest
        first, blocks, start = 0, 2, 0
    else:
        wq, wk, wv, pack_a, own_part, far_part, sib_part, pack, dkt, dvt = rest
        first, blocks, start = 1, 1, 2
    low, low_lane, high_lane = halves(lanes)
    low_row = (iota((lanes, 1), 0) < lanes // 2).astype(F32).astype(BF16)
    high_row = 1.0 - low_row
    local = slice(2 * first * shard, 2 * (first + 1) * shard)
    query_grads = [[] for _ in range(blocks)]

    def prepare(p):
        lefts, deltas, turned_q, turned_s = [], [], [], []
        for b in range(blocks):
            span = slice(b * shard, (b + 1) * shard)
            scaled = dctx[p, (start + b) * shard : (start + b + 1) * shard, :].astype(F32) * rinv[p, span, :]
            product = scaled * ctx[p, span, :]
            deltas.append(jnp.sum(jnp.where(low, product, 0.0), 1, keepdims=True))
            deltas.append(jnp.sum(jnp.where(low, 0.0, product), 1, keepdims=True))
            scaled = scaled.astype(BF16)
            lefts += [scaled * low_lane, scaled * high_lane]
            q = q_rem[p] if b == 1 else q_loc[p, first * shard : (first + 1) * shard, :]
            q_t, s_t = jnp.transpose(q), jnp.transpose(scaled)
            turned_q += [q_t * low_row, q_t * high_row]
            turned_s += [s_t * low_row, s_t * high_row]
        weights = jnp.concatenate([e[b * pairs + p] for b in range(blocks)], 0)
        values = jnp.concatenate([v_loc[p, local, :], v_rem[p]], 0)
        slopes = dot_nt(jnp.concatenate(lefts, 0), values) - jnp.concatenate(deltas, 0)
        steep = weights * slopes.astype(BF16)
        return jnp.concatenate(turned_q, 1), jnp.concatenate(turned_s, 1), weights, steep

    prepared = [prepare(p) for p in range(pairs)]
    for p, (turned_q, turned_s, weights, steep) in enumerate(prepared):
        keys = jnp.concatenate([k_loc[p, local, :], k_rem[p]], 0)
        grad_q = dot(steep, keys)
        for b in range(blocks):
            one = grad_q[2 * b * shard : (2 * b + 1) * shard]
            two = grad_q[(2 * b + 1) * shard : (2 * b + 2) * shard]
            query_grads[b].append(jnp.where(low, one, two).astype(BF16))
        dkt[p] = dot(turned_q, steep).astype(BF16)
        dvt[p] = dot(turned_s, weights).astype(BF16)
    keys = dkt.shape[2]
    key_t = dkt[...].reshape(width, keys)
    value_t = dvt[...].reshape(width, keys)
    part = jnp.transpose(dot(wk[...], key_t) + dot(wv[...], value_t))
    from_q = dot_nt(jnp.concatenate([jnp.concatenate(g, 1) for g in query_grads], 0), wq[...])
    pieces = [part[k * shard : (k + 1) * shard] for k in range(4)]
    pieces[0] = pieces[0] + from_q[:shard]
    if is_moved:
        pieces[2] = pieces[2] + from_q[shard:]
    gain = jnp.zeros((1, width), F32)
    for piece, x in zip(pieces, (own[first], sib[first], far[0], far_sib[0])):
        x = x[:shard].astype(F32)
        gain = gain + jnp.sum(piece * (x * inverse_rms(x)), 0, keepdims=True)
    if is_moved:
        pack_small(ranks, *small, pack)
        pack[0:1, :] = gain
        own_part[0] = pieces[0]
        own_part[1] = pieces[2]
    else:
        pack[...] = pack_a[...]
        pack[0:1, :] = pack_a[0:1, :] + gain
        own_part[0] = pieces[0]
        far_part[0] = pieces[2].astype(BF16)
    sib_part[0, :shard] = pieces[1].astype(BF16)
    sib_part[1, :shard] = pieces[3].astype(BF16)


def pack_small(ranks, grads, lines, mix, side, left, pack):
    mid, width = grads.shape[0] // 2, grads.shape[1]
    inner, outer, square = mid // ranks, width // ranks, ranks * ranks
    line = iota((2 * square, width), 0)
    line = line - ranks * block_of(line, ranks, 2 * ranks)
    own_block = (line == block_of(iota((2 * square, width), 1), outer, ranks)).astype(F32)
    factor = block_of(iota((2 * ranks, 2 * square), 1), ranks, 2 * ranks)
    spread = (factor == iota((2 * ranks, 2 * square), 0)).astype(F32)
    column = iota((outer, width), 1)
    by_b = (column - outer * block_of(column, outer, ranks) == iota((outer, width), 0)).astype(F32)
    group = block_of(iota((2 * ranks, 2 * mid), 1), inner, 2 * ranks)
    by_c = (group == iota((2 * ranks, 2 * mid), 0)).astype(F32)
    column = iota((2 * inner, 2 * mid), 1)
    place = column - inner * block_of(column, inner, 2 * ranks) + inner * (column >= mid).astype(jnp.int32)
    by_j = (place == iota((2 * inner, 2 * mid), 0)).astype(F32)
    column = iota((2 * ranks, square), 1)
    major = block_of(column, ranks, ranks)
    minor = column - ranks * major
    row = iota((2 * ranks, square), 0)
    widen = jnp.where(row < ranks, (row == minor).astype(F32), (row - ranks == major).astype(F32))
    column = iota((2 * square, square), 1)
    major = block_of(column, ranks, ranks)
    minor = column - ranks * major
    row = iota((2 * square, square), 0)
    inside = row - ranks * block_of(row, ranks, 2 * ranks)
    keep = jnp.where(row < square, (inside == major).astype(F32), (inside == minor).astype(F32))
    grads = grads[...]
    product = dot_nt(left[...], grads)
    ends = dot_nt(dot(spread, dot(mix[...] * side[...], grads) * own_block), by_b)
    sides = dot_nt(dot(spread, product * mix[...]), by_j)
    core = dot(spread, dot(dot_nt(product * side[...], by_c), widen) * keep)
    pack[...] = jnp.zeros(pack.shape, F32)
    pack[1:4, :] = lines[0:3, :]
    pack[4:8, 0:outer] = ends[:ranks]
    pack[4:8, 256 : 256 + outer] = ends[ranks:]
    pack[4:8, 512 : 512 + inner] = sides[:ranks, :inner]
    pack[4:8, 640 : 640 + inner] = sides[ranks:, inner:]
    pack[4:8, 704 : 704 + square] = core[:ranks] + core[ranks:]


def norm_back(x, grad, hidden_grad, gain):
    x = x.astype(F32)
    inv = inverse_rms(x)
    hat = x * inv
    c = grad * gain[...][None, :]
    return hidden_grad + inv * (c - hat * jnp.mean(hat * c, -1, keepdims=True))


def return_kernel(_, far, own_part, from_sib, far_part, from_sib_b, out, hidden_grad, gain, result):
    shard = out.shape[1]
    result[0] = (far_part[0].astype(F32) + from_sib_b[1, :shard].astype(F32)).astype(BF16)
    result[1] = out[1]
    grad = own_part[1] + from_sib[1].astype(F32)
    result[2] = norm_back(far[0, :shard], grad, hidden_grad[shard : 2 * shard, :], gain).astype(BF16)


def last_kernel(
    own, part_a, sib_a, part_b, sib_b, returned, hidden_grad, gain, out, output, grad_input
):
    rows, shard, width = out.shape
    row = moved_row(rows)
    other = rows - 1 - row
    output[row] = out[0]
    output[1] = out[2]
    output[other] = returned[1]
    grad_input[other] = returned[2]
    grad = part_a[0] + sib_a[0].astype(F32)
    grad_input[row] = norm_back(own[0, :shard], grad, hidden_grad[0:shard, :], gain).astype(BF16)
    grad = part_b[0] + sib_b[0, :shard].astype(F32) + returned[0].astype(F32)
    grad_input[1] = norm_back(own[1, :shard], grad, hidden_grad[2 * shard :, :], gain).astype(BF16)


def unpack_kernel(ranks, mid, near_pack, far_pack, _, g1, g2, shared, dl, dr, ul, ur, bd, bu):
    width = near_pack.shape[1]
    pack = near_pack[...] + far_pack[...]
    inner, outer = mid // ranks, width // ranks
    g1[...] = pack[0]
    g2[...] = pack[1]
    bu[...] = pack[2]
    bd[...] = pack[3, 0:mid]
    dl[...] = pack[4:8, 0:outer]
    ur[...] = pack[4:8, 256 : 256 + outer]
    dr[...] = pack[4:8, 512 : 512 + inner]
    ul[...] = pack[4:8, 640 : 640 + inner]
    for k in range(ranks):
        shared[:, k, :] = pack[4:8, 704 + k * ranks : 704 + (k + 1) * ranks]


def exchange(value, axis, bit):
    count = lax.axis_size(axis)
    return lax.ppermute(value, axis, [(k, k ^ bit) for k in range(count)])


def shards(
    inputs, cotangent, segment_ids, bucket_table, position_bias, query_weight, key_weight, value_weight, out_weight,
    hidden_in, hidden_out, gain_first, gain_second, shared, down_left, down_right, up_left_vectors, up_right,
    bias_down, bias_up,
):
    rows, shard, width = inputs.shape
    heads = position_bias.shape[1]
    hidden = hidden_in.shape[1]
    parts = lax.axis_size("seq")
    ranks, mid = shared.shape[0], bias_down.shape[0]
    pairs, tokens, keys = heads // 2, rows * shard, shard * parts
    lanes = width // pairs
    inner, outer, square = mid // ranks, width // ranks, ranks * ranks
    padded = shard + 8

    own, a_send, b_send, cot_send = call(
        pick_kernel,
        [((2, padded, width), BF16), ((1, padded, width), BF16), ((1, padded, width), BF16), ((1, shard, width), BF16)],
        (Far(inputs), Far(cotangent), Far(segment_ids)),
        8,
        1.0,
        [((rows, shard), jnp.int32)],
        6,
    )
    a_far = exchange(a_send, "seq", 2)
    b_far = exchange(b_send, "seq", 2)
    cot_far = exchange(cot_send, "seq", 2)
    sib = exchange(own, "seq", 1)

    small = (
        bucket_table, jnp.transpose(position_bias), shared, down_left, down_right, up_left_vectors, up_right,
        bias_down, bias_up, gain_first, gain_second,
    )
    large = (query_weight, key_weight, value_weight, out_weight, hidden_in, hidden_out)
    tiles, down_t, up, *expanded = call(
        functools.partial(setup_kernel, shard, parts),
        [((2 * parts - 1, pairs, 2 * shard, shard), F32), ((mid, width), BF16), ((mid, width), BF16)]
        + [((2 * square, 2 * mid), F32)] * 2 + [((2 * square, width), F32)]
        + [(x.shape, x.dtype) for x in small[7:] + large],
        [Far(x) for x in small + large],
        8,
        4.0,
        [((16, 2 * keys), F32), ((square, ranks), F32), ((square, ranks), F32)]
        + [(x.shape, x.dtype) for x in small[:7]],
        len(small) + len(large),
    )
    bd, bu, gain1, gain2, wq, wk, wv, wo, win, wout = expanded[3:]
    expanded = expanded[:3]
    k_loc, v_loc, q_loc = call(
        local_kernel,
        [((pairs, 4 * shard, lanes), BF16), ((pairs, 4 * shard, lanes), BF16), ((pairs, 2 * shard, lanes), BF16)],
        (own, sib, wq, wk, wv, gain1),
        8,
        2.0,
    )
    a_far, k_loc = lax.optimization_barrier((a_far, k_loc))
    a_far_sib = exchange(a_far, "seq", 1)
    a_far_sib, b_far = lax.optimization_barrier((a_far_sib, b_far))
    b_far_sib = exchange(b_far, "seq", 1)
    proj = ((pairs, 2 * shard, lanes), BF16)
    weights = (wq, wk, wv, wo, gain1)
    ka, va, qa, ea, ctx_a, rinv_a, hid_a = call(
        functools.partial(attention_kernel, True),
        [
            proj, proj, ((pairs, shard, lanes), BF16), ((2 * pairs, 2 * shard, keys), BF16),
            ((pairs, 2 * shard, lanes), F32), ((pairs, 2 * shard, lanes), F32), ((2 * shard, width), F32),
        ],
        (own, sib, a_far, a_far_sib, k_loc, v_loc, q_loc, tiles, *weights),
        12,
        3.0,
    )
    kb, vb, eb, ctx_b, rinv_b, hid_b = call(
        functools.partial(attention_kernel, False),
        [
            proj, proj, ((pairs, 2 * shard, keys), BF16),
            ((pairs, shard, lanes), F32), ((pairs, shard, lanes), F32), ((shard, width), F32),
        ],
        (own, sib, b_far, b_far_sib, k_loc, v_loc, q_loc, tiles, *weights),
        12,
        3.0,
    )
    out, hidden_grad, dctx, adapter_grad, lines = call(
        middle_kernel,
        [
            ((rows, shard, width), BF16), ((tokens, width), F32), ((pairs, tokens, lanes), BF16),
            ((2 * mid, width), F32), ((8, width), F32),
        ],
        (
            hid_a, hid_b, cotangent, cot_far, win, wout, wo, gain2, bd, bu, down_t, up,
        ),
        20,
        12.0,
        [((tokens, width), BF16), ((tokens, hidden), BF16), ((tokens, hidden), BF16)],
    )
    turned = [((pairs, lanes, keys), BF16)] * 2
    part_a, sib_part_a, pack_a = call(
        functools.partial(backward_kernel, True, ranks),
        [((2, shard, width), F32), ((2, shard, width), BF16), ((8, width), F32)],
        (
            own, sib, a_far, a_far_sib, dctx, ctx_a, rinv_a, ea, k_loc, v_loc, q_loc, ka, va, qa,
            wq, wk, wv, adapter_grad, lines, *expanded,
        ),
        14,
        6.0,
        turned,
    )
    sib_a = exchange(sib_part_a, "seq", 1)
    part_b, far_part, sib_part_b, pack = call(
        functools.partial(backward_kernel, False, ranks),
        [((1, shard, width), F32), ((1, shard, width), BF16), ((2, shard, width), BF16), ((8, width), F32)],
        (
            own, sib, b_far, b_far_sib, dctx, ctx_b, rinv_b, eb, k_loc, v_loc, q_loc, kb, vb,
            wq, wk, wv, pack_a,
        ),
        14,
        3.6,
        turned,
    )
    sib_part_b, sib_a = lax.optimization_barrier((sib_part_b, sib_a))
    sib_b = exchange(sib_part_b, "seq", 1)
    pack = pack + exchange(pack, "seq", 1)
    (back,) = call(
        return_kernel,
        [((rows, shard, width), BF16)],
        (pack, a_far, part_a, sib_a, far_part, sib_b, out, hidden_grad, gain1),
        16,
        0.5,
    )
    returned = exchange(back, "seq", 2)
    bit = 1
    while bit < lax.axis_size("batch"):
        pack = pack + exchange(pack, "batch", bit)
        bit *= 2
    far_pack = exchange(pack, "seq", 2)
    output, grad_input = call(
        last_kernel,
        [((rows, shard, width), BF16), ((rows, shard, width), BF16)],
        (own, part_a, sib_a, part_b, sib_b, returned, hidden_grad, gain1, out),
        16,
        1.0,
        last=True,
    )
    grads = call(
        functools.partial(unpack_kernel, ranks, mid),
        [
            ((width,), F32), ((width,), F32), ((ranks, ranks, ranks), F32), ((ranks, outer), F32),
            ((ranks, inner), F32), ((ranks, inner), F32), ((ranks, outer), F32), ((mid,), F32), ((width,), F32),
        ],
        (pack, far_pack, Far(grad_input)),
        8,
        0.5,
        last=True,
    )
    return (output, grad_input, *grads)


def solution(mesh):
    rows = P("batch", "seq", None)
    in_specs = (rows, rows, P("batch", "seq")) + (P(),) * 17
    out_specs = (rows, rows) + (P(),) * 9
    return jax.shard_map(shards, mesh=mesh, in_specs=in_specs, out_specs=out_specs, check_vma=False)
```

```python
import functools

import jax
import jax.numpy as jnp
from jax import lax
from jax.experimental import pallas as pl
from jax.experimental.pallas import tpu as pltpu
from jax.sharding import PartitionSpec as P

F32 = jnp.float32
BF16 = jnp.bfloat16
HI = lax.Precision.HIGHEST
epsilon = 1e-06
masked = -1e30
gelu_a = 0.7978845608028654
gelu_b = 0.044715
MIB = 1024 * 1024
VM = pl.BlockSpec(memory_space=pltpu.VMEM)


def dot(a, b, precision=None):
    return lax.dot_general(a, b, (((1,), (0,)), ((), ())), precision=precision, preferred_element_type=F32)


def dot_nt(a, b, precision=None):
    return lax.dot_general(a, b, (((1,), (1,)), ((), ())), precision=precision, preferred_element_type=F32)


def dot_tn(a, b, precision=None):
    return lax.dot_general(a, b, (((0,), (0,)), ((), ())), precision=precision, preferred_element_type=F32)


def iota(shape, axis):
    return lax.broadcasted_iota(jnp.int32, shape, axis)


def block_of(index, size, count):
    total = jnp.zeros_like(index)
    for k in range(1, count):
        total = total + (index >= k * size).astype(jnp.int32)
    return total


def gelu_pair(v):
    square = v * v
    h = 0.5 + 0.5 * jnp.tanh(v * (gelu_a + gelu_a * gelu_b * square))
    g = v * h
    slope = h + (g - g * h) * (2.0 * gelu_a + 6.0 * gelu_a * gelu_b * square)
    return g, slope


def inverse_rms(x):
    return lax.rsqrt(jnp.mean(x * x, -1, keepdims=True) + epsilon)


class Far:
    def __init__(self, value):
        self.value = value


def near(value):
    return pltpu.with_memory_space_constraint(value, pltpu.VMEM)


def call(kernel, outs, args, limit, micros, scratch=(), copies=0, last=False):
    specs = [pl.BlockSpec(memory_space=pl.ANY) if isinstance(a, Far) else VM for a in args]
    args = [pltpu.with_memory_space_constraint(a.value, pltpu.HBM) if isinstance(a, Far) else near(a) for a in args]
    scratch = [pltpu.VMEM(shape, kind) for shape, kind in scratch]
    if copies:
        scratch.append(pltpu.SemaphoreType.DMA((copies,)))
    made = jax.ShapeDtypeStruct if last else pltpu.VMEM
    return pl.pallas_call(
        kernel,
        out_shape=[made(shape, kind) for shape, kind in outs],
        in_specs=specs,
        out_specs=[VM] * len(outs),
        scratch_shapes=scratch,
        compiler_params=pltpu.CompilerParams(vmem_limit_bytes=limit * MIB),
        cost_estimate=pl.CostEstimate(flops=int(micros * 1.1e9), bytes_accessed=0, transcendentals=0),
    )(*args)


def start_copies(pairs, sems):
    started = [pltpu.make_async_copy(source, target, sems.at[k]) for k, (source, target) in enumerate(pairs)]
    for one in started:
        one.start()
    return started


def pick_kernel(inputs, cotangent, segment_ids, own, a_send, b_send, cot_send, ids, sems):
    rows, shard, width = inputs.shape
    extra = own.shape[1] - shard
    row = moved_row(rows)
    other = rows - 1 - row
    body = pl.ds(0, shard)
    started = start_copies(
        [
            (segment_ids, ids),
            (inputs.at[other], a_send.at[0, body]),
            (inputs.at[1], b_send.at[0, body]),
            (inputs.at[row], own.at[0, body]),
            (inputs.at[1], own.at[1, body]),
            (cotangent.at[other], cot_send.at[0]),
        ],
        sems,
    )
    started[0].wait()
    for target, k, source in ((own, 0, row), (own, 1, 1), (a_send, 0, other), (b_send, 0, 1)):
        line = jnp.broadcast_to(ids[pl.ds(source, 1), :].astype(F32).astype(BF16), (extra, shard))
        target[k, shard:, :] = jnp.zeros((extra, width), BF16)
        target[k, shard:, 0:shard] = line
    for one in started[1:]:
        one.wait()


def setup_kernel(
    shard, parts, table_far, position_far, shared_far, dl_far, dr_far, ul_far, ur_far, bd_far, bu_far, g1_far, g2_far,
    wq_far, wk_far, wv_far, wo_far, wout_far,
    tiles, down_t, up, mix, side, left, bd, bu, g1, g2, wq, wk, wv, wo, wout,
    tab, sh16, sh16t, table, position_bias, shared, dl, dr, ul, ur, sems,
):
    started = start_copies(
        [
            (table_far, table), (position_far, position_bias), (shared_far, shared), (dl_far, dl), (dr_far, dr),
            (ul_far, ul), (ur_far, ur), (bd_far, bd), (bu_far, bu), (g1_far, g1), (g2_far, g2),
            (wq_far, wq), (wk_far, wk), (wv_far, wv), (wo_far, wo), (wout_far, wout),
        ],
        sems,
    )
    for one in started[:11]:
        one.wait()
    heads = position_bias.shape[0]
    ranks, (mid, width) = shared.shape[0], down_t.shape
    inner, outer = mid // ranks, width // ranks
    square = ranks * ranks
    hits = (table[...][None, :] == iota((position_bias.shape[1], table.shape[0]), 0)).astype(F32)
    tab[0:heads, 0 : table.shape[0]] = dot(position_bias[...], hits, HI)
    for k in range(2 * parts - 1):
        for h in range(heads):
            line = tab[h : h + 1, k * shard : (k + 2) * shard]
            turned = pltpu.roll(jnp.broadcast_to(line, (shard, 2 * shard)), shard + 1, 1, stride=1, stride_axis=0)
            tiles[k, h // 2, (h % 2) * shard : (h % 2 + 1) * shard, :] = turned[:, :shard]
    eye = (iota((ranks, ranks), 0) == iota((ranks, ranks), 1)).astype(F32)
    for i in range(ranks):
        block = shared[i]
        sh16[i * ranks : (i + 1) * ranks, :] = block
        sh16t[i * ranks : (i + 1) * ranks, :] = dot_tn(block, eye, HI)
    spread, by_c, by_j, by_b, own_block = selectors(ranks, mid, width)
    mix[...] = jnp.zeros(mix.shape, F32)
    side[...] = jnp.zeros(side.shape, F32)
    shx, shtx = dot(sh16[...], by_c, HI), dot(sh16t[...], by_c, HI)
    drx, ulx = dot(dot(spread, dr[...], HI), by_j, HI), dot(dot(spread, ul[...], HI), by_j, HI)
    dlx = dot(dot(spread, dl[...], HI), by_b, HI) * own_block
    urx = dot(dot(spread, ur[...], HI), by_b, HI) * own_block
    mix[:square, :mid] = shx
    mix[square:, mid:] = shtx
    side[:square, :mid] = drx
    side[square:, mid:] = ulx
    left[:square, :] = dlx
    left[square:, :] = urx
    down_t[...] = dot_tn(shx * drx, dlx, HI).astype(BF16)
    up[...] = dot_tn(shtx * ulx, urx, HI).astype(BF16)
    for one in started[11:]:
        one.wait()


def selectors(ranks, mid, width):
    inner, outer, square = mid // ranks, width // ranks, ranks * ranks
    spread = (block_of(iota((square, ranks), 0), ranks, ranks) == iota((square, ranks), 1)).astype(F32)
    by_c = (block_of(iota((ranks, mid), 1), inner, ranks) == iota((ranks, mid), 0)).astype(F32)
    column = iota((inner, mid), 1)
    by_j = (column - inner * block_of(column, inner, ranks) == iota((inner, mid), 0)).astype(F32)
    column = iota((outer, width), 1)
    by_b = (column - outer * block_of(column, outer, ranks) == iota((outer, width), 0)).astype(F32)
    line = iota((square, width), 0)
    own_block = (
        line - ranks * block_of(line, ranks, ranks) == block_of(iota((square, width), 1), outer, ranks)
    ).astype(F32)
    return spread, by_c, by_j, by_b, own_block


def moved_row(rows):
    half = lax.axis_size("seq") // 2
    return jnp.where(lax.axis_index("seq") < half, 0, rows - 1)


def normed(x, gain):
    x = x.astype(F32)
    return (x * inverse_rms(x) * gain[...][None, :]).astype(BF16)


def project(x, weight, target, at):
    pairs, _, lanes = target.shape
    count = x.shape[0]
    for t in range(pairs // 2):
        result = dot(x, weight[:, 2 * t * lanes : (2 * t + 2) * lanes]).astype(BF16)
        target[2 * t, at : at + count, :] = result[:, :lanes]
        target[2 * t + 1, at : at + count, :] = result[:, lanes:]


def local_kernel(own, sib, wq, wk, wv, gain, k_loc, v_loc, q_loc):
    shard = q_loc.shape[1] // 2
    blocks = [normed(x, gain) for x in (own[0, :shard], sib[0, :shard], own[1, :shard], sib[1, :shard])]
    x = jnp.concatenate(blocks, 0)
    project(x, wk, k_loc, 0)
    project(x, wv, v_loc, 0)
    project(jnp.concatenate([blocks[0], blocks[2]], 0), wq, q_loc, 0)


def segment_features(blocks, shard, lanes):
    lane = iota((shard, lanes), 1)
    keys, queries = [], []
    for block in blocks:
        line = block[shard : shard + 1, 0:shard].astype(F32)
        same = lane.astype(F32) == jnp.transpose(jnp.broadcast_to(line, (lanes, shard)))
        keys.append(same.astype(F32).astype(BF16))
        queries.append(jnp.where((lane < 3) & jnp.logical_not(same), masked, 0.0).astype(BF16))
    return jnp.concatenate(keys, 0), queries


def halves(lanes):
    low = iota((1, lanes), 1) < lanes // 2
    low_lane = low.astype(F32).astype(BF16)
    return low, low_lane, 1.0 - low_lane


def attention_kernel(
    is_moved, own, sib, far, far_sib, k_loc, v_loc, q_loc, tiles,
    wq, wk, wv, wo, gain, *rest,
):
    pairs, _, lanes = k_loc.shape
    shard = q_loc.shape[1] // 2
    if is_moved:
        win_far, k_rem, v_rem, q_rem, e, ctx, rinv, hid, win, sems = rest
        fetches = start_copies([(win_far, win)], sems)
        first, queries = 0, [0, 2]
    else:
        k_rem, v_rem, e, ctx, rinv, hid = rest
        fetches = []
        first, queries = 1, [0]
    place = lax.axis_index("seq")
    parts = lax.axis_size("seq")
    far_low = normed(far[0, :shard], gain)
    x = jnp.concatenate([far_low, normed(far_sib[0, :shard], gain)], 0)
    project(x, wk, k_rem, 0)
    project(x, wv, v_rem, 0)
    if is_moved:
        project(far_low, wq, q_rem, 0)
    key_feature, query_feature = segment_features(
        (own.at[first], sib.at[first], far.at[0], far_sib.at[0]), shard, lanes
    )
    local = slice(2 * first * shard, 2 * (first + 1) * shard)
    contexts = [[] for _ in queries]
    low, low_lane, high_lane = halves(lanes)
    for p in range(pairs):
        keys = jnp.concatenate([k_loc[p, local, :], k_rem[p]], 0)
        values = jnp.concatenate([v_loc[p, local, :], v_rem[p]], 0)
        lefts, biases = [], []
        for block in queries:
            q = q_rem[p] if block == 2 else q_loc[p, first * shard : (first + 1) * shard, :]
            feature = query_feature[block]
            lefts.append(jnp.concatenate([q * low_lane, feature], 1))
            lefts.append(jnp.concatenate([q * high_lane, feature], 1))
            at = jnp.bitwise_xor(place, block)
            biases.append(
                jnp.concatenate([tiles[jnp.bitwise_xor(place, k) - at + parts - 1, p] for k in range(parts)], 1)
            )
        scores = dot_nt(jnp.concatenate(lefts, 0), jnp.concatenate([keys, key_feature], 1))
        scores = scores + jnp.concatenate(biases, 0)
        weights = jnp.exp(scores - jnp.max(scores, 1, keepdims=True)).astype(BF16)
        both = dot(weights, jnp.concatenate([values, jnp.ones(values.shape, BF16)], 1))
        scale = 1.0 / both[:, lanes:]
        mixed = both[:, :lanes] * scale
        for b in range(len(queries)):
            one = slice(2 * b * shard, (2 * b + 1) * shard)
            two = slice((2 * b + 1) * shard, (2 * b + 2) * shard)
            span = slice(b * shard, (b + 1) * shard)
            e[b * pairs + p] = weights[2 * b * shard : 2 * (b + 1) * shard]
            kept = jnp.where(low, mixed[one], mixed[two])
            ctx[p, span, :] = kept
            rinv[p, span, :] = jnp.where(low, scale[one], scale[two])
            contexts[b].append(kept.astype(BF16))
    context = jnp.concatenate([jnp.concatenate(c, 1) for c in contexts], 0)
    x = jnp.concatenate([own[first, :shard]] + ([far[0, :shard]] if is_moved else []), 0).astype(F32)
    hid[...] = x + dot(context, wo[...])
    for one in fetches:
        one.wait()


def middle_kernel(
    hid_a, hid_b, cot, cot_far, win, wout, wo, gain2, bd, bu, down_t, up,
    out, out_send, hidden_grad, dctx, adapter_grad, lines, low, act, gslope,
):
    rows, shard, width = cot.shape
    hidden = win.shape[1]
    pairs, _, lanes = dctx.shape
    state = jnp.concatenate([hid_a[...], hid_b[...]], 0)
    inv2 = inverse_rms(state)
    low[...] = (state * inv2 * gain2[...][None, :]).astype(BF16)
    chunk = 2 * lanes
    for j in range(hidden // chunk):
        cols = slice(j * chunk, (j + 1) * chunk)
        g, slope = gelu_pair(dot(low[...], win[:, cols]))
        gslope[:, cols] = slope.astype(BF16)
        act[:, cols] = g.astype(BF16)
    branch = dot(act[...], wout[...])
    row = moved_row(rows)
    branch_low = branch.astype(BF16)
    g, slope = gelu_pair(dot_nt(branch_low, down_t[...]) + bd[...][None, :])
    g_low = g.astype(BF16)
    up_low = jnp.concatenate([cot[row], cot_far[0], cot[1]], 0)
    upstream = up_low.astype(F32)
    gb = dot_nt(up_low, up[...]) * slope
    gb_low = gb.astype(BF16)
    low[...] = (upstream + dot(gb_low, down_t[...])).astype(BF16)
    result = state + branch + dot(g_low, up[...]) + bu[...][None, :]
    for b in range(rows):
        out[b] = result[b * shard : (b + 1) * shard].astype(BF16)
    out_send[0] = result[shard : 2 * shard].astype(BF16)
    mid = g.shape[1]
    adapter_grad[:mid, :] = dot_tn(gb_low, branch_low)
    adapter_grad[mid:, :] = dot_tn(g_low, up_low)
    grad2 = jnp.zeros((rows * shard, width), F32)
    chunk = 6 * lanes
    for j in range(hidden // chunk):
        cols = slice(j * chunk, (j + 1) * chunk)
        pre = (dot_nt(low[...], wout[cols, :]) * gslope[:, cols].astype(F32)).astype(BF16)
        grad2 = grad2 + dot_nt(pre, win[:, cols])
    state = jnp.concatenate([hid_a[...], hid_b[...]], 0)
    inv2 = inverse_rms(state)
    hat2 = state * inv2
    c = grad2 * gain2[...][None, :]
    total = upstream + inv2 * (c - hat2 * jnp.mean(hat2 * c, -1, keepdims=True))
    hidden_grad[...] = total
    low[...] = total.astype(BF16)
    lines[...] = jnp.zeros(lines.shape, F32)
    lines[0:1, :] = jnp.sum(grad2 * hat2, 0, keepdims=True)
    lines[1:2, :] = jnp.sum(upstream, 0, keepdims=True)
    lines[2:3, 0 : gb.shape[1]] = jnp.sum(gb, 0, keepdims=True)
    for t in range(pairs // 2):
        part = dot_nt(low[...], wo[2 * t * lanes : (2 * t + 2) * lanes, :]).astype(BF16)
        dctx[2 * t] = part[:, :lanes]
        dctx[2 * t + 1] = part[:, lanes:]


def backward_kernel(
    is_moved, ranks, own, sib, far, far_sib, dctx, ctx, rinv, e, k_loc, v_loc, q_loc, k_rem, v_rem, *rest,
):
    pairs, _, lanes = dctx.shape
    shard, width = q_loc.shape[1] // 2, pairs * lanes
    if is_moved:
        q_rem, wq, wk, wv, *rest = rest
        *small, own_part, sib_part, pack, dkt, dvt = rest
        first, blocks, start = 0, 2, 0
    else:
        wq, wk, wv, pack_a, own_part, far_part, sib_part, pack, dkt, dvt = rest
        first, blocks, start = 1, 1, 2
    low, low_lane, high_lane = halves(lanes)
    low_row = (iota((lanes, 1), 0) < lanes // 2).astype(F32).astype(BF16)
    high_row = 1.0 - low_row
    local = slice(2 * first * shard, 2 * (first + 1) * shard)
    query_grads = [[] for _ in range(blocks)]

    def prepare(p):
        lefts, deltas, turned_q, turned_s = [], [], [], []
        for b in range(blocks):
            span = slice(b * shard, (b + 1) * shard)
            scaled = dctx[p, (start + b) * shard : (start + b + 1) * shard, :].astype(F32) * rinv[p, span, :]
            product = scaled * ctx[p, span, :]
            deltas.append(jnp.sum(jnp.where(low, product, 0.0), 1, keepdims=True))
            deltas.append(jnp.sum(jnp.where(low, 0.0, product), 1, keepdims=True))
            scaled = scaled.astype(BF16)
            lefts += [scaled * low_lane, scaled * high_lane]
            q = q_rem[p] if b == 1 else q_loc[p, first * shard : (first + 1) * shard, :]
            q_t, s_t = jnp.transpose(q), jnp.transpose(scaled)
            turned_q += [q_t * low_row, q_t * high_row]
            turned_s += [s_t * low_row, s_t * high_row]
        weights = jnp.concatenate([e[b * pairs + p] for b in range(blocks)], 0)
        values = jnp.concatenate([v_loc[p, local, :], v_rem[p]], 0)
        slopes = dot_nt(jnp.concatenate(lefts, 0), values) - jnp.concatenate(deltas, 0)
        steep = weights * slopes.astype(BF16)
        return jnp.concatenate(turned_q, 1), jnp.concatenate(turned_s, 1), weights, steep

    prepared = [prepare(p) for p in range(pairs)]
    for p, (turned_q, turned_s, weights, steep) in enumerate(prepared):
        keys = jnp.concatenate([k_loc[p, local, :], k_rem[p]], 0)
        grad_q = dot(steep, keys)
        for b in range(blocks):
            one = grad_q[2 * b * shard : (2 * b + 1) * shard]
            two = grad_q[(2 * b + 1) * shard : (2 * b + 2) * shard]
            query_grads[b].append(jnp.where(low, one, two).astype(BF16))
        dkt[p] = dot(turned_q, steep).astype(BF16)
        dvt[p] = dot(turned_s, weights).astype(BF16)
    keys = dkt.shape[2]
    key_t = dkt[...].reshape(width, keys)
    value_t = dvt[...].reshape(width, keys)
    part = jnp.transpose(dot(wk[...], key_t) + dot(wv[...], value_t))
    from_q = dot_nt(jnp.concatenate([jnp.concatenate(g, 1) for g in query_grads], 0), wq[...])
    pieces = [part[k * shard : (k + 1) * shard] for k in range(4)]
    pieces[0] = pieces[0] + from_q[:shard]
    if is_moved:
        pieces[2] = pieces[2] + from_q[shard:]
    gain = jnp.zeros((1, width), F32)
    for piece, x in zip(pieces, (own[first], sib[first], far[0], far_sib[0])):
        x = x[:shard].astype(F32)
        gain = gain + jnp.sum(piece * (x * inverse_rms(x)), 0, keepdims=True)
    if is_moved:
        pack_small(ranks, *small, pack)
        pack[0:1, :] = gain
        own_part[0] = pieces[0]
        own_part[1] = pieces[2]
    else:
        pack[...] = pack_a[...]
        pack[0:1, :] = pack_a[0:1, :] + gain
        own_part[0] = pieces[0]
        far_part[0] = pieces[2].astype(BF16)
    sib_part[0, :shard] = pieces[1].astype(BF16)
    sib_part[1, :shard] = pieces[3].astype(BF16)


def pack_small(ranks, grads, lines, mix, side, left, pack):
    mid, width = grads.shape[0] // 2, grads.shape[1]
    inner, outer, square = mid // ranks, width // ranks, ranks * ranks
    line = iota((2 * square, width), 0)
    line = line - ranks * block_of(line, ranks, 2 * ranks)
    own_block = (line == block_of(iota((2 * square, width), 1), outer, ranks)).astype(F32)
    factor = block_of(iota((2 * ranks, 2 * square), 1), ranks, 2 * ranks)
    spread = (factor == iota((2 * ranks, 2 * square), 0)).astype(F32)
    column = iota((outer, width), 1)
    by_b = (column - outer * block_of(column, outer, ranks) == iota((outer, width), 0)).astype(F32)
    group = block_of(iota((2 * ranks, 2 * mid), 1), inner, 2 * ranks)
    by_c = (group == iota((2 * ranks, 2 * mid), 0)).astype(F32)
    column = iota((2 * inner, 2 * mid), 1)
    place = column - inner * block_of(column, inner, 2 * ranks) + inner * (column >= mid).astype(jnp.int32)
    by_j = (place == iota((2 * inner, 2 * mid), 0)).astype(F32)
    column = iota((2 * ranks, square), 1)
    major = block_of(column, ranks, ranks)
    minor = column - ranks * major
    row = iota((2 * ranks, square), 0)
    widen = jnp.where(row < ranks, (row == minor).astype(F32), (row - ranks == major).astype(F32))
    column = iota((2 * square, square), 1)
    major = block_of(column, ranks, ranks)
    minor = column - ranks * major
    row = iota((2 * square, square), 0)
    inside = row - ranks * block_of(row, ranks, 2 * ranks)
    keep = jnp.where(row < square, (inside == major).astype(F32), (inside == minor).astype(F32))
    grads = grads[...]
    product = dot_nt(left[...], grads)
    ends = dot_nt(dot(spread, dot(mix[...] * side[...], grads) * own_block), by_b)
    sides = dot_nt(dot(spread, product * mix[...]), by_j)
    core = dot(spread, dot(dot_nt(product * side[...], by_c), widen) * keep)
    pack[...] = jnp.zeros(pack.shape, F32)
    pack[1:4, :] = lines[0:3, :]
    pack[4:8, 0:outer] = ends[:ranks]
    pack[4:8, 256 : 256 + outer] = ends[ranks:]
    pack[4:8, 512 : 512 + inner] = sides[:ranks, :inner]
    pack[4:8, 640 : 640 + inner] = sides[ranks:, inner:]
    pack[4:8, 704 : 704 + square] = core[:ranks] + core[ranks:]


def norm_back(x, grad, hidden_grad, gain):
    x = x.astype(F32)
    inv = inverse_rms(x)
    hat = x * inv
    c = grad * gain[...][None, :]
    return hidden_grad + inv * (c - hat * jnp.mean(hat * c, -1, keepdims=True))


def return_kernel(far, own_part, from_sib, far_part, from_sib_b, hidden_grad, gain, far_sum, back):
    shard = back.shape[1]
    far_sum[0] = (far_part[0].astype(F32) + from_sib_b[1, :shard].astype(F32)).astype(BF16)
    grad = own_part[1] + from_sib[1].astype(F32)
    back[0] = norm_back(far[0, :shard], grad, hidden_grad[shard : 2 * shard, :], gain).astype(BF16)


def last_kernel(
    own, part_a, sib_a, part_b, sib_b, far_sum, hidden_grad, gain, out, out_far, back, output, grad_input
):
    rows, shard, width = out.shape
    row = moved_row(rows)
    other = rows - 1 - row
    output[row] = out[0]
    output[1] = out[2]
    output[other] = out_far[0]
    grad_input[other] = back[0]
    grad = part_a[0] + sib_a[0].astype(F32)
    grad_input[row] = norm_back(own[0, :shard], grad, hidden_grad[0:shard, :], gain).astype(BF16)
    grad = part_b[0] + sib_b[0].astype(F32) + far_sum[0].astype(F32)
    grad_input[1] = norm_back(own[1, :shard], grad, hidden_grad[2 * shard :, :], gain).astype(BF16)


def unpack_kernel(ranks, mid, near_pack, far_pack, _, g1, g2, shared, dl, dr, ul, ur, bd, bu):
    width = near_pack.shape[1]
    pack = near_pack[...] + far_pack[...]
    inner, outer = mid // ranks, width // ranks
    g1[...] = pack[0]
    g2[...] = pack[1]
    bu[...] = pack[2]
    bd[...] = pack[3, 0:mid]
    dl[...] = pack[4:8, 0:outer]
    ur[...] = pack[4:8, 256 : 256 + outer]
    dr[...] = pack[4:8, 512 : 512 + inner]
    ul[...] = pack[4:8, 640 : 640 + inner]
    for k in range(ranks):
        shared[:, k, :] = pack[4:8, 704 + k * ranks : 704 + (k + 1) * ranks]


def add_kernel(a, b, c):
    c[...] = a[...] + b[...]


def exchange(value, axis, bit):
    count = lax.axis_size(axis)
    return lax.ppermute(value, axis, [(k, k ^ bit) for k in range(count)])


def shards(
    inputs, cotangent, segment_ids, bucket_table, position_bias, query_weight, key_weight, value_weight, out_weight,
    hidden_in, hidden_out, gain_first, gain_second, shared, down_left, down_right, up_left_vectors, up_right,
    bias_down, bias_up,
):
    rows, shard, width = inputs.shape
    heads = position_bias.shape[1]
    hidden = hidden_in.shape[1]
    parts = lax.axis_size("seq")
    ranks, mid = shared.shape[0], bias_down.shape[0]
    pairs, tokens, keys = heads // 2, rows * shard, shard * parts
    lanes = width // pairs
    inner, outer, square = mid // ranks, width // ranks, ranks * ranks
    padded = shard + 8

    own, a_send, b_send, cot_send = call(
        pick_kernel,
        [((2, padded, width), BF16), ((1, padded, width), BF16), ((1, padded, width), BF16), ((1, shard, width), BF16)],
        (Far(inputs), Far(cotangent), Far(segment_ids)),
        8,
        1.0,
        [((rows, shard), jnp.int32)],
        6,
    )
    a_far = exchange(a_send, "seq", 2)
    b_far = exchange(b_send, "seq", 2)
    cot_far = exchange(cot_send, "seq", 2)
    sib = exchange(own, "seq", 1)

    small = (
        bucket_table, jnp.transpose(position_bias), shared, down_left, down_right, up_left_vectors, up_right,
        bias_down, bias_up, gain_first, gain_second,
    )
    large = (query_weight, key_weight, value_weight, out_weight, hidden_out)
    tiles, down_t, up, *expanded = call(
        functools.partial(setup_kernel, shard, parts),
        [((2 * parts - 1, pairs, 2 * shard, shard), F32), ((mid, width), BF16), ((mid, width), BF16)]
        + [((2 * square, 2 * mid), F32)] * 2 + [((2 * square, width), F32)]
        + [(x.shape, x.dtype) for x in small[7:] + large],
        [Far(x) for x in small + large],
        8,
        20.0,
        [((16, 2 * keys), F32), ((square, ranks), F32), ((square, ranks), F32)]
        + [(x.shape, x.dtype) for x in small[:7]],
        len(small) + len(large),
    )
    bd, bu, gain1, gain2, wq, wk, wv, wo, wout = expanded[3:]
    expanded = expanded[:3]
    k_loc, v_loc, q_loc = call(
        local_kernel,
        [((pairs, 4 * shard, lanes), BF16), ((pairs, 4 * shard, lanes), BF16), ((pairs, 2 * shard, lanes), BF16)],
        (own, sib, wq, wk, wv, gain1),
        8,
        20.0,
    )
    a_far, k_loc = lax.optimization_barrier((a_far, k_loc))
    a_far_sib = exchange(a_far, "seq", 1)
    a_far_sib, b_far = lax.optimization_barrier((a_far_sib, b_far))
    b_far_sib = exchange(b_far, "seq", 1)
    proj = ((pairs, 2 * shard, lanes), BF16)
    weights = (wq, wk, wv, wo, gain1)
    ka, va, qa, ea, ctx_a, rinv_a, hid_a, win = call(
        functools.partial(attention_kernel, True),
        [
            proj, proj, ((pairs, shard, lanes), BF16), ((2 * pairs, 2 * shard, keys), BF16),
            ((pairs, 2 * shard, lanes), F32), ((pairs, 2 * shard, lanes), F32), ((2 * shard, width), F32),
            (hidden_in.shape, BF16),
        ],
        (own, sib, a_far, a_far_sib, k_loc, v_loc, q_loc, tiles, *weights, Far(hidden_in)),
        12,
        3.0,
        copies=1,
    )
    kb, vb, eb, ctx_b, rinv_b, hid_b = call(
        functools.partial(attention_kernel, False),
        [
            proj, proj, ((pairs, 2 * shard, keys), BF16),
            ((pairs, shard, lanes), F32), ((pairs, shard, lanes), F32), ((shard, width), F32),
        ],
        (own, sib, b_far, b_far_sib, k_loc, v_loc, q_loc, tiles, *weights),
        12,
        3.0,
    )
    out, out_send, hidden_grad, dctx, adapter_grad, lines = call(
        middle_kernel,
        [
            ((rows, shard, width), BF16), ((1, shard, width), BF16), ((tokens, width), F32), ((pairs, tokens, lanes), BF16),
            ((2 * mid, width), F32), ((8, width), F32),
        ],
        (
            hid_a, hid_b, cotangent, cot_far, win, wout, wo, gain2, bd, bu, down_t, up,
        ),
        20,
        12.0,
        [((tokens, width), BF16), ((tokens, hidden), BF16), ((tokens, hidden), BF16)],
    )
    turned = [((pairs, lanes, keys), BF16)] * 2
    part_a, sib_part_a, pack_a = call(
        functools.partial(backward_kernel, True, ranks),
        [((2, shard, width), F32), ((2, shard, width), BF16), ((8, width), F32)],
        (
            own, sib, a_far, a_far_sib, dctx, ctx_a, rinv_a, ea, k_loc, v_loc, q_loc, ka, va, qa,
            wq, wk, wv, adapter_grad, lines, *expanded,
        ),
        14,
        6.0,
        turned,
    )
    sib_a = exchange(sib_part_a, "seq", 1)
    part_b, far_part, sib_part_b, pack = call(
        functools.partial(backward_kernel, False, ranks),
        [((1, shard, width), F32), ((1, shard, width), BF16), ((2, shard, width), BF16), ((8, width), F32)],
        (
            own, sib, b_far, b_far_sib, dctx, ctx_b, rinv_b, eb, k_loc, v_loc, q_loc, kb, vb,
            wq, wk, wv, pack_a,
        ),
        14,
        3.6,
        turned,
    )
    sib_part_b, sib_a = lax.optimization_barrier((sib_part_b, sib_a))
    sib_b = exchange(sib_part_b, "seq", 1)
    far_sum, back = call(
        return_kernel,
        [((1, shard, width), BF16), ((1, shard, width), BF16)],
        (a_far, part_a, sib_a, far_part, sib_b, hidden_grad, gain1),
        16,
        0.5,
    )
    far_sum = exchange(far_sum, "seq", 2)
    back = exchange(back, "seq", 2)
    out_far = exchange(out_send, "seq", 2)
    (pack,) = call(add_kernel, [((8, width), F32)], (pack, exchange(pack, "seq", 2)), 4, 10.0)
    bit = 1
    while 2 * bit < lax.axis_size("batch"):
        pack = pack + exchange(pack, "batch", bit)
        bit *= 2
    pack = pack + exchange(pack, "seq", 1)
    far_pack = exchange(pack, "batch", bit)
    rowed = ((rows, shard, width), BF16)
    output, grad_input = call(
        last_kernel,
        [rowed, rowed],
        (own, part_a, sib_a, part_b, sib_b, far_sum, hidden_grad, gain1, out, out_far, back),
        16,
        1.0,
        last=True,
    )
    grads = call(
        functools.partial(unpack_kernel, ranks, mid),
        [
            ((width,), F32), ((width,), F32), ((ranks, ranks, ranks), F32), ((ranks, outer), F32),
            ((ranks, inner), F32), ((ranks, inner), F32), ((ranks, outer), F32), ((mid,), F32), ((width,), F32),
        ],
        (pack, far_pack, Far(grad_input)),
        8,
        0.5,
        last=True,
    )
    return (output, grad_input, *grads)


def solution(mesh):
    rows = P("batch", "seq", None)
    in_specs = (rows, rows, P("batch", "seq")) + (P(),) * 17
    out_specs = (rows, rows) + (P(),) * 9
    return jax.shard_map(shards, mesh=mesh, in_specs=in_specs, out_specs=out_specs, check_vma=False)
```

```python
import functools

import jax
import jax.numpy as jnp
from jax import lax
from jax.experimental import pallas as pl
from jax.experimental.pallas import tpu as pltpu
from jax.sharding import PartitionSpec as P

F32 = jnp.float32
BF16 = jnp.bfloat16
HI = lax.Precision.HIGHEST
epsilon = 1e-06
masked = -1e30
gelu_a = 0.7978845608028654
gelu_b = 0.044715
MIB = 1024 * 1024
VM = pl.BlockSpec(memory_space=pltpu.VMEM)


def dot(a, b, precision=None):
    return lax.dot_general(a, b, (((1,), (0,)), ((), ())), precision=precision, preferred_element_type=F32)


def dot_nt(a, b, precision=None):
    return lax.dot_general(a, b, (((1,), (1,)), ((), ())), precision=precision, preferred_element_type=F32)


def dot_tn(a, b, precision=None):
    return lax.dot_general(a, b, (((0,), (0,)), ((), ())), precision=precision, preferred_element_type=F32)


def iota(shape, axis):
    return lax.broadcasted_iota(jnp.int32, shape, axis)


def block_of(index, size, count):
    total = jnp.zeros_like(index)
    for k in range(1, count):
        total = total + (index >= k * size).astype(jnp.int32)
    return total


def gelu_pair(v):
    square = v * v
    h = 0.5 + 0.5 * jnp.tanh(v * (gelu_a + gelu_a * gelu_b * square))
    g = v * h
    slope = h + (g - g * h) * (2.0 * gelu_a + 6.0 * gelu_a * gelu_b * square)
    return g, slope


def inverse_rms(x):
    return lax.rsqrt(jnp.mean(x * x, -1, keepdims=True) + epsilon)


class Far:
    def __init__(self, value):
        self.value = value


def near(value):
    return pltpu.with_memory_space_constraint(value, pltpu.VMEM)


def call(kernel, outs, args, limit, micros, scratch=(), copies=0, last=False, aliases=()):
    specs = [pl.BlockSpec(memory_space=pl.ANY) if isinstance(a, Far) else VM for a in args]
    args = [pltpu.with_memory_space_constraint(a.value, pltpu.HBM) if isinstance(a, Far) else near(a) for a in args]
    scratch = [pltpu.VMEM(shape, kind) for shape, kind in scratch]
    if copies:
        scratch.append(pltpu.SemaphoreType.DMA((copies,)))
    made = jax.ShapeDtypeStruct if last else pltpu.VMEM
    return pl.pallas_call(
        kernel,
        out_shape=[made(shape, kind) for shape, kind in outs],
        in_specs=specs,
        out_specs=[pl.BlockSpec(memory_space=pl.ANY if aliases else pltpu.VMEM)] * len(outs),
        input_output_aliases=dict(aliases),
        scratch_shapes=scratch,
        compiler_params=pltpu.CompilerParams(vmem_limit_bytes=limit * MIB),
        cost_estimate=pl.CostEstimate(flops=int(micros * 1.1e9), bytes_accessed=0, transcendentals=0),
    )(*args)


def start_copies(pairs, sems):
    started = [pltpu.make_async_copy(source, target, sems.at[k]) for k, (source, target) in enumerate(pairs)]
    for one in started:
        one.start()
    return started


def pick_kernel(inputs, cotangent, segment_ids, own, a_send, b_send, cot_send, ids, sems):
    rows, shard, width = inputs.shape
    extra = own.shape[1] - shard
    row = moved_row(rows)
    other = rows - 1 - row
    body = pl.ds(0, shard)
    started = start_copies(
        [
            (segment_ids, ids),
            (inputs.at[other], a_send.at[0, body]),
            (inputs.at[1], b_send.at[0, body]),
            (inputs.at[row], own.at[0, body]),
            (inputs.at[1], own.at[1, body]),
            (cotangent.at[other], cot_send.at[0]),
        ],
        sems,
    )
    started[0].wait()
    for target, k, source in ((own, 0, row), (own, 1, 1), (a_send, 0, other), (b_send, 0, 1)):
        line = jnp.broadcast_to(ids[pl.ds(source, 1), :].astype(F32).astype(BF16), (extra, shard))
        target[k, shard:, :] = jnp.zeros((extra, width), BF16)
        target[k, shard:, 0:shard] = line
    for one in started[1:]:
        one.wait()


def setup_kernel(
    shard, parts, table_far, position_far, shared_far, dl_far, dr_far, ul_far, ur_far, bd_far, bu_far, g1_far, g2_far,
    wq_far, wk_far, wv_far, wo_far, wout_far,
    tiles, down_t, up, mix, side, left, bd, bu, g1, g2, wq, wk, wv, wo, wout,
    tab, sh16, sh16t, table, position_bias, shared, dl, dr, ul, ur, sems,
):
    started = start_copies(
        [
            (table_far, table), (position_far, position_bias), (shared_far, shared), (dl_far, dl), (dr_far, dr),
            (ul_far, ul), (ur_far, ur), (bd_far, bd), (bu_far, bu), (g1_far, g1), (g2_far, g2),
            (wq_far, wq), (wk_far, wk), (wv_far, wv), (wo_far, wo), (wout_far, wout),
        ],
        sems,
    )
    for one in started[:11]:
        one.wait()
    heads = position_bias.shape[0]
    ranks, (mid, width) = shared.shape[0], down_t.shape
    inner, outer = mid // ranks, width // ranks
    square = ranks * ranks
    hits = (table[...][None, :] == iota((position_bias.shape[1], table.shape[0]), 0)).astype(F32)
    tab[0:heads, 0 : table.shape[0]] = dot(position_bias[...], hits, HI)
    for k in range(2 * parts - 1):
        for h in range(heads):
            line = tab[h : h + 1, k * shard : (k + 2) * shard]
            turned = pltpu.roll(jnp.broadcast_to(line, (shard, 2 * shard)), shard + 1, 1, stride=1, stride_axis=0)
            tiles[k, h // 2, (h % 2) * shard : (h % 2 + 1) * shard, :] = turned[:, :shard]
    eye = (iota((ranks, ranks), 0) == iota((ranks, ranks), 1)).astype(F32)
    for i in range(ranks):
        block = shared[i]
        sh16[i * ranks : (i + 1) * ranks, :] = block
        sh16t[i * ranks : (i + 1) * ranks, :] = dot_tn(block, eye, HI)
    spread, by_c, by_j, by_b, own_block = selectors(ranks, mid, width)
    mix[...] = jnp.zeros(mix.shape, F32)
    side[...] = jnp.zeros(side.shape, F32)
    shx, shtx = dot(sh16[...], by_c, HI), dot(sh16t[...], by_c, HI)
    drx, ulx = dot(dot(spread, dr[...], HI), by_j, HI), dot(dot(spread, ul[...], HI), by_j, HI)
    dlx = dot(dot(spread, dl[...], HI), by_b, HI) * own_block
    urx = dot(dot(spread, ur[...], HI), by_b, HI) * own_block
    mix[:square, :mid] = shx
    mix[square:, mid:] = shtx
    side[:square, :mid] = drx
    side[square:, mid:] = ulx
    left[:square, :] = dlx
    left[square:, :] = urx
    down_t[...] = dot_tn(shx * drx, dlx, HI).astype(BF16)
    up[...] = dot_tn(shtx * ulx, urx, HI).astype(BF16)
    for one in started[11:]:
        one.wait()


def selectors(ranks, mid, width):
    inner, outer, square = mid // ranks, width // ranks, ranks * ranks
    spread = (block_of(iota((square, ranks), 0), ranks, ranks) == iota((square, ranks), 1)).astype(F32)
    by_c = (block_of(iota((ranks, mid), 1), inner, ranks) == iota((ranks, mid), 0)).astype(F32)
    column = iota((inner, mid), 1)
    by_j = (column - inner * block_of(column, inner, ranks) == iota((inner, mid), 0)).astype(F32)
    column = iota((outer, width), 1)
    by_b = (column - outer * block_of(column, outer, ranks) == iota((outer, width), 0)).astype(F32)
    line = iota((square, width), 0)
    own_block = (
        line - ranks * block_of(line, ranks, ranks) == block_of(iota((square, width), 1), outer, ranks)
    ).astype(F32)
    return spread, by_c, by_j, by_b, own_block


def moved_row(rows):
    half = lax.axis_size("seq") // 2
    return jnp.where(lax.axis_index("seq") < half, 0, rows - 1)


def normed(x, gain):
    x = x.astype(F32)
    return (x * inverse_rms(x) * gain[...][None, :]).astype(BF16)


def project(x, weight, target, at):
    pairs, _, lanes = target.shape
    count = x.shape[0]
    for t in range(pairs // 2):
        result = dot(x, weight[:, 2 * t * lanes : (2 * t + 2) * lanes]).astype(BF16)
        target[2 * t, at : at + count, :] = result[:, :lanes]
        target[2 * t + 1, at : at + count, :] = result[:, lanes:]


def local_kernel(own, sib, wq, wk, wv, gain, k_loc, v_loc, q_loc):
    shard = q_loc.shape[1] // 2
    blocks = [normed(x, gain) for x in (own[0, :shard], sib[0, :shard], own[1, :shard], sib[1, :shard])]
    x = jnp.concatenate(blocks, 0)
    project(x, wk, k_loc, 0)
    project(x, wv, v_loc, 0)
    project(jnp.concatenate([blocks[0], blocks[2]], 0), wq, q_loc, 0)


def segment_features(blocks, shard, lanes):
    lane = iota((shard, lanes), 1)
    keys, queries = [], []
    for block in blocks:
        line = block[shard : shard + 1, 0:shard].astype(F32)
        same = lane.astype(F32) == jnp.transpose(jnp.broadcast_to(line, (lanes, shard)))
        keys.append(same.astype(F32).astype(BF16))
        queries.append(jnp.where((lane < 3) & jnp.logical_not(same), masked, 0.0).astype(BF16))
    return jnp.concatenate(keys, 0), queries


def halves(lanes):
    low = iota((1, lanes), 1) < lanes // 2
    low_lane = low.astype(F32).astype(BF16)
    return low, low_lane, 1.0 - low_lane


def attention_kernel(
    is_moved, own, sib, far, far_sib, k_loc, v_loc, q_loc, tiles,
    wq, wk, wv, wo, gain, *rest,
):
    pairs, _, lanes = k_loc.shape
    shard = q_loc.shape[1] // 2
    if is_moved:
        win_far, k_rem, v_rem, q_rem, e, ctx, rinv, hid, win, sems = rest
        fetches = start_copies([(win_far, win)], sems)
        first, queries = 0, [0, 2]
    else:
        k_rem, v_rem, e, ctx, rinv, hid = rest
        fetches = []
        first, queries = 1, [0]
    place = lax.axis_index("seq")
    parts = lax.axis_size("seq")
    far_low = normed(far[0, :shard], gain)
    x = jnp.concatenate([far_low, normed(far_sib[0, :shard], gain)], 0)
    project(x, wk, k_rem, 0)
    project(x, wv, v_rem, 0)
    if is_moved:
        project(far_low, wq, q_rem, 0)
    key_feature, query_feature = segment_features(
        (own.at[first], sib.at[first], far.at[0], far_sib.at[0]), shard, lanes
    )
    local = slice(2 * first * shard, 2 * (first + 1) * shard)
    contexts = [[] for _ in queries]
    low, low_lane, high_lane = halves(lanes)
    for p in range(pairs):
        keys = jnp.concatenate([k_loc[p, local, :], k_rem[p]], 0)
        values = jnp.concatenate([v_loc[p, local, :], v_rem[p]], 0)
        lefts, biases = [], []
        for block in queries:
            q = q_rem[p] if block == 2 else q_loc[p, first * shard : (first + 1) * shard, :]
            feature = query_feature[block]
            lefts.append(jnp.concatenate([q * low_lane, feature], 1))
            lefts.append(jnp.concatenate([q * high_lane, feature], 1))
            at = jnp.bitwise_xor(place, block)
            biases.append(
                jnp.concatenate([tiles[jnp.bitwise_xor(place, k) - at + parts - 1, p] for k in range(parts)], 1)
            )
        scores = dot_nt(jnp.concatenate(lefts, 0), jnp.concatenate([keys, key_feature], 1))
        scores = scores + jnp.concatenate(biases, 0)
        weights = jnp.exp(scores - jnp.max(scores, 1, keepdims=True)).astype(BF16)
        both = dot(weights, jnp.concatenate([values, jnp.ones(values.shape, BF16)], 1))
        scale = 1.0 / both[:, lanes:]
        mixed = both[:, :lanes] * scale
        for b in range(len(queries)):
            one = slice(2 * b * shard, (2 * b + 1) * shard)
            two = slice((2 * b + 1) * shard, (2 * b + 2) * shard)
            span = slice(b * shard, (b + 1) * shard)
            e[b * pairs + p] = weights[2 * b * shard : 2 * (b + 1) * shard]
            kept = jnp.where(low, mixed[one], mixed[two])
            ctx[p, span, :] = kept
            rinv[p, span, :] = jnp.where(low, scale[one], scale[two])
            contexts[b].append(kept.astype(BF16))
    context = jnp.concatenate([jnp.concatenate(c, 1) for c in contexts], 0)
    x = jnp.concatenate([own[first, :shard]] + ([far[0, :shard]] if is_moved else []), 0).astype(F32)
    hid[...] = x + dot(context, wo[...])
    for one in fetches:
        one.wait()


def middle_kernel(
    ranks, hid_a, hid_b, cot, cot_far, win, wout, gain2, bd, bu, down_t, up, mix, side, left,
    out, out_send, hidden_grad, low_grad, pack, low, act, gslope, adapter_grad,
):
    rows, shard, width = cot.shape
    hidden = win.shape[1]
    state = jnp.concatenate([hid_a[...], hid_b[...]], 0)
    inv2 = inverse_rms(state)
    low[...] = (state * inv2 * gain2[...][None, :]).astype(BF16)
    chunk = width // 3
    for j in range(hidden // chunk):
        cols = slice(j * chunk, (j + 1) * chunk)
        g, slope = gelu_pair(dot(low[...], win[:, cols]))
        gslope[:, cols] = slope.astype(BF16)
        act[:, cols] = g.astype(BF16)
    branch = dot(act[...], wout[...])
    row = moved_row(rows)
    branch_low = branch.astype(BF16)
    g, slope = gelu_pair(dot_nt(branch_low, down_t[...]) + bd[...][None, :])
    g_low = g.astype(BF16)
    up_low = jnp.concatenate([cot[row], cot_far[0], cot[1]], 0)
    upstream = up_low.astype(F32)
    gb = dot_nt(up_low, up[...]) * slope
    gb_low = gb.astype(BF16)
    low[...] = (upstream + dot(gb_low, down_t[...])).astype(BF16)
    result = state + branch + dot(g_low, up[...]) + bu[...][None, :]
    for b in range(rows):
        out[b] = result[b * shard : (b + 1) * shard].astype(BF16)
    out_send[0] = result[shard : 2 * shard].astype(BF16)
    mid = g.shape[1]
    adapter_grad[:mid, :] = dot_tn(gb_low, branch_low)
    adapter_grad[mid:, :] = dot_tn(g_low, up_low)
    grad2 = jnp.zeros((rows * shard, width), F32)
    chunk = width
    for j in range(hidden // chunk):
        cols = slice(j * chunk, (j + 1) * chunk)
        pre = (dot_nt(low[...], wout[cols, :]) * gslope[:, cols].astype(F32)).astype(BF16)
        if j == 1:
            pack_small(ranks, adapter_grad, mix, side, left, pack)
        grad2 = grad2 + dot_nt(pre, win[:, cols])
    state = jnp.concatenate([hid_a[...], hid_b[...]], 0)
    inv2 = inverse_rms(state)
    hat2 = state * inv2
    c = grad2 * gain2[...][None, :]
    total = upstream + inv2 * (c - hat2 * jnp.mean(hat2 * c, -1, keepdims=True))
    hidden_grad[...] = total
    low_grad[...] = total.astype(BF16)
    pack[1:2, :] = jnp.sum(grad2 * hat2, 0, keepdims=True)
    pack[2:3, :] = jnp.sum(upstream, 0, keepdims=True)
    pack[3:4, 0:mid] = jnp.sum(gb, 0, keepdims=True)


def backward_kernel(
    is_moved, own, sib, far, far_sib, ctx, rinv, e, k_loc, v_loc, q_loc, k_rem, v_rem, *rest,
):
    pairs, _, lanes = k_loc.shape
    shard, width = q_loc.shape[1] // 2, pairs * lanes
    if is_moved:
        q_rem, wq, wk, wv, wo, low_grad, pack_in, own_part, sib_part, pack, dctx_b, dkt, dvt, dctx = rest
        first, blocks = 0, 2
        for t in range(pairs // 2):
            part = dot_nt(low_grad[...], wo[2 * t * lanes : (2 * t + 2) * lanes, :]).astype(BF16)
            for k in range(2):
                dctx[2 * t + k] = part[: 2 * shard, k * lanes : (k + 1) * lanes]
                dctx_b[2 * t + k] = part[2 * shard :, k * lanes : (k + 1) * lanes]
    else:
        wq, wk, wv, dctx, pack_in, own_part, far_part, sib_part, pack, dkt, dvt = rest
        first, blocks = 1, 1
    low, low_lane, high_lane = halves(lanes)
    low_row = (iota((lanes, 1), 0) < lanes // 2).astype(F32).astype(BF16)
    high_row = 1.0 - low_row
    local = slice(2 * first * shard, 2 * (first + 1) * shard)
    query_grads = [[] for _ in range(blocks)]

    def prepare(p):
        lefts, deltas, turned_q, turned_s = [], [], [], []
        for b in range(blocks):
            span = slice(b * shard, (b + 1) * shard)
            scaled = dctx[p, span, :].astype(F32) * rinv[p, span, :]
            product = scaled * ctx[p, span, :]
            deltas.append(jnp.sum(jnp.where(low, product, 0.0), 1, keepdims=True))
            deltas.append(jnp.sum(jnp.where(low, 0.0, product), 1, keepdims=True))
            scaled = scaled.astype(BF16)
            lefts += [scaled * low_lane, scaled * high_lane]
            q = q_rem[p] if b == 1 else q_loc[p, first * shard : (first + 1) * shard, :]
            q_t, s_t = jnp.transpose(q), jnp.transpose(scaled)
            turned_q += [q_t * low_row, q_t * high_row]
            turned_s += [s_t * low_row, s_t * high_row]
        weights = jnp.concatenate([e[b * pairs + p] for b in range(blocks)], 0)
        values = jnp.concatenate([v_loc[p, local, :], v_rem[p]], 0)
        slopes = dot_nt(jnp.concatenate(lefts, 0), values) - jnp.concatenate(deltas, 0)
        steep = weights * slopes.astype(BF16)
        return jnp.concatenate(turned_q, 1), jnp.concatenate(turned_s, 1), weights, steep

    prepared = [prepare(p) for p in range(pairs)]
    for p, (turned_q, turned_s, weights, steep) in enumerate(prepared):
        keys = jnp.concatenate([k_loc[p, local, :], k_rem[p]], 0)
        grad_q = dot(steep, keys)
        for b in range(blocks):
            one = grad_q[2 * b * shard : (2 * b + 1) * shard]
            two = grad_q[(2 * b + 1) * shard : (2 * b + 2) * shard]
            query_grads[b].append(jnp.where(low, one, two).astype(BF16))
        dkt[p] = dot(turned_q, steep).astype(BF16)
        dvt[p] = dot(turned_s, weights).astype(BF16)
    keys = dkt.shape[2]
    key_t = dkt[...].reshape(width, keys)
    value_t = dvt[...].reshape(width, keys)
    part = jnp.transpose(dot(wk[...], key_t) + dot(wv[...], value_t))
    from_q = dot_nt(jnp.concatenate([jnp.concatenate(g, 1) for g in query_grads], 0), wq[...])
    pieces = [part[k * shard : (k + 1) * shard] for k in range(4)]
    pieces[0] = pieces[0] + from_q[:shard]
    if is_moved:
        pieces[2] = pieces[2] + from_q[shard:]
    gain = jnp.zeros((1, width), F32)
    for piece, x in zip(pieces, (own[first], sib[first], far[0], far_sib[0])):
        x = x[:shard].astype(F32)
        gain = gain + jnp.sum(piece * (x * inverse_rms(x)), 0, keepdims=True)
    pack[...] = pack_in[...]
    pack[0:1, :] = pack_in[0:1, :] + gain
    if is_moved:
        own_part[0] = pieces[0]
        own_part[1] = pieces[2]
    else:
        own_part[0] = pieces[0]
        far_part[0] = pieces[2].astype(BF16)
    sib_part[0, :shard] = pieces[1].astype(BF16)
    sib_part[1, :shard] = pieces[3].astype(BF16)


def pack_small(ranks, grads, mix, side, left, pack):
    mid, width = grads.shape[0] // 2, grads.shape[1]
    inner, outer, square = mid // ranks, width // ranks, ranks * ranks
    line = iota((2 * square, width), 0)
    line = line - ranks * block_of(line, ranks, 2 * ranks)
    own_block = (line == block_of(iota((2 * square, width), 1), outer, ranks)).astype(F32)
    factor = block_of(iota((2 * ranks, 2 * square), 1), ranks, 2 * ranks)
    spread = (factor == iota((2 * ranks, 2 * square), 0)).astype(F32)
    column = iota((outer, width), 1)
    by_b = (column - outer * block_of(column, outer, ranks) == iota((outer, width), 0)).astype(F32)
    group = block_of(iota((2 * ranks, 2 * mid), 1), inner, 2 * ranks)
    by_c = (group == iota((2 * ranks, 2 * mid), 0)).astype(F32)
    column = iota((2 * inner, 2 * mid), 1)
    place = column - inner * block_of(column, inner, 2 * ranks) + inner * (column >= mid).astype(jnp.int32)
    by_j = (place == iota((2 * inner, 2 * mid), 0)).astype(F32)
    column = iota((2 * ranks, square), 1)
    major = block_of(column, ranks, ranks)
    minor = column - ranks * major
    row = iota((2 * ranks, square), 0)
    widen = jnp.where(row < ranks, (row == minor).astype(F32), (row - ranks == major).astype(F32))
    column = iota((2 * square, square), 1)
    major = block_of(column, ranks, ranks)
    minor = column - ranks * major
    row = iota((2 * square, square), 0)
    inside = row - ranks * block_of(row, ranks, 2 * ranks)
    keep = jnp.where(row < square, (inside == major).astype(F32), (inside == minor).astype(F32))
    grads = grads[...]
    product = dot_nt(left[...], grads)
    ends = dot_nt(dot(spread, dot(mix[...] * side[...], grads) * own_block), by_b)
    sides = dot_nt(dot(spread, product * mix[...]), by_j)
    core = dot(spread, dot(dot_nt(product * side[...], by_c), widen) * keep)
    pack[...] = jnp.zeros(pack.shape, F32)
    pack[4:8, 0:outer] = ends[:ranks]
    pack[4:8, 256 : 256 + outer] = ends[ranks:]
    pack[4:8, 512 : 512 + inner] = sides[:ranks, :inner]
    pack[4:8, 640 : 640 + inner] = sides[ranks:, inner:]
    pack[4:8, 704 : 704 + square] = core[:ranks] + core[ranks:]


def norm_back(x, grad, hidden_grad, gain):
    x = x.astype(F32)
    inv = inverse_rms(x)
    hat = x * inv
    c = grad * gain[...][None, :]
    return hidden_grad + inv * (c - hat * jnp.mean(hat * c, -1, keepdims=True))


def return_kernel(far, own_part, from_sib, far_part, from_sib_b, hidden_grad, gain, back):
    shard = back.shape[1]
    back[0] = (far_part[0].astype(F32) + from_sib_b[1, :shard].astype(F32)).astype(BF16)
    grad = own_part[1] + from_sib[1].astype(F32)
    back[1] = norm_back(far[0, :shard], grad, hidden_grad[shard : 2 * shard, :], gain).astype(BF16)


def own_rows_kernel(own, part_a, sib_a, hidden_grad, gain, out, output, grad_input):
    rows, shard, width = out.shape
    row = moved_row(rows)
    output[row] = out[0]
    output[1] = out[2]
    grad = part_a[0] + sib_a[0].astype(F32)
    grad_input[row] = norm_back(own[0, :shard], grad, hidden_grad[0:shard, :], gain).astype(BF16)


def last_kernel(own, part_b, sib_b, hidden_grad, gain, out_far, back, _, __, output, grad_input, grad_b, sems):
    rows, shard, width = output.shape
    other = rows - 1 - moved_row(rows)
    started = start_copies([(out_far.at[0], output.at[other]), (back.at[1], grad_input.at[other])], sems)
    grad = part_b[0] + sib_b[0].astype(F32) + back[0].astype(F32)
    grad_b[...] = norm_back(own[1, :shard], grad, hidden_grad[2 * shard :, :], gain).astype(BF16)
    own_copy = pltpu.make_async_copy(grad_b, grad_input.at[1], sems.at[2])
    own_copy.start()
    for one in (*started, own_copy):
        one.wait()


def unpack_kernel(ranks, mid, near_pack, far_pack, _, g1, g2, shared, dl, dr, ul, ur, bd, bu):
    width = near_pack.shape[1]
    pack = near_pack[...] + far_pack[...]
    inner, outer = mid // ranks, width // ranks
    g1[...] = pack[0]
    g2[...] = pack[1]
    bu[...] = pack[2]
    bd[...] = pack[3, 0:mid]
    dl[...] = pack[4:8, 0:outer]
    ur[...] = pack[4:8, 256 : 256 + outer]
    dr[...] = pack[4:8, 512 : 512 + inner]
    ul[...] = pack[4:8, 640 : 640 + inner]
    for k in range(ranks):
        shared[:, k, :] = pack[4:8, 704 + k * ranks : 704 + (k + 1) * ranks]


def add_kernel(a, b, c):
    c[...] = a[...] + b[...]


def exchange(value, axis, bit):
    count = lax.axis_size(axis)
    return lax.ppermute(value, axis, [(k, k ^ bit) for k in range(count)])


def shards(
    inputs, cotangent, segment_ids, bucket_table, position_bias, query_weight, key_weight, value_weight, out_weight,
    hidden_in, hidden_out, gain_first, gain_second, shared, down_left, down_right, up_left_vectors, up_right,
    bias_down, bias_up,
):
    rows, shard, width = inputs.shape
    heads = position_bias.shape[1]
    hidden = hidden_in.shape[1]
    parts = lax.axis_size("seq")
    ranks, mid = shared.shape[0], bias_down.shape[0]
    pairs, tokens, keys = heads // 2, rows * shard, shard * parts
    lanes = width // pairs
    inner, outer, square = mid // ranks, width // ranks, ranks * ranks
    padded = shard + 8

    own, a_send, b_send, cot_send = call(
        pick_kernel,
        [((2, padded, width), BF16), ((1, padded, width), BF16), ((1, padded, width), BF16), ((1, shard, width), BF16)],
        (Far(inputs), Far(cotangent), Far(segment_ids)),
        8,
        1.0,
        [((rows, shard), jnp.int32)],
        6,
    )
    a_far = exchange(a_send, "seq", 2)
    b_far = exchange(b_send, "seq", 2)
    cot_far = exchange(cot_send, "seq", 2)
    sib = exchange(own, "seq", 1)

    small = (
        bucket_table, jnp.transpose(position_bias), shared, down_left, down_right, up_left_vectors, up_right,
        bias_down, bias_up, gain_first, gain_second,
    )
    large = (query_weight, key_weight, value_weight, out_weight, hidden_out)
    tiles, down_t, up, *expanded = call(
        functools.partial(setup_kernel, shard, parts),
        [((2 * parts - 1, pairs, 2 * shard, shard), F32), ((mid, width), BF16), ((mid, width), BF16)]
        + [((2 * square, 2 * mid), F32)] * 2 + [((2 * square, width), F32)]
        + [(x.shape, x.dtype) for x in small[7:] + large],
        [Far(x) for x in small + large],
        8,
        20.0,
        [((16, 2 * keys), F32), ((square, ranks), F32), ((square, ranks), F32)]
        + [(x.shape, x.dtype) for x in small[:7]],
        len(small) + len(large),
    )
    bd, bu, gain1, gain2, wq, wk, wv, wo, wout = expanded[3:]
    expanded = expanded[:3]
    k_loc, v_loc, q_loc = call(
        local_kernel,
        [((pairs, 4 * shard, lanes), BF16), ((pairs, 4 * shard, lanes), BF16), ((pairs, 2 * shard, lanes), BF16)],
        (own, sib, wq, wk, wv, gain1),
        8,
        20.0,
    )
    a_far, k_loc = lax.optimization_barrier((a_far, k_loc))
    a_far_sib = exchange(a_far, "seq", 1)
    a_far_sib, b_far = lax.optimization_barrier((a_far_sib, b_far))
    b_far_sib = exchange(b_far, "seq", 1)
    proj = ((pairs, 2 * shard, lanes), BF16)
    weights = (wq, wk, wv, wo, gain1)
    ka, va, qa, ea, ctx_a, rinv_a, hid_a, win = call(
        functools.partial(attention_kernel, True),
        [
            proj, proj, ((pairs, shard, lanes), BF16), ((2 * pairs, 2 * shard, keys), BF16),
            ((pairs, 2 * shard, lanes), F32), ((pairs, 2 * shard, lanes), F32), ((2 * shard, width), F32),
            (hidden_in.shape, BF16),
        ],
        (own, sib, a_far, a_far_sib, k_loc, v_loc, q_loc, tiles, *weights, Far(hidden_in)),
        12,
        3.0,
        copies=1,
    )
    kb, vb, eb, ctx_b, rinv_b, hid_b = call(
        functools.partial(attention_kernel, False),
        [
            proj, proj, ((pairs, 2 * shard, keys), BF16),
            ((pairs, shard, lanes), F32), ((pairs, shard, lanes), F32), ((shard, width), F32),
        ],
        (own, sib, b_far, b_far_sib, k_loc, v_loc, q_loc, tiles, *weights),
        12,
        3.0,
    )
    out, out_send, hidden_grad, low_grad, pack_m = call(
        functools.partial(middle_kernel, ranks),
        [
            ((rows, shard, width), BF16), ((1, shard, width), BF16), ((tokens, width), F32), ((tokens, width), BF16),
            ((8, width), F32),
        ],
        (
            hid_a, hid_b, cotangent, cot_far, win, wout, gain2, bd, bu, down_t, up, *expanded,
        ),
        20,
        12.0,
        [((tokens, width), BF16), ((tokens, hidden), BF16), ((tokens, hidden), BF16), ((2 * mid, width), F32)],
    )
    turned = [((pairs, lanes, keys), BF16)] * 2
    part_a, sib_part_a, pack_a, dctx_b = call(
        functools.partial(backward_kernel, True),
        [
            ((2, shard, width), F32), ((2, shard, width), BF16), ((8, width), F32), ((pairs, shard, lanes), BF16),
        ],
        (
            own, sib, a_far, a_far_sib, ctx_a, rinv_a, ea, k_loc, v_loc, q_loc, ka, va, qa,
            wq, wk, wv, wo, low_grad, pack_m,
        ),
        14,
        6.0,
        turned + [((pairs, 2 * shard, lanes), BF16)],
    )
    sib_a = exchange(sib_part_a, "seq", 1)
    part_b, far_part, sib_part_b, pack = call(
        functools.partial(backward_kernel, False),
        [((1, shard, width), F32), ((1, shard, width), BF16), ((2, shard, width), BF16), ((8, width), F32)],
        (
            own, sib, b_far, b_far_sib, ctx_b, rinv_b, eb, k_loc, v_loc, q_loc, kb, vb,
            wq, wk, wv, dctx_b, pack_a,
        ),
        14,
        3.6,
        turned,
    )
    sib_part_b, sib_a = lax.optimization_barrier((sib_part_b, sib_a))
    sib_b = exchange(sib_part_b, "seq", 1)
    (back,) = call(
        return_kernel,
        [((2, shard, width), BF16)],
        (a_far, part_a, sib_a, far_part, sib_b, hidden_grad, gain1),
        16,
        0.5,
    )
    back = exchange(back, "seq", 2)
    out_far = exchange(out_send, "seq", 2)
    (pack,) = call(add_kernel, [((8, width), F32)], (pack, exchange(pack, "seq", 2)), 4, 10.0)
    bit = 1
    while 2 * bit < lax.axis_size("batch"):
        pack = pack + exchange(pack, "batch", bit)
        bit *= 2
    pack = pack + exchange(pack, "seq", 1)
    far_pack = exchange(pack, "batch", bit)
    rowed = ((rows, shard, width), BF16)
    output, grad_input = call(
        own_rows_kernel, [rowed, rowed], (own, part_a, sib_a, hidden_grad, gain1, out), 16, 1.0, last=True
    )
    output, grad_input = call(
        last_kernel,
        [rowed, rowed],
        (own, part_b, sib_b, hidden_grad, gain1, out_far, back, Far(output), Far(grad_input)),
        16,
        1.0,
        [((shard, width), BF16)],
        copies=3,
        last=True,
        aliases={7: 0, 8: 1},
    )
    grads = call(
        functools.partial(unpack_kernel, ranks, mid),
        [
            ((width,), F32), ((width,), F32), ((ranks, ranks, ranks), F32), ((ranks, outer), F32),
            ((ranks, inner), F32), ((ranks, inner), F32), ((ranks, outer), F32), ((mid,), F32), ((width,), F32),
        ],
        (pack, far_pack, Far(grad_input)),
        8,
        0.5,
        last=True,
    )
    return (output, grad_input, *grads)


def solution(mesh):
    rows = P("batch", "seq", None)
    in_specs = (rows, rows, P("batch", "seq")) + (P(),) * 17
    out_specs = (rows, rows) + (P(),) * 9
    return jax.shard_map(shards, mesh=mesh, in_specs=in_specs, out_specs=out_specs, check_vma=False)
```

```python
import functools

import jax
import jax.numpy as jnp
from jax import lax
from jax.experimental import pallas as pl
from jax.experimental.pallas import tpu as pltpu
from jax.sharding import PartitionSpec as P

F32 = jnp.float32
BF16 = jnp.bfloat16
HI = lax.Precision.HIGHEST
epsilon = 1e-06
masked = -1e30
gelu_a = 0.7978845608028654
gelu_b = 0.044715
MIB = 1024 * 1024
VM = pl.BlockSpec(memory_space=pltpu.VMEM)


def dot(a, b, precision=None):
    return lax.dot_general(a, b, (((1,), (0,)), ((), ())), precision=precision, preferred_element_type=F32)


def dot_nt(a, b, precision=None):
    return lax.dot_general(a, b, (((1,), (1,)), ((), ())), precision=precision, preferred_element_type=F32)


def dot_tn(a, b, precision=None):
    return lax.dot_general(a, b, (((0,), (0,)), ((), ())), precision=precision, preferred_element_type=F32)


def iota(shape, axis):
    return lax.broadcasted_iota(jnp.int32, shape, axis)


def block_of(index, size, count):
    total = jnp.zeros_like(index)
    for k in range(1, count):
        total = total + (index >= k * size).astype(jnp.int32)
    return total


def gelu_pair(v):
    square = v * v
    h = 0.5 + 0.5 * jnp.tanh(v * (gelu_a + gelu_a * gelu_b * square))
    g = v * h
    slope = h + (g - g * h) * (2.0 * gelu_a + 6.0 * gelu_a * gelu_b * square)
    return g, slope


def inverse_rms(x):
    return lax.rsqrt(jnp.mean(x * x, -1, keepdims=True) + epsilon)


class Far:
    def __init__(self, value):
        self.value = value


def near(value):
    return pltpu.with_memory_space_constraint(value, pltpu.VMEM)


def call(kernel, outs, args, limit, micros, scratch=(), copies=0, last=False, aliases=()):
    specs = [pl.BlockSpec(memory_space=pl.ANY) if isinstance(a, Far) else VM for a in args]
    args = [pltpu.with_memory_space_constraint(a.value, pltpu.HBM) if isinstance(a, Far) else near(a) for a in args]
    scratch = [pltpu.VMEM(shape, kind) for shape, kind in scratch]
    if copies:
        scratch.append(pltpu.SemaphoreType.DMA((copies,)))
    made = jax.ShapeDtypeStruct if last else pltpu.VMEM
    return pl.pallas_call(
        kernel,
        out_shape=[made(shape, kind) for shape, kind in outs],
        in_specs=specs,
        out_specs=[pl.BlockSpec(memory_space=pl.ANY if aliases else pltpu.VMEM)] * len(outs),
        input_output_aliases=dict(aliases),
        scratch_shapes=scratch,
        compiler_params=pltpu.CompilerParams(vmem_limit_bytes=limit * MIB),
        cost_estimate=pl.CostEstimate(flops=int(micros * 1.1e9), bytes_accessed=0, transcendentals=0),
    )(*args)


def start_copies(pairs, sems):
    started = [pltpu.make_async_copy(source, target, sems.at[k]) for k, (source, target) in enumerate(pairs)]
    for one in started:
        one.start()
    return started


def pick_kernel(inputs, cotangent, segment_ids, own, a_send, b_send, cot_send, ids, sems):
    rows, shard, width = inputs.shape
    extra = own.shape[1] - shard
    row = moved_row(rows)
    other = rows - 1 - row
    body = pl.ds(0, shard)
    started = start_copies(
        [
            (segment_ids, ids),
            (inputs.at[other], a_send.at[0, body]),
            (inputs.at[1], b_send.at[0, body]),
            (inputs.at[row], own.at[0, body]),
            (inputs.at[1], own.at[1, body]),
            (cotangent.at[other], cot_send.at[0]),
        ],
        sems,
    )
    started[0].wait()
    for target, k, source in ((own, 0, row), (own, 1, 1), (a_send, 0, other), (b_send, 0, 1)):
        line = jnp.broadcast_to(ids[pl.ds(source, 1), :].astype(F32).astype(BF16), (extra, shard))
        target[k, shard:, :] = jnp.zeros((extra, width), BF16)
        target[k, shard:, 0:shard] = line
    for one in started[1:]:
        one.wait()


def setup_kernel(
    shard, parts, table_far, position_far, shared_far, dl_far, dr_far, ul_far, ur_far, bd_far, bu_far, g1_far, g2_far,
    wq_far, wk_far, wv_far, wo_far, wout_far,
    tiles, down_t, up, mix, side, left, bd, bu, g1, g2, wq, wk, wv, wo, wout,
    tab, sh16, sh16t, table, position_bias, shared, dl, dr, ul, ur, sems,
):
    started = start_copies(
        [
            (table_far, table), (position_far, position_bias), (shared_far, shared), (dl_far, dl), (dr_far, dr),
            (ul_far, ul), (ur_far, ur), (bd_far, bd), (bu_far, bu), (g1_far, g1), (g2_far, g2),
            (wq_far, wq), (wk_far, wk), (wv_far, wv), (wo_far, wo), (wout_far, wout),
        ],
        sems,
    )
    for one in started[:11]:
        one.wait()
    heads = position_bias.shape[0]
    ranks, (mid, width) = shared.shape[0], down_t.shape
    inner, outer = mid // ranks, width // ranks
    square = ranks * ranks
    hits = (table[...][None, :] == iota((position_bias.shape[1], table.shape[0]), 0)).astype(F32)
    tab[0:heads, 0 : table.shape[0]] = dot(position_bias[...], hits, HI)
    for k in range(2 * parts - 1):
        for h in range(heads):
            line = tab[h : h + 1, k * shard : (k + 2) * shard]
            turned = pltpu.roll(jnp.broadcast_to(line, (shard, 2 * shard)), shard + 1, 1, stride=1, stride_axis=0)
            tiles[k, h // 2, (h % 2) * shard : (h % 2 + 1) * shard, :] = turned[:, :shard]
    eye = (iota((ranks, ranks), 0) == iota((ranks, ranks), 1)).astype(F32)
    for i in range(ranks):
        block = shared[i]
        sh16[i * ranks : (i + 1) * ranks, :] = block
        sh16t[i * ranks : (i + 1) * ranks, :] = dot_tn(block, eye, HI)
    spread, by_c, by_j, by_b, own_block = selectors(ranks, mid, width)
    mix[...] = jnp.zeros(mix.shape, F32)
    side[...] = jnp.zeros(side.shape, F32)
    shx, shtx = dot(sh16[...], by_c, HI), dot(sh16t[...], by_c, HI)
    drx, ulx = dot(dot(spread, dr[...], HI), by_j, HI), dot(dot(spread, ul[...], HI), by_j, HI)
    dlx = dot(dot(spread, dl[...], HI), by_b, HI) * own_block
    urx = dot(dot(spread, ur[...], HI), by_b, HI) * own_block
    mix[:square, :mid] = shx
    mix[square:, mid:] = shtx
    side[:square, :mid] = drx
    side[square:, mid:] = ulx
    left[:square, :] = dlx
    left[square:, :] = urx
    down_t[...] = dot_tn(shx * drx, dlx, HI).astype(BF16)
    up[...] = dot_tn(shtx * ulx, urx, HI).astype(BF16)
    for one in started[11:]:
        one.wait()


def selectors(ranks, mid, width):
    inner, outer, square = mid // ranks, width // ranks, ranks * ranks
    spread = (block_of(iota((square, ranks), 0), ranks, ranks) == iota((square, ranks), 1)).astype(F32)
    by_c = (block_of(iota((ranks, mid), 1), inner, ranks) == iota((ranks, mid), 0)).astype(F32)
    column = iota((inner, mid), 1)
    by_j = (column - inner * block_of(column, inner, ranks) == iota((inner, mid), 0)).astype(F32)
    column = iota((outer, width), 1)
    by_b = (column - outer * block_of(column, outer, ranks) == iota((outer, width), 0)).astype(F32)
    line = iota((square, width), 0)
    own_block = (
        line - ranks * block_of(line, ranks, ranks) == block_of(iota((square, width), 1), outer, ranks)
    ).astype(F32)
    return spread, by_c, by_j, by_b, own_block


def moved_row(rows):
    half = lax.axis_size("seq") // 2
    return jnp.where(lax.axis_index("seq") < half, 0, rows - 1)


def normed(x, gain):
    x = x.astype(F32)
    return (x * inverse_rms(x) * gain[...][None, :]).astype(BF16)


def project(x, weight, target, at):
    pairs, _, lanes = target.shape
    count = x.shape[0]
    for t in range(pairs // 2):
        result = dot(x, weight[:, 2 * t * lanes : (2 * t + 2) * lanes]).astype(BF16)
        target[2 * t, at : at + count, :] = result[:, :lanes]
        target[2 * t + 1, at : at + count, :] = result[:, lanes:]


def local_kernel(own, sib, wq, wk, wv, gain, k_loc, v_loc, q_loc):
    shard = q_loc.shape[1] // 2
    blocks = [normed(x, gain) for x in (own[0, :shard], sib[0, :shard], own[1, :shard], sib[1, :shard])]
    x = jnp.concatenate(blocks, 0)
    project(x, wk, k_loc, 0)
    project(x, wv, v_loc, 0)
    project(jnp.concatenate([blocks[0], blocks[2]], 0), wq, q_loc, 0)


def segment_features(blocks, shard, lanes):
    lane = iota((shard, lanes), 1)
    keys, queries = [], []
    for block in blocks:
        line = block[shard : shard + 1, 0:shard].astype(F32)
        same = lane.astype(F32) == jnp.transpose(jnp.broadcast_to(line, (lanes, shard)))
        keys.append(same.astype(F32).astype(BF16))
        queries.append(jnp.where((lane < 3) & jnp.logical_not(same), masked, 0.0).astype(BF16))
    return jnp.concatenate(keys, 0), queries


def halves(lanes):
    low = iota((1, lanes), 1) < lanes // 2
    low_lane = low.astype(F32).astype(BF16)
    return low, low_lane, 1.0 - low_lane


def attention_kernel(
    is_moved, own, sib, far, far_sib, k_loc, v_loc, q_loc, tiles,
    wq, wk, wv, wo, gain, *rest,
):
    pairs, _, lanes = k_loc.shape
    shard = q_loc.shape[1] // 2
    if is_moved:
        win_far, k_rem, v_rem, q_rem, e, ctx, rinv, hid, win, sems = rest
        fetches = start_copies([(win_far, win)], sems)
        first, queries = 0, [0, 2]
    else:
        k_rem, v_rem, e, ctx, rinv, hid = rest
        fetches = []
        first, queries = 1, [0]
    place = lax.axis_index("seq")
    parts = lax.axis_size("seq")
    far_low = normed(far[0, :shard], gain)
    x = jnp.concatenate([far_low, normed(far_sib[0, :shard], gain)], 0)
    project(x, wk, k_rem, 0)
    project(x, wv, v_rem, 0)
    if is_moved:
        project(far_low, wq, q_rem, 0)
    key_feature, query_feature = segment_features(
        (own.at[first], sib.at[first], far.at[0], far_sib.at[0]), shard, lanes
    )
    local = slice(2 * first * shard, 2 * (first + 1) * shard)
    contexts = [[] for _ in queries]
    low, low_lane, high_lane = halves(lanes)
    for p in range(pairs):
        keys = jnp.concatenate([k_loc[p, local, :], k_rem[p]], 0)
        values = jnp.concatenate([v_loc[p, local, :], v_rem[p]], 0)
        lefts, biases = [], []
        for block in queries:
            q = q_rem[p] if block == 2 else q_loc[p, first * shard : (first + 1) * shard, :]
            feature = query_feature[block]
            lefts.append(jnp.concatenate([q * low_lane, feature], 1))
            lefts.append(jnp.concatenate([q * high_lane, feature], 1))
            at = jnp.bitwise_xor(place, block)
            biases.append(
                jnp.concatenate([tiles[jnp.bitwise_xor(place, k) - at + parts - 1, p] for k in range(parts)], 1)
            )
        scores = dot_nt(jnp.concatenate(lefts, 0), jnp.concatenate([keys, key_feature], 1))
        scores = scores + jnp.concatenate(biases, 0)
        weights = jnp.exp(scores - jnp.max(scores, 1, keepdims=True)).astype(BF16)
        both = dot(weights, jnp.concatenate([values, jnp.ones(values.shape, BF16)], 1))
        scale = 1.0 / both[:, lanes:]
        mixed = both[:, :lanes] * scale
        for b in range(len(queries)):
            one = slice(2 * b * shard, (2 * b + 1) * shard)
            two = slice((2 * b + 1) * shard, (2 * b + 2) * shard)
            span = slice(b * shard, (b + 1) * shard)
            e[b * pairs + p] = weights[2 * b * shard : 2 * (b + 1) * shard]
            kept = jnp.where(low, mixed[one], mixed[two])
            ctx[p, span, :] = kept
            rinv[p, span, :] = jnp.where(low, scale[one], scale[two])
            contexts[b].append(kept.astype(BF16))
    context = jnp.concatenate([jnp.concatenate(c, 1) for c in contexts], 0)
    x = jnp.concatenate([own[first, :shard]] + ([far[0, :shard]] if is_moved else []), 0).astype(F32)
    hid[...] = x + dot(context, wo[...])
    for one in fetches:
        one.wait()


def middle_kernel(
    ranks, hid_a, hid_b, cot, cot_far, win, wout, gain2, bd, bu, down_t, up, mix, side, left,
    out, out_send, hidden_grad, low_grad, pack, low, act, gslope, adapter_grad,
):
    rows, shard, width = cot.shape
    hidden = win.shape[1]
    state = jnp.concatenate([hid_a[...], hid_b[...]], 0)
    inv2 = inverse_rms(state)
    low[...] = (state * inv2 * gain2[...][None, :]).astype(BF16)
    chunk = width // 3
    for j in range(hidden // chunk):
        cols = slice(j * chunk, (j + 1) * chunk)
        g, slope = gelu_pair(dot(low[...], win[:, cols]))
        gslope[:, cols] = slope.astype(BF16)
        act[:, cols] = g.astype(BF16)
    branch = dot(act[...], wout[...])
    row = moved_row(rows)
    branch_low = branch.astype(BF16)
    g, slope = gelu_pair(dot_nt(branch_low, down_t[...]) + bd[...][None, :])
    g_low = g.astype(BF16)
    up_low = jnp.concatenate([cot[row], cot_far[0], cot[1]], 0)
    upstream = up_low.astype(F32)
    gb = dot_nt(up_low, up[...]) * slope
    gb_low = gb.astype(BF16)
    low[...] = (upstream + dot(gb_low, down_t[...])).astype(BF16)
    result = state + branch + dot(g_low, up[...]) + bu[...][None, :]
    for b in range(rows):
        out[b] = result[b * shard : (b + 1) * shard].astype(BF16)
    out_send[0] = result[shard : 2 * shard].astype(BF16)
    mid = g.shape[1]
    adapter_grad[:mid, :] = dot_tn(gb_low, branch_low)
    adapter_grad[mid:, :] = dot_tn(g_low, up_low)
    grad2 = jnp.zeros((rows * shard, width), F32)
    chunk = width
    for j in range(hidden // chunk):
        cols = slice(j * chunk, (j + 1) * chunk)
        pre = (dot_nt(low[...], wout[cols, :]) * gslope[:, cols].astype(F32)).astype(BF16)
        if j == 1:
            pack_small(ranks, adapter_grad, mix, side, left, pack)
        grad2 = grad2 + dot_nt(pre, win[:, cols])
    state = jnp.concatenate([hid_a[...], hid_b[...]], 0)
    inv2 = inverse_rms(state)
    hat2 = state * inv2
    c = grad2 * gain2[...][None, :]
    total = upstream + inv2 * (c - hat2 * jnp.mean(hat2 * c, -1, keepdims=True))
    hidden_grad[...] = total
    low_grad[...] = total.astype(BF16)
    pack[1:2, :] = jnp.sum(grad2 * hat2, 0, keepdims=True)
    pack[2:3, :] = jnp.sum(upstream, 0, keepdims=True)
    pack[3:4, 0:mid] = jnp.sum(gb, 0, keepdims=True)


def backward_kernel(
    is_moved, own, sib, far, far_sib, ctx, rinv, e, k_loc, v_loc, q_loc, k_rem, v_rem, *rest,
):
    pairs, _, lanes = k_loc.shape
    shard, width = q_loc.shape[1] // 2, pairs * lanes
    if is_moved:
        q_rem, wq, wk, wv, wo, low_grad, pack_in, own_part, sib_part, pack, dctx_b, dkt, dvt, dctx = rest
        first, blocks = 0, 2
        for t in range(pairs // 2):
            part = dot_nt(low_grad[...], wo[2 * t * lanes : (2 * t + 2) * lanes, :]).astype(BF16)
            for k in range(2):
                dctx[2 * t + k] = part[: 2 * shard, k * lanes : (k + 1) * lanes]
                dctx_b[2 * t + k] = part[2 * shard :, k * lanes : (k + 1) * lanes]
    else:
        wq, wk, wv, dctx, pack_in, own_part, far_part, sib_part, pack, dkt, dvt = rest
        first, blocks = 1, 1
    low, low_lane, high_lane = halves(lanes)
    low_row = (iota((lanes, 1), 0) < lanes // 2).astype(F32).astype(BF16)
    high_row = 1.0 - low_row
    local = slice(2 * first * shard, 2 * (first + 1) * shard)
    query_grads = [[] for _ in range(blocks)]

    def prepare(p):
        lefts, deltas, turned_q, turned_s = [], [], [], []
        for b in range(blocks):
            span = slice(b * shard, (b + 1) * shard)
            scaled = dctx[p, span, :].astype(F32) * rinv[p, span, :]
            product = scaled * ctx[p, span, :]
            deltas.append(jnp.sum(jnp.where(low, product, 0.0), 1, keepdims=True))
            deltas.append(jnp.sum(jnp.where(low, 0.0, product), 1, keepdims=True))
            scaled = scaled.astype(BF16)
            lefts += [scaled * low_lane, scaled * high_lane]
            q = q_rem[p] if b == 1 else q_loc[p, first * shard : (first + 1) * shard, :]
            q_t, s_t = jnp.transpose(q), jnp.transpose(scaled)
            turned_q += [q_t * low_row, q_t * high_row]
            turned_s += [s_t * low_row, s_t * high_row]
        weights = jnp.concatenate([e[b * pairs + p] for b in range(blocks)], 0)
        values = jnp.concatenate([v_loc[p, local, :], v_rem[p]], 0)
        slopes = dot_nt(jnp.concatenate(lefts, 0), values) - jnp.concatenate(deltas, 0)
        steep = weights * slopes.astype(BF16)
        return jnp.concatenate(turned_q, 1), jnp.concatenate(turned_s, 1), weights, steep

    prepared = [prepare(p) for p in range(pairs)]
    for p, (turned_q, turned_s, weights, steep) in enumerate(prepared):
        keys = jnp.concatenate([k_loc[p, local, :], k_rem[p]], 0)
        grad_q = dot(steep, keys)
        for b in range(blocks):
            one = grad_q[2 * b * shard : (2 * b + 1) * shard]
            two = grad_q[(2 * b + 1) * shard : (2 * b + 2) * shard]
            query_grads[b].append(jnp.where(low, one, two).astype(BF16))
        dkt[p] = dot(turned_q, steep).astype(BF16)
        dvt[p] = dot(turned_s, weights).astype(BF16)
    keys = dkt.shape[2]
    key_t = dkt[...].reshape(width, keys)
    value_t = dvt[...].reshape(width, keys)
    part = jnp.transpose(dot(wk[...], key_t) + dot(wv[...], value_t))
    from_q = dot_nt(jnp.concatenate([jnp.concatenate(g, 1) for g in query_grads], 0), wq[...])
    pieces = [part[k * shard : (k + 1) * shard] for k in range(4)]
    pieces[0] = pieces[0] + from_q[:shard]
    if is_moved:
        pieces[2] = pieces[2] + from_q[shard:]
    gain = jnp.zeros((1, width), F32)
    for piece, x in zip(pieces, (own[first], sib[first], far[0], far_sib[0])):
        x = x[:shard].astype(F32)
        gain = gain + jnp.sum(piece * (x * inverse_rms(x)), 0, keepdims=True)
    pack[...] = pack_in[...]
    pack[0:1, :] = pack_in[0:1, :] + gain
    if is_moved:
        own_part[0] = pieces[0]
        own_part[1] = pieces[2]
    else:
        own_part[0] = pieces[0]
        far_part[0] = pieces[2].astype(BF16)
    sib_part[0, :shard] = pieces[1].astype(BF16)
    sib_part[1, :shard] = pieces[3].astype(BF16)


def pack_small(ranks, grads, mix, side, left, pack):
    mid, width = grads.shape[0] // 2, grads.shape[1]
    inner, outer, square = mid // ranks, width // ranks, ranks * ranks
    line = iota((2 * square, width), 0)
    line = line - ranks * block_of(line, ranks, 2 * ranks)
    own_block = (line == block_of(iota((2 * square, width), 1), outer, ranks)).astype(F32)
    factor = block_of(iota((2 * ranks, 2 * square), 1), ranks, 2 * ranks)
    spread = (factor == iota((2 * ranks, 2 * square), 0)).astype(F32)
    column = iota((outer, width), 1)
    by_b = (column - outer * block_of(column, outer, ranks) == iota((outer, width), 0)).astype(F32)
    group = block_of(iota((2 * ranks, 2 * mid), 1), inner, 2 * ranks)
    by_c = (group == iota((2 * ranks, 2 * mid), 0)).astype(F32)
    column = iota((2 * inner, 2 * mid), 1)
    place = column - inner * block_of(column, inner, 2 * ranks) + inner * (column >= mid).astype(jnp.int32)
    by_j = (place == iota((2 * inner, 2 * mid), 0)).astype(F32)
    column = iota((2 * ranks, square), 1)
    major = block_of(column, ranks, ranks)
    minor = column - ranks * major
    row = iota((2 * ranks, square), 0)
    widen = jnp.where(row < ranks, (row == minor).astype(F32), (row - ranks == major).astype(F32))
    column = iota((2 * square, square), 1)
    major = block_of(column, ranks, ranks)
    minor = column - ranks * major
    row = iota((2 * square, square), 0)
    inside = row - ranks * block_of(row, ranks, 2 * ranks)
    keep = jnp.where(row < square, (inside == major).astype(F32), (inside == minor).astype(F32))
    grads = grads[...]
    product = dot_nt(left[...], grads)
    ends = dot_nt(dot(spread, dot(mix[...] * side[...], grads) * own_block), by_b)
    sides = dot_nt(dot(spread, product * mix[...]), by_j)
    core = dot(spread, dot(dot_nt(product * side[...], by_c), widen) * keep)
    pack[...] = jnp.zeros(pack.shape, F32)
    pack[4:8, 0:outer] = ends[:ranks]
    pack[4:8, 256 : 256 + outer] = ends[ranks:]
    pack[4:8, 512 : 512 + inner] = sides[:ranks, :inner]
    pack[4:8, 640 : 640 + inner] = sides[ranks:, inner:]
    pack[4:8, 704 : 704 + square] = core[:ranks] + core[ranks:]


def norm_back(x, grad, hidden_grad, gain):
    x = x.astype(F32)
    inv = inverse_rms(x)
    hat = x * inv
    c = grad * gain[...][None, :]
    return hidden_grad + inv * (c - hat * jnp.mean(hat * c, -1, keepdims=True))


def return_kernel(far, own_part, from_sib, far_part, from_sib_b, hidden_grad, gain, back):
    shard = back.shape[1]
    back[0] = (far_part[0].astype(F32) + from_sib_b[1, :shard].astype(F32)).astype(BF16)
    grad = own_part[1] + from_sib[1].astype(F32)
    back[1] = norm_back(far[0, :shard], grad, hidden_grad[shard : 2 * shard, :], gain).astype(BF16)


def own_rows_kernel(own, part_a, sib_a, hidden_grad, gain, out, output, grad_input, mark):
    mark[...] = jnp.zeros(mark.shape, F32)
    rows, shard, width = out.shape
    row = moved_row(rows)
    output[row] = out[0]
    output[1] = out[2]
    grad = part_a[0] + sib_a[0].astype(F32)
    grad_input[row] = norm_back(own[0, :shard], grad, hidden_grad[0:shard, :], gain).astype(BF16)


def last_kernel(own, part_b, sib_b, hidden_grad, gain, out_far, back, _, __, output, grad_input, grad_b, sems):
    rows, shard, width = output.shape
    other = rows - 1 - moved_row(rows)
    started = start_copies([(out_far.at[0], output.at[other]), (back.at[1], grad_input.at[other])], sems)
    grad = part_b[0] + sib_b[0].astype(F32) + back[0].astype(F32)
    grad_b[...] = norm_back(own[1, :shard], grad, hidden_grad[2 * shard :, :], gain).astype(BF16)
    own_copy = pltpu.make_async_copy(grad_b, grad_input.at[1], sems.at[2])
    own_copy.start()
    for one in (*started, own_copy):
        one.wait()


def unpack_kernel(ranks, mid, near_pack, far_pack, _, g1, g2, shared, dl, dr, ul, ur, bd, bu):
    width = near_pack.shape[1]
    pack = near_pack[...] + far_pack[...]
    inner, outer = mid // ranks, width // ranks
    g1[...] = pack[0]
    g2[...] = pack[1]
    bu[...] = pack[2]
    bd[...] = pack[3, 0:mid]
    dl[...] = pack[4:8, 0:outer]
    ur[...] = pack[4:8, 256 : 256 + outer]
    dr[...] = pack[4:8, 512 : 512 + inner]
    ul[...] = pack[4:8, 640 : 640 + inner]
    for k in range(ranks):
        shared[:, k, :] = pack[4:8, 704 + k * ranks : 704 + (k + 1) * ranks]


def add_kernel(a, b, c):
    c[...] = a[...] + b[...]


def exchange(value, axis, bit):
    count = lax.axis_size(axis)
    return lax.ppermute(value, axis, [(k, k ^ bit) for k in range(count)])


def shards(
    inputs, cotangent, segment_ids, bucket_table, position_bias, query_weight, key_weight, value_weight, out_weight,
    hidden_in, hidden_out, gain_first, gain_second, shared, down_left, down_right, up_left_vectors, up_right,
    bias_down, bias_up,
):
    rows, shard, width = inputs.shape
    heads = position_bias.shape[1]
    hidden = hidden_in.shape[1]
    parts = lax.axis_size("seq")
    ranks, mid = shared.shape[0], bias_down.shape[0]
    pairs, tokens, keys = heads // 2, rows * shard, shard * parts
    lanes = width // pairs
    inner, outer, square = mid // ranks, width // ranks, ranks * ranks
    padded = shard + 8

    own, a_send, b_send, cot_send = call(
        pick_kernel,
        [((2, padded, width), BF16), ((1, padded, width), BF16), ((1, padded, width), BF16), ((1, shard, width), BF16)],
        (Far(inputs), Far(cotangent), Far(segment_ids)),
        8,
        1.0,
        [((rows, shard), jnp.int32)],
        6,
    )
    a_far = exchange(a_send, "seq", 2)
    b_far = exchange(b_send, "seq", 2)
    cot_far = exchange(cot_send, "seq", 2)
    sib = exchange(own, "seq", 1)

    small = (
        bucket_table, jnp.transpose(position_bias), shared, down_left, down_right, up_left_vectors, up_right,
        bias_down, bias_up, gain_first, gain_second,
    )
    large = (query_weight, key_weight, value_weight, out_weight, hidden_out)
    tiles, down_t, up, *expanded = call(
        functools.partial(setup_kernel, shard, parts),
        [((2 * parts - 1, pairs, 2 * shard, shard), F32), ((mid, width), BF16), ((mid, width), BF16)]
        + [((2 * square, 2 * mid), F32)] * 2 + [((2 * square, width), F32)]
        + [(x.shape, x.dtype) for x in small[7:] + large],
        [Far(x) for x in small + large],
        8,
        20.0,
        [((16, 2 * keys), F32), ((square, ranks), F32), ((square, ranks), F32)]
        + [(x.shape, x.dtype) for x in small[:7]],
        len(small) + len(large),
    )
    bd, bu, gain1, gain2, wq, wk, wv, wo, wout = expanded[3:]
    expanded = expanded[:3]
    k_loc, v_loc, q_loc = call(
        local_kernel,
        [((pairs, 4 * shard, lanes), BF16), ((pairs, 4 * shard, lanes), BF16), ((pairs, 2 * shard, lanes), BF16)],
        (own, sib, wq, wk, wv, gain1),
        8,
        20.0,
    )
    a_far, k_loc = lax.optimization_barrier((a_far, k_loc))
    a_far_sib = exchange(a_far, "seq", 1)
    a_far_sib, b_far = lax.optimization_barrier((a_far_sib, b_far))
    b_far_sib = exchange(b_far, "seq", 1)
    proj = ((pairs, 2 * shard, lanes), BF16)
    weights = (wq, wk, wv, wo, gain1)
    ka, va, qa, ea, ctx_a, rinv_a, hid_a, win = call(
        functools.partial(attention_kernel, True),
        [
            proj, proj, ((pairs, shard, lanes), BF16), ((2 * pairs, 2 * shard, keys), BF16),
            ((pairs, 2 * shard, lanes), F32), ((pairs, 2 * shard, lanes), F32), ((2 * shard, width), F32),
            (hidden_in.shape, BF16),
        ],
        (own, sib, a_far, a_far_sib, k_loc, v_loc, q_loc, tiles, *weights, Far(hidden_in)),
        12,
        3.0,
        copies=1,
    )
    kb, vb, eb, ctx_b, rinv_b, hid_b = call(
        functools.partial(attention_kernel, False),
        [
            proj, proj, ((pairs, 2 * shard, keys), BF16),
            ((pairs, shard, lanes), F32), ((pairs, shard, lanes), F32), ((shard, width), F32),
        ],
        (own, sib, b_far, b_far_sib, k_loc, v_loc, q_loc, tiles, *weights),
        12,
        3.0,
    )
    out, out_send, hidden_grad, low_grad, pack_m = call(
        functools.partial(middle_kernel, ranks),
        [
            ((rows, shard, width), BF16), ((1, shard, width), BF16), ((tokens, width), F32), ((tokens, width), BF16),
            ((8, width), F32),
        ],
        (
            hid_a, hid_b, cotangent, cot_far, win, wout, gain2, bd, bu, down_t, up, *expanded,
        ),
        20,
        12.0,
        [((tokens, width), BF16), ((tokens, hidden), BF16), ((tokens, hidden), BF16), ((2 * mid, width), F32)],
    )
    turned = [((pairs, lanes, keys), BF16)] * 2
    part_a, sib_part_a, pack_a, dctx_b = call(
        functools.partial(backward_kernel, True),
        [
            ((2, shard, width), F32), ((2, shard, width), BF16), ((8, width), F32), ((pairs, shard, lanes), BF16),
        ],
        (
            own, sib, a_far, a_far_sib, ctx_a, rinv_a, ea, k_loc, v_loc, q_loc, ka, va, qa,
            wq, wk, wv, wo, low_grad, pack_m,
        ),
        14,
        6.0,
        turned + [((pairs, 2 * shard, lanes), BF16)],
    )
    sib_a = exchange(sib_part_a, "seq", 1)
    part_b, far_part, sib_part_b, pack = call(
        functools.partial(backward_kernel, False),
        [((1, shard, width), F32), ((1, shard, width), BF16), ((2, shard, width), BF16), ((8, width), F32)],
        (
            own, sib, b_far, b_far_sib, ctx_b, rinv_b, eb, k_loc, v_loc, q_loc, kb, vb,
            wq, wk, wv, dctx_b, pack_a,
        ),
        14,
        3.6,
        turned,
    )
    sib_part_b, sib_a = lax.optimization_barrier((sib_part_b, sib_a))
    sib_b = exchange(sib_part_b, "seq", 1)
    (back,) = call(
        return_kernel,
        [((2, shard, width), BF16)],
        (a_far, part_a, sib_a, far_part, sib_b, hidden_grad, gain1),
        16,
        0.5,
    )
    back = exchange(back, "seq", 2)
    out_far = exchange(out_send, "seq", 2)
    (pack,) = call(add_kernel, [((8, width), F32)], (pack, exchange(pack, "seq", 2)), 4, 10.0)
    first, second, third = (exchange(pack, "batch", k) for k in (1, 2, 3))
    pack = (pack + first) + (second + third)
    bit = 4
    while 2 * bit < lax.axis_size("batch"):
        pack = pack + exchange(pack, "batch", bit)
        bit *= 2
    pack = pack + exchange(pack, "seq", 1)
    far_pack = exchange(pack, "batch", bit)
    rowed = ((rows, shard, width), BF16)
    output, grad_input, mark = call(
        own_rows_kernel, [rowed, rowed, ((8, 128), F32)], (own, part_a, sib_a, hidden_grad, gain1, out), 16, 0.0, last=True
    )
    output, grad_input = call(
        last_kernel,
        [rowed, rowed],
        (own, part_b, sib_b, hidden_grad, gain1, out_far, back, Far(output), Far(grad_input)),
        16,
        1.0,
        [((shard, width), BF16)],
        copies=3,
        last=True,
        aliases={7: 0, 8: 1},
    )
    grads = call(
        functools.partial(unpack_kernel, ranks, mid),
        [
            ((width,), F32), ((width,), F32), ((ranks, ranks, ranks), F32), ((ranks, outer), F32),
            ((ranks, inner), F32), ((ranks, inner), F32), ((ranks, outer), F32), ((mid,), F32), ((width,), F32),
        ],
        (pack, far_pack, Far(mark)),
        8,
        0.5,
        last=True,
    )
    return (output, grad_input, *grads)


def solution(mesh):
    rows = P("batch", "seq", None)
    in_specs = (rows, rows, P("batch", "seq")) + (P(),) * 17
    out_specs = (rows, rows) + (P(),) * 9
    return jax.shard_map(shards, mesh=mesh, in_specs=in_specs, out_specs=out_specs, check_vma=False)
```

```python
import functools

import jax
import jax.numpy as jnp
from jax import lax
from jax.experimental import pallas as pl
from jax.experimental.pallas import tpu as pltpu
from jax.sharding import PartitionSpec as P

F32 = jnp.float32
BF16 = jnp.bfloat16
HI = lax.Precision.HIGHEST
epsilon = 1e-06
masked = -1e30
gelu_a = 0.7978845608028654
gelu_b = 0.044715
MIB = 1024 * 1024
VM = pl.BlockSpec(memory_space=pltpu.VMEM)


def dot(a, b, precision=None):
    return lax.dot_general(a, b, (((1,), (0,)), ((), ())), precision=precision, preferred_element_type=F32)


def dot_nt(a, b, precision=None):
    return lax.dot_general(a, b, (((1,), (1,)), ((), ())), precision=precision, preferred_element_type=F32)


def dot_tn(a, b, precision=None):
    return lax.dot_general(a, b, (((0,), (0,)), ((), ())), precision=precision, preferred_element_type=F32)


def iota(shape, axis):
    return lax.broadcasted_iota(jnp.int32, shape, axis)


def block_of(index, size, count):
    total = jnp.zeros_like(index)
    for k in range(1, count):
        total = total + (index >= k * size).astype(jnp.int32)
    return total


def gelu_pair(v):
    square = v * v
    h = 0.5 + 0.5 * jnp.tanh(v * (gelu_a + gelu_a * gelu_b * square))
    g = v * h
    slope = h + (g - g * h) * (2.0 * gelu_a + 6.0 * gelu_a * gelu_b * square)
    return g, slope


def inverse_rms(x):
    return lax.rsqrt(jnp.mean(x * x, -1, keepdims=True) + epsilon)


class Far:
    def __init__(self, value):
        self.value = value


def near(value):
    return pltpu.with_memory_space_constraint(value, pltpu.VMEM)


def call(kernel, outs, args, limit, micros, scratch=(), copies=0, last=False, aliases=()):
    specs = [pl.BlockSpec(memory_space=pl.ANY) if isinstance(a, Far) else VM for a in args]
    args = [pltpu.with_memory_space_constraint(a.value, pltpu.HBM) if isinstance(a, Far) else near(a) for a in args]
    scratch = [pltpu.VMEM(shape, kind) for shape, kind in scratch]
    if copies:
        scratch.append(pltpu.SemaphoreType.DMA((copies,)))
    made = jax.ShapeDtypeStruct if last else pltpu.VMEM
    return pl.pallas_call(
        kernel,
        out_shape=[made(shape, kind) for shape, kind in outs],
        in_specs=specs,
        out_specs=[pl.BlockSpec(memory_space=pl.ANY if aliases else pltpu.VMEM)] * len(outs),
        input_output_aliases=dict(aliases),
        scratch_shapes=scratch,
        compiler_params=pltpu.CompilerParams(vmem_limit_bytes=limit * MIB),
        cost_estimate=pl.CostEstimate(flops=int(micros * 1.1e9), bytes_accessed=0, transcendentals=0),
    )(*args)


def start_copies(pairs, sems):
    started = [pltpu.make_async_copy(source, target, sems.at[k]) for k, (source, target) in enumerate(pairs)]
    for one in started:
        one.start()
    return started


def pick_kernel(inputs, cotangent, segment_ids, own, a_send, b_send, cot_send, ids, sems):
    rows, shard, width = inputs.shape
    extra = own.shape[1] - shard
    row = moved_row(rows)
    other = rows - 1 - row
    body = pl.ds(0, shard)
    started = start_copies(
        [
            (segment_ids, ids),
            (inputs.at[other], a_send.at[0, body]),
            (inputs.at[1], b_send.at[0, body]),
            (inputs.at[row], own.at[0, body]),
            (inputs.at[1], own.at[1, body]),
            (cotangent.at[other], cot_send.at[0]),
        ],
        sems,
    )
    started[0].wait()
    for target, k, source in ((own, 0, row), (own, 1, 1), (a_send, 0, other), (b_send, 0, 1)):
        line = jnp.broadcast_to(ids[pl.ds(source, 1), :].astype(F32).astype(BF16), (extra, shard))
        target[k, shard:, :] = jnp.zeros((extra, width), BF16)
        target[k, shard:, 0:shard] = line
    for one in started[1:]:
        one.wait()


def setup_kernel(
    shard, parts, table_far, position_far, shared_far, dl_far, dr_far, ul_far, ur_far, bd_far, bu_far, g1_far, g2_far,
    wq_far, wk_far, wv_far, wo_far, wout_far,
    tiles, down_t, up, mix, side, left, bd, bu, g1, g2, wq, wk, wv, wo, wout,
    tab, sh16, sh16t, table, position_bias, shared, dl, dr, ul, ur, sems,
):
    started = start_copies(
        [
            (table_far, table), (position_far, position_bias), (shared_far, shared), (dl_far, dl), (dr_far, dr),
            (ul_far, ul), (ur_far, ur), (bd_far, bd), (bu_far, bu), (g1_far, g1), (g2_far, g2),
            (wq_far, wq), (wk_far, wk), (wv_far, wv), (wo_far, wo), (wout_far, wout),
        ],
        sems,
    )
    for one in started[:11]:
        one.wait()
    heads = position_bias.shape[0]
    ranks, (mid, width) = shared.shape[0], down_t.shape
    inner, outer = mid // ranks, width // ranks
    square = ranks * ranks
    hits = (table[...][None, :] == iota((position_bias.shape[1], table.shape[0]), 0)).astype(F32)
    tab[0:heads, 0 : table.shape[0]] = dot(position_bias[...], hits, HI)
    for k in range(2 * parts - 1):
        for h in range(heads):
            line = tab[h : h + 1, k * shard : (k + 2) * shard]
            turned = pltpu.roll(jnp.broadcast_to(line, (shard, 2 * shard)), shard + 1, 1, stride=1, stride_axis=0)
            tiles[k, h // 2, (h % 2) * shard : (h % 2 + 1) * shard, :] = turned[:, :shard]
    eye = (iota((ranks, ranks), 0) == iota((ranks, ranks), 1)).astype(F32)
    for i in range(ranks):
        block = shared[i]
        sh16[i * ranks : (i + 1) * ranks, :] = block
        sh16t[i * ranks : (i + 1) * ranks, :] = dot_tn(block, eye, HI)
    spread, by_c, by_j, by_b, own_block = selectors(ranks, mid, width)
    mix[...] = jnp.zeros(mix.shape, F32)
    side[...] = jnp.zeros(side.shape, F32)
    shx, shtx = dot(sh16[...], by_c, HI), dot(sh16t[...], by_c, HI)
    drx, ulx = dot(dot(spread, dr[...], HI), by_j, HI), dot(dot(spread, ul[...], HI), by_j, HI)
    dlx = dot(dot(spread, dl[...], HI), by_b, HI) * own_block
    urx = dot(dot(spread, ur[...], HI), by_b, HI) * own_block
    mix[:square, :mid] = shx
    mix[square:, mid:] = shtx
    side[:square, :mid] = drx
    side[square:, mid:] = ulx
    left[:square, :] = dlx
    left[square:, :] = urx
    down_t[...] = dot_tn(shx * drx, dlx, HI).astype(BF16)
    up[...] = dot_tn(shtx * ulx, urx, HI).astype(BF16)
    for one in started[11:]:
        one.wait()


def selectors(ranks, mid, width):
    inner, outer, square = mid // ranks, width // ranks, ranks * ranks
    spread = (block_of(iota((square, ranks), 0), ranks, ranks) == iota((square, ranks), 1)).astype(F32)
    by_c = (block_of(iota((ranks, mid), 1), inner, ranks) == iota((ranks, mid), 0)).astype(F32)
    column = iota((inner, mid), 1)
    by_j = (column - inner * block_of(column, inner, ranks) == iota((inner, mid), 0)).astype(F32)
    column = iota((outer, width), 1)
    by_b = (column - outer * block_of(column, outer, ranks) == iota((outer, width), 0)).astype(F32)
    line = iota((square, width), 0)
    own_block = (
        line - ranks * block_of(line, ranks, ranks) == block_of(iota((square, width), 1), outer, ranks)
    ).astype(F32)
    return spread, by_c, by_j, by_b, own_block


def moved_row(rows):
    half = lax.axis_size("seq") // 2
    return jnp.where(lax.axis_index("seq") < half, 0, rows - 1)


def normed(x, gain):
    x = x.astype(F32)
    return (x * inverse_rms(x) * gain[...][None, :]).astype(BF16)


def project(x, weight, target, at):
    pairs, _, lanes = target.shape
    count = x.shape[0]
    for t in range(pairs // 2):
        result = dot(x, weight[:, 2 * t * lanes : (2 * t + 2) * lanes]).astype(BF16)
        target[2 * t, at : at + count, :] = result[:, :lanes]
        target[2 * t + 1, at : at + count, :] = result[:, lanes:]


def local_kernel(own, sib, wq, wk, wv, gain, k_loc, v_loc, q_loc):
    shard = q_loc.shape[1] // 2
    blocks = [normed(x, gain) for x in (own[0, :shard], sib[0, :shard], own[1, :shard], sib[1, :shard])]
    x = jnp.concatenate(blocks, 0)
    project(x, wk, k_loc, 0)
    project(x, wv, v_loc, 0)
    project(jnp.concatenate([blocks[0], blocks[2]], 0), wq, q_loc, 0)


def segment_features(blocks, shard, lanes):
    lane = iota((shard, lanes), 1)
    keys, queries = [], []
    for block in blocks:
        line = block[shard : shard + 1, 0:shard].astype(F32)
        same = lane.astype(F32) == jnp.transpose(jnp.broadcast_to(line, (lanes, shard)))
        keys.append(same.astype(F32).astype(BF16))
        queries.append(jnp.where((lane < 3) & jnp.logical_not(same), masked, 0.0).astype(BF16))
    return jnp.concatenate(keys, 0), queries


def halves(lanes):
    low = iota((1, lanes), 1) < lanes // 2
    low_lane = low.astype(F32).astype(BF16)
    return low, low_lane, 1.0 - low_lane


def attention_kernel(
    is_moved, own, sib, far, far_sib, k_loc, v_loc, q_loc, tiles,
    wq, wk, wv, wo, gain, *rest,
):
    pairs, _, lanes = k_loc.shape
    shard = q_loc.shape[1] // 2
    if is_moved:
        win_far, k_rem, v_rem, q_rem, e, ctx, rinv, hid, win, sems = rest
        fetches = start_copies([(win_far, win)], sems)
        first, queries = 0, [0, 2]
    else:
        k_rem, v_rem, e, ctx, rinv, hid = rest
        fetches = []
        first, queries = 1, [0]
    place = lax.axis_index("seq")
    parts = lax.axis_size("seq")
    far_low = normed(far[0, :shard], gain)
    x = jnp.concatenate([far_low, normed(far_sib[0, :shard], gain)], 0)
    project(x, wk, k_rem, 0)
    project(x, wv, v_rem, 0)
    if is_moved:
        project(far_low, wq, q_rem, 0)
    key_feature, query_feature = segment_features(
        (own.at[first], sib.at[first], far.at[0], far_sib.at[0]), shard, lanes
    )
    local = slice(2 * first * shard, 2 * (first + 1) * shard)
    contexts = [[] for _ in queries]
    low, low_lane, high_lane = halves(lanes)
    for p in range(pairs):
        keys = jnp.concatenate([k_loc[p, local, :], k_rem[p]], 0)
        values = jnp.concatenate([v_loc[p, local, :], v_rem[p]], 0)
        lefts, biases = [], []
        for block in queries:
            q = q_rem[p] if block == 2 else q_loc[p, first * shard : (first + 1) * shard, :]
            feature = query_feature[block]
            lefts.append(jnp.concatenate([q * low_lane, feature], 1))
            lefts.append(jnp.concatenate([q * high_lane, feature], 1))
            at = jnp.bitwise_xor(place, block)
            biases.append(
                jnp.concatenate([tiles[jnp.bitwise_xor(place, k) - at + parts - 1, p] for k in range(parts)], 1)
            )
        scores = dot_nt(jnp.concatenate(lefts, 0), jnp.concatenate([keys, key_feature], 1))
        scores = scores + jnp.concatenate(biases, 0)
        weights = jnp.exp(scores - jnp.max(scores, 1, keepdims=True)).astype(BF16)
        both = dot(weights, jnp.concatenate([values, jnp.ones(values.shape, BF16)], 1))
        scale = 1.0 / both[:, lanes:]
        mixed = both[:, :lanes] * scale
        for b in range(len(queries)):
            one = slice(2 * b * shard, (2 * b + 1) * shard)
            two = slice((2 * b + 1) * shard, (2 * b + 2) * shard)
            span = slice(b * shard, (b + 1) * shard)
            e[b * pairs + p] = weights[2 * b * shard : 2 * (b + 1) * shard]
            kept = jnp.where(low, mixed[one], mixed[two])
            ctx[p, span, :] = kept
            rinv[p, span, :] = jnp.where(low, scale[one], scale[two])
            contexts[b].append(kept.astype(BF16))
    context = jnp.concatenate([jnp.concatenate(c, 1) for c in contexts], 0)
    x = jnp.concatenate([own[first, :shard]] + ([far[0, :shard]] if is_moved else []), 0).astype(F32)
    hid[...] = x + dot(context, wo[...])
    for one in fetches:
        one.wait()


def middle_kernel(
    ranks, hid_a, hid_b, cot, cot_far, win, wout, gain2, bd, bu, down_t, up, mix, side, left,
    out, out_send, hidden_grad, low_grad, pack, low, act, gslope, adapter_grad,
):
    rows, shard, width = cot.shape
    hidden = win.shape[1]
    state = jnp.concatenate([hid_a[...], hid_b[...]], 0)
    inv2 = inverse_rms(state)
    low[...] = (state * inv2 * gain2[...][None, :]).astype(BF16)
    chunk = width // 3
    for j in range(hidden // chunk):
        cols = slice(j * chunk, (j + 1) * chunk)
        g, slope = gelu_pair(dot(low[...], win[:, cols]))
        gslope[:, cols] = slope.astype(BF16)
        act[:, cols] = g.astype(BF16)
    branch = dot(act[...], wout[...])
    row = moved_row(rows)
    branch_low = branch.astype(BF16)
    g, slope = gelu_pair(dot_nt(branch_low, down_t[...]) + bd[...][None, :])
    g_low = g.astype(BF16)
    up_low = jnp.concatenate([cot[row], cot_far[0], cot[1]], 0)
    upstream = up_low.astype(F32)
    gb = dot_nt(up_low, up[...]) * slope
    gb_low = gb.astype(BF16)
    low[...] = (upstream + dot(gb_low, down_t[...])).astype(BF16)
    result = state + branch + dot(g_low, up[...]) + bu[...][None, :]
    for b in range(rows):
        out[b] = result[b * shard : (b + 1) * shard].astype(BF16)
    out_send[0] = result[shard : 2 * shard].astype(BF16)
    mid = g.shape[1]
    adapter_grad[:mid, :] = dot_tn(gb_low, branch_low)
    adapter_grad[mid:, :] = dot_tn(g_low, up_low)
    grad2 = jnp.zeros((rows * shard, width), F32)
    chunk = width
    for j in range(hidden // chunk):
        cols = slice(j * chunk, (j + 1) * chunk)
        pre = (dot_nt(low[...], wout[cols, :]) * gslope[:, cols].astype(F32)).astype(BF16)
        if j == 1:
            pack_small(ranks, adapter_grad, mix, side, left, pack)
        grad2 = grad2 + dot_nt(pre, win[:, cols])
    state = jnp.concatenate([hid_a[...], hid_b[...]], 0)
    inv2 = inverse_rms(state)
    hat2 = state * inv2
    c = grad2 * gain2[...][None, :]
    total = upstream + inv2 * (c - hat2 * jnp.mean(hat2 * c, -1, keepdims=True))
    hidden_grad[...] = total
    low_grad[...] = total.astype(BF16)
    pack[1:2, :] = jnp.sum(grad2 * hat2, 0, keepdims=True)
    pack[2:3, :] = jnp.sum(upstream, 0, keepdims=True)
    pack[3:4, 0:mid] = jnp.sum(gb, 0, keepdims=True)


def backward_kernel(
    is_moved, own, sib, far, far_sib, ctx, rinv, e, k_loc, v_loc, q_loc, k_rem, v_rem, *rest,
):
    pairs, _, lanes = k_loc.shape
    shard, width = q_loc.shape[1] // 2, pairs * lanes
    if is_moved:
        q_rem, wq, wk, wv, wo, low_grad, pack_in, own_part, sib_part, pack, dctx_b, dkt, dvt, dctx = rest
        first, blocks = 0, 2
        for t in range(pairs // 2):
            part = dot_nt(low_grad[...], wo[2 * t * lanes : (2 * t + 2) * lanes, :]).astype(BF16)
            for k in range(2):
                dctx[2 * t + k] = part[: 2 * shard, k * lanes : (k + 1) * lanes]
                dctx_b[2 * t + k] = part[2 * shard :, k * lanes : (k + 1) * lanes]
    else:
        wq, wk, wv, dctx, pack_in, own_part, far_part, sib_part, pack, dkt, dvt = rest
        first, blocks = 1, 1
    low, low_lane, high_lane = halves(lanes)
    low_row = (iota((lanes, 1), 0) < lanes // 2).astype(F32).astype(BF16)
    high_row = 1.0 - low_row
    local = slice(2 * first * shard, 2 * (first + 1) * shard)
    query_grads = [[] for _ in range(blocks)]

    def prepare(p):
        lefts, deltas, turned_q, turned_s = [], [], [], []
        for b in range(blocks):
            span = slice(b * shard, (b + 1) * shard)
            scaled = dctx[p, span, :].astype(F32) * rinv[p, span, :]
            product = scaled * ctx[p, span, :]
            deltas.append(jnp.sum(jnp.where(low, product, 0.0), 1, keepdims=True))
            deltas.append(jnp.sum(jnp.where(low, 0.0, product), 1, keepdims=True))
            scaled = scaled.astype(BF16)
            lefts += [scaled * low_lane, scaled * high_lane]
            q = q_rem[p] if b == 1 else q_loc[p, first * shard : (first + 1) * shard, :]
            q_t, s_t = jnp.transpose(q), jnp.transpose(scaled)
            turned_q += [q_t * low_row, q_t * high_row]
            turned_s += [s_t * low_row, s_t * high_row]
        weights = jnp.concatenate([e[b * pairs + p] for b in range(blocks)], 0)
        values = jnp.concatenate([v_loc[p, local, :], v_rem[p]], 0)
        slopes = dot_nt(jnp.concatenate(lefts, 0), values) - jnp.concatenate(deltas, 0)
        steep = weights * slopes.astype(BF16)
        return jnp.concatenate(turned_q, 1), jnp.concatenate(turned_s, 1), weights, steep

    prepared = [prepare(p) for p in range(pairs)]
    for p, (turned_q, turned_s, weights, steep) in enumerate(prepared):
        keys = jnp.concatenate([k_loc[p, local, :], k_rem[p]], 0)
        grad_q = dot(steep, keys)
        for b in range(blocks):
            one = grad_q[2 * b * shard : (2 * b + 1) * shard]
            two = grad_q[(2 * b + 1) * shard : (2 * b + 2) * shard]
            query_grads[b].append(jnp.where(low, one, two).astype(BF16))
        dkt[p] = dot(turned_q, steep).astype(BF16)
        dvt[p] = dot(turned_s, weights).astype(BF16)
    keys = dkt.shape[2]
    key_t = dkt[...].reshape(width, keys)
    value_t = dvt[...].reshape(width, keys)
    part = jnp.transpose(dot(wk[...], key_t) + dot(wv[...], value_t))
    from_q = dot_nt(jnp.concatenate([jnp.concatenate(g, 1) for g in query_grads], 0), wq[...])
    pieces = [part[k * shard : (k + 1) * shard] for k in range(4)]
    pieces[0] = pieces[0] + from_q[:shard]
    if is_moved:
        pieces[2] = pieces[2] + from_q[shard:]
    gain = jnp.zeros((1, width), F32)
    for piece, x in zip(pieces, (own[first], sib[first], far[0], far_sib[0])):
        x = x[:shard].astype(F32)
        gain = gain + jnp.sum(piece * (x * inverse_rms(x)), 0, keepdims=True)
    pack[...] = pack_in[...]
    pack[0:1, :] = pack_in[0:1, :] + gain
    if is_moved:
        own_part[0] = pieces[0]
        own_part[1] = pieces[2]
    else:
        own_part[0] = pieces[0]
        far_part[0] = pieces[2].astype(BF16)
    sib_part[0, :shard] = pieces[1].astype(BF16)
    sib_part[1, :shard] = pieces[3].astype(BF16)


def pack_small(ranks, grads, mix, side, left, pack):
    mid, width = grads.shape[0] // 2, grads.shape[1]
    inner, outer, square = mid // ranks, width // ranks, ranks * ranks
    line = iota((2 * square, width), 0)
    line = line - ranks * block_of(line, ranks, 2 * ranks)
    own_block = (line == block_of(iota((2 * square, width), 1), outer, ranks)).astype(F32)
    factor = block_of(iota((2 * ranks, 2 * square), 1), ranks, 2 * ranks)
    spread = (factor == iota((2 * ranks, 2 * square), 0)).astype(F32)
    column = iota((outer, width), 1)
    by_b = (column - outer * block_of(column, outer, ranks) == iota((outer, width), 0)).astype(F32)
    group = block_of(iota((2 * ranks, 2 * mid), 1), inner, 2 * ranks)
    by_c = (group == iota((2 * ranks, 2 * mid), 0)).astype(F32)
    column = iota((2 * inner, 2 * mid), 1)
    place = column - inner * block_of(column, inner, 2 * ranks) + inner * (column >= mid).astype(jnp.int32)
    by_j = (place == iota((2 * inner, 2 * mid), 0)).astype(F32)
    column = iota((2 * ranks, square), 1)
    major = block_of(column, ranks, ranks)
    minor = column - ranks * major
    row = iota((2 * ranks, square), 0)
    widen = jnp.where(row < ranks, (row == minor).astype(F32), (row - ranks == major).astype(F32))
    column = iota((2 * square, square), 1)
    major = block_of(column, ranks, ranks)
    minor = column - ranks * major
    row = iota((2 * square, square), 0)
    inside = row - ranks * block_of(row, ranks, 2 * ranks)
    keep = jnp.where(row < square, (inside == major).astype(F32), (inside == minor).astype(F32))
    grads = grads[...]
    product = dot_nt(left[...], grads)
    ends = dot_nt(dot(spread, dot(mix[...] * side[...], grads) * own_block), by_b)
    sides = dot_nt(dot(spread, product * mix[...]), by_j)
    core = dot(spread, dot(dot_nt(product * side[...], by_c), widen) * keep)
    pack[...] = jnp.zeros(pack.shape, F32)
    pack[4:8, 0:outer] = ends[:ranks]
    pack[4:8, 256 : 256 + outer] = ends[ranks:]
    pack[4:8, 512 : 512 + inner] = sides[:ranks, :inner]
    pack[4:8, 640 : 640 + inner] = sides[ranks:, inner:]
    pack[4:8, 704 : 704 + square] = core[:ranks] + core[ranks:]


def norm_back(x, grad, hidden_grad, gain):
    x = x.astype(F32)
    inv = inverse_rms(x)
    hat = x * inv
    c = grad * gain[...][None, :]
    return hidden_grad + inv * (c - hat * jnp.mean(hat * c, -1, keepdims=True))


def return_kernel(far, own_part, from_sib, out, hidden_grad, gain, back):
    shard = back.shape[1]
    back[0] = out[0]
    grad = own_part[1] + from_sib[1].astype(F32)
    back[1] = norm_back(far[0, :shard], grad, hidden_grad[shard : 2 * shard, :], gain).astype(BF16)


def far_sum_kernel(far_part, from_sib, total):
    total[0] = (far_part[0].astype(F32) + from_sib[1].astype(F32)).astype(BF16)


def own_rows_kernel(own, part_a, sib_a, hidden_grad, gain, out, back, output, grad_input, mark):
    mark[...] = jnp.zeros(mark.shape, F32)
    rows, shard, width = out.shape
    row = moved_row(rows)
    other = rows - 1 - row
    output[row] = out[0]
    output[1] = out[2]
    output[other] = back[0]
    grad_input[other] = back[1]
    grad = part_a[0] + sib_a[0].astype(F32)
    grad_input[row] = norm_back(own[0, :shard], grad, hidden_grad[0:shard, :], gain).astype(BF16)


def last_kernel(own, part_b, sib_b, hidden_grad, gain, far_sum, _, grad_input, grad_b, sems):
    shard = grad_input.shape[1]
    grad = part_b[0] + sib_b[0].astype(F32) + far_sum[0].astype(F32)
    grad_b[...] = norm_back(own[1, :shard], grad, hidden_grad[2 * shard :, :], gain).astype(BF16)
    (copy,) = start_copies([(grad_b, grad_input.at[1])], sems)
    copy.wait()


def unpack_kernel(ranks, mid, near_pack, far_pack, _, g1, g2, shared, dl, dr, ul, ur, bd, bu):
    width = near_pack.shape[1]
    pack = near_pack[...] + far_pack[...]
    inner, outer = mid // ranks, width // ranks
    g1[...] = pack[0]
    g2[...] = pack[1]
    bu[...] = pack[2]
    bd[...] = pack[3, 0:mid]
    dl[...] = pack[4:8, 0:outer]
    ur[...] = pack[4:8, 256 : 256 + outer]
    dr[...] = pack[4:8, 512 : 512 + inner]
    ul[...] = pack[4:8, 640 : 640 + inner]
    for k in range(ranks):
        shared[:, k, :] = pack[4:8, 704 + k * ranks : 704 + (k + 1) * ranks]


def add_kernel(a, b, c):
    c[...] = a[...] + b[...]


def exchange(value, axis, bit):
    count = lax.axis_size(axis)
    return lax.ppermute(value, axis, [(k, k ^ bit) for k in range(count)])


def shards(
    inputs, cotangent, segment_ids, bucket_table, position_bias, query_weight, key_weight, value_weight, out_weight,
    hidden_in, hidden_out, gain_first, gain_second, shared, down_left, down_right, up_left_vectors, up_right,
    bias_down, bias_up,
):
    rows, shard, width = inputs.shape
    heads = position_bias.shape[1]
    hidden = hidden_in.shape[1]
    parts = lax.axis_size("seq")
    ranks, mid = shared.shape[0], bias_down.shape[0]
    pairs, tokens, keys = heads // 2, rows * shard, shard * parts
    lanes = width // pairs
    inner, outer, square = mid // ranks, width // ranks, ranks * ranks
    padded = shard + 8

    own, a_send, b_send, cot_send = call(
        pick_kernel,
        [((2, padded, width), BF16), ((1, padded, width), BF16), ((1, padded, width), BF16), ((1, shard, width), BF16)],
        (Far(inputs), Far(cotangent), Far(segment_ids)),
        8,
        1.0,
        [((rows, shard), jnp.int32)],
        6,
    )
    a_far = exchange(a_send, "seq", 2)
    b_far = exchange(b_send, "seq", 2)
    cot_far = exchange(cot_send, "seq", 2)
    sib = exchange(own, "seq", 1)

    small = (
        bucket_table, jnp.transpose(position_bias), shared, down_left, down_right, up_left_vectors, up_right,
        bias_down, bias_up, gain_first, gain_second,
    )
    large = (query_weight, key_weight, value_weight, out_weight, hidden_out)
    tiles, down_t, up, *expanded = call(
        functools.partial(setup_kernel, shard, parts),
        [((2 * parts - 1, pairs, 2 * shard, shard), F32), ((mid, width), BF16), ((mid, width), BF16)]
        + [((2 * square, 2 * mid), F32)] * 2 + [((2 * square, width), F32)]
        + [(x.shape, x.dtype) for x in small[7:] + large],
        [Far(x) for x in small + large],
        8,
        20.0,
        [((16, 2 * keys), F32), ((square, ranks), F32), ((square, ranks), F32)]
        + [(x.shape, x.dtype) for x in small[:7]],
        len(small) + len(large),
    )
    bd, bu, gain1, gain2, wq, wk, wv, wo, wout = expanded[3:]
    expanded = expanded[:3]
    k_loc, v_loc, q_loc = call(
        local_kernel,
        [((pairs, 4 * shard, lanes), BF16), ((pairs, 4 * shard, lanes), BF16), ((pairs, 2 * shard, lanes), BF16)],
        (own, sib, wq, wk, wv, gain1),
        8,
        20.0,
    )
    a_far, k_loc = lax.optimization_barrier((a_far, k_loc))
    a_far_sib = exchange(a_far, "seq", 1)
    a_far_sib, b_far = lax.optimization_barrier((a_far_sib, b_far))
    b_far_sib = exchange(b_far, "seq", 1)
    proj = ((pairs, 2 * shard, lanes), BF16)
    weights = (wq, wk, wv, wo, gain1)
    ka, va, qa, ea, ctx_a, rinv_a, hid_a, win = call(
        functools.partial(attention_kernel, True),
        [
            proj, proj, ((pairs, shard, lanes), BF16), ((2 * pairs, 2 * shard, keys), BF16),
            ((pairs, 2 * shard, lanes), F32), ((pairs, 2 * shard, lanes), F32), ((2 * shard, width), F32),
            (hidden_in.shape, BF16),
        ],
        (own, sib, a_far, a_far_sib, k_loc, v_loc, q_loc, tiles, *weights, Far(hidden_in)),
        12,
        3.0,
        copies=1,
    )
    kb, vb, eb, ctx_b, rinv_b, hid_b = call(
        functools.partial(attention_kernel, False),
        [
            proj, proj, ((pairs, 2 * shard, keys), BF16),
            ((pairs, shard, lanes), F32), ((pairs, shard, lanes), F32), ((shard, width), F32),
        ],
        (own, sib, b_far, b_far_sib, k_loc, v_loc, q_loc, tiles, *weights),
        12,
        3.0,
    )
    out, out_send, hidden_grad, low_grad, pack_m = call(
        functools.partial(middle_kernel, ranks),
        [
            ((rows, shard, width), BF16), ((1, shard, width), BF16), ((tokens, width), F32), ((tokens, width), BF16),
            ((8, width), F32),
        ],
        (
            hid_a, hid_b, cotangent, cot_far, win, wout, gain2, bd, bu, down_t, up, *expanded,
        ),
        20,
        12.0,
        [((tokens, width), BF16), ((tokens, hidden), BF16), ((tokens, hidden), BF16), ((2 * mid, width), F32)],
    )
    turned = [((pairs, lanes, keys), BF16)] * 2
    part_a, sib_part_a, pack_a, dctx_b = call(
        functools.partial(backward_kernel, True),
        [
            ((2, shard, width), F32), ((2, shard, width), BF16), ((8, width), F32), ((pairs, shard, lanes), BF16),
        ],
        (
            own, sib, a_far, a_far_sib, ctx_a, rinv_a, ea, k_loc, v_loc, q_loc, ka, va, qa,
            wq, wk, wv, wo, low_grad, pack_m,
        ),
        14,
        6.0,
        turned + [((pairs, 2 * shard, lanes), BF16)],
    )
    sib_a = exchange(sib_part_a, "seq", 1)
    part_b, far_part, sib_part_b, pack = call(
        functools.partial(backward_kernel, False),
        [((1, shard, width), F32), ((1, shard, width), BF16), ((2, shard, width), BF16), ((8, width), F32)],
        (
            own, sib, b_far, b_far_sib, ctx_b, rinv_b, eb, k_loc, v_loc, q_loc, kb, vb,
            wq, wk, wv, dctx_b, pack_a,
        ),
        14,
        3.6,
        turned,
    )
    sib_part_b, sib_a = lax.optimization_barrier((sib_part_b, sib_a))
    sib_b = exchange(sib_part_b, "seq", 1)
    sib_a, pack = lax.optimization_barrier((sib_a, pack))
    (back,) = call(
        return_kernel,
        [((2, shard, width), BF16)],
        (a_far, part_a, sib_a, out_send, hidden_grad, gain1),
        16,
        0.5,
    )
    back = exchange(back, "seq", 2)
    (far_sum,) = call(far_sum_kernel, [((1, shard, width), BF16)], (far_part, sib_b), 8, 0.2)
    far_sum = exchange(far_sum, "seq", 2)
    (pack,) = call(add_kernel, [((8, width), F32)], (pack, exchange(pack, "seq", 2)), 4, 10.0)
    first, second, third = (exchange(pack, "batch", k) for k in (1, 2, 3))
    pack = (pack + first) + (second + third)
    bit = 4
    while 2 * bit < lax.axis_size("batch"):
        pack = pack + exchange(pack, "batch", bit)
        bit *= 2
    pack = pack + exchange(pack, "seq", 1)
    far_pack = exchange(pack, "batch", bit)
    rowed = ((rows, shard, width), BF16)
    output, grad_input, mark = call(
        own_rows_kernel, [rowed, rowed, ((8, 128), F32)], (own, part_a, sib_a, hidden_grad, gain1, out, back), 16, 0.0, last=True
    )
    (grad_input,) = call(
        last_kernel,
        [rowed],
        (own, part_b, sib_b, hidden_grad, gain1, far_sum, Far(grad_input)),
        16,
        1.0,
        [((shard, width), BF16)],
        copies=1,
        last=True,
        aliases={6: 0},
    )
    grads = call(
        functools.partial(unpack_kernel, ranks, mid),
        [
            ((width,), F32), ((width,), F32), ((ranks, ranks, ranks), F32), ((ranks, outer), F32),
            ((ranks, inner), F32), ((ranks, inner), F32), ((ranks, outer), F32), ((mid,), F32), ((width,), F32),
        ],
        (pack, far_pack, Far(mark)),
        8,
        0.5,
        last=True,
    )
    return (output, grad_input, *grads)


def solution(mesh):
    rows = P("batch", "seq", None)
    in_specs = (rows, rows, P("batch", "seq")) + (P(),) * 17
    out_specs = (rows, rows) + (P(),) * 9
    return jax.shard_map(shards, mesh=mesh, in_specs=in_specs, out_specs=out_specs, check_vma=False)
```

```python
import functools

import jax
import jax.numpy as jnp
from jax import lax
from jax.experimental import pallas as pl
from jax.experimental.pallas import tpu as pltpu
from jax.sharding import PartitionSpec as P

F32 = jnp.float32
BF16 = jnp.bfloat16
HI = lax.Precision.HIGHEST
epsilon = 1e-06
masked = -1e30
gelu_a = 0.7978845608028654
gelu_b = 0.044715
MIB = 1024 * 1024
VM = pl.BlockSpec(memory_space=pltpu.VMEM)


def dot(a, b, precision=None):
    return lax.dot_general(a, b, (((1,), (0,)), ((), ())), precision=precision, preferred_element_type=F32)


def dot_nt(a, b, precision=None):
    return lax.dot_general(a, b, (((1,), (1,)), ((), ())), precision=precision, preferred_element_type=F32)


def dot_tn(a, b, precision=None):
    return lax.dot_general(a, b, (((0,), (0,)), ((), ())), precision=precision, preferred_element_type=F32)


def iota(shape, axis):
    return lax.broadcasted_iota(jnp.int32, shape, axis)


def block_of(index, size, count):
    total = jnp.zeros_like(index)
    for k in range(1, count):
        total = total + (index >= k * size).astype(jnp.int32)
    return total


def gelu_pair(v):
    square = v * v
    h = 0.5 + 0.5 * jnp.tanh(v * (gelu_a + gelu_a * gelu_b * square))
    g = v * h
    slope = h + (g - g * h) * (2.0 * gelu_a + 6.0 * gelu_a * gelu_b * square)
    return g, slope


def inverse_rms(x):
    return lax.rsqrt(jnp.mean(x * x, -1, keepdims=True) + epsilon)


class Far:
    def __init__(self, value):
        self.value = value


def near(value):
    return pltpu.with_memory_space_constraint(value, pltpu.VMEM)


def call(kernel, outs, args, limit, micros, scratch=(), copies=0, last=False, aliases=()):
    specs = [pl.BlockSpec(memory_space=pl.ANY) if isinstance(a, Far) else VM for a in args]
    args = [pltpu.with_memory_space_constraint(a.value, pltpu.HBM) if isinstance(a, Far) else near(a) for a in args]
    scratch = [pltpu.VMEM(shape, kind) for shape, kind in scratch]
    if copies:
        scratch.append(pltpu.SemaphoreType.DMA((copies,)))
    made = jax.ShapeDtypeStruct if last else pltpu.VMEM
    return pl.pallas_call(
        kernel,
        out_shape=[made(shape, kind) for shape, kind in outs],
        in_specs=specs,
        out_specs=[pl.BlockSpec(memory_space=pl.ANY if aliases else pltpu.VMEM)] * len(outs),
        input_output_aliases=dict(aliases),
        scratch_shapes=scratch,
        compiler_params=pltpu.CompilerParams(vmem_limit_bytes=limit * MIB),
        cost_estimate=pl.CostEstimate(flops=int(micros * 1.1e9), bytes_accessed=0, transcendentals=0),
    )(*args)


def start_copies(pairs, sems):
    started = [pltpu.make_async_copy(source, target, sems.at[k]) for k, (source, target) in enumerate(pairs)]
    for one in started:
        one.start()
    return started


def pick_kernel(inputs, cotangent, segment_ids, own, a_send, b_send, cot_send, ids, sems):
    rows, shard, width = inputs.shape
    extra = own.shape[1] - shard
    row = moved_row(rows)
    other = rows - 1 - row
    body = pl.ds(0, shard)
    started = start_copies(
        [
            (segment_ids, ids),
            (inputs.at[other], a_send.at[0, body]),
            (inputs.at[1], b_send.at[0, body]),
            (inputs.at[row], own.at[0, body]),
            (inputs.at[1], own.at[1, body]),
            (cotangent.at[other], cot_send.at[0]),
        ],
        sems,
    )
    started[0].wait()
    for target, k, source in ((own, 0, row), (own, 1, 1), (a_send, 0, other), (b_send, 0, 1)):
        line = jnp.broadcast_to(ids[pl.ds(source, 1), :].astype(F32).astype(BF16), (extra, shard))
        target[k, shard:, :] = jnp.zeros((extra, width), BF16)
        target[k, shard:, 0:shard] = line
    for one in started[1:]:
        one.wait()


def setup_kernel(
    shard, parts, table_far, position_far, shared_far, dl_far, dr_far, ul_far, ur_far, bd_far, bu_far, g1_far, g2_far,
    wq_far, wk_far, wv_far, wo_far, wout_far,
    tiles, down_t, up, mix, side, left, bd, bu, g1, g2, wq, wk, wv, wo, wout,
    tab, sh16, sh16t, table, position_bias, shared, dl, dr, ul, ur, sems,
):
    started = start_copies(
        [
            (table_far, table), (position_far, position_bias), (shared_far, shared), (dl_far, dl), (dr_far, dr),
            (ul_far, ul), (ur_far, ur), (bd_far, bd), (bu_far, bu), (g1_far, g1), (g2_far, g2),
            (wq_far, wq), (wk_far, wk), (wv_far, wv), (wo_far, wo), (wout_far, wout),
        ],
        sems,
    )
    for one in started[:11]:
        one.wait()
    heads = position_bias.shape[0]
    ranks, (mid, width) = shared.shape[0], down_t.shape
    inner, outer = mid // ranks, width // ranks
    square = ranks * ranks
    hits = (table[...][None, :] == iota((position_bias.shape[1], table.shape[0]), 0)).astype(F32)
    tab[0:heads, 0 : table.shape[0]] = dot(position_bias[...], hits, HI)
    for k in range(2 * parts - 1):
        for h in range(heads):
            line = tab[h : h + 1, k * shard : (k + 2) * shard]
            turned = pltpu.roll(jnp.broadcast_to(line, (shard, 2 * shard)), shard + 1, 1, stride=1, stride_axis=0)
            tiles[k, h // 2, (h % 2) * shard : (h % 2 + 1) * shard, :] = turned[:, :shard]
    eye = (iota((ranks, ranks), 0) == iota((ranks, ranks), 1)).astype(F32)
    for i in range(ranks):
        block = shared[i]
        sh16[i * ranks : (i + 1) * ranks, :] = block
        sh16t[i * ranks : (i + 1) * ranks, :] = dot_tn(block, eye, HI)
    spread, by_c, by_j, by_b, own_block = selectors(ranks, mid, width)
    mix[...] = jnp.zeros(mix.shape, F32)
    side[...] = jnp.zeros(side.shape, F32)
    shx, shtx = dot(sh16[...], by_c, HI), dot(sh16t[...], by_c, HI)
    drx, ulx = dot(dot(spread, dr[...], HI), by_j, HI), dot(dot(spread, ul[...], HI), by_j, HI)
    dlx = dot(dot(spread, dl[...], HI), by_b, HI) * own_block
    urx = dot(dot(spread, ur[...], HI), by_b, HI) * own_block
    mix[:square, :mid] = shx
    mix[square:, mid:] = shtx
    side[:square, :mid] = drx
    side[square:, mid:] = ulx
    left[:square, :] = dlx
    left[square:, :] = urx
    down_t[...] = dot_tn(shx * drx, dlx, HI).astype(BF16)
    up[...] = dot_tn(shtx * ulx, urx, HI).astype(BF16)
    for one in started[11:]:
        one.wait()


def selectors(ranks, mid, width):
    inner, outer, square = mid // ranks, width // ranks, ranks * ranks
    spread = (block_of(iota((square, ranks), 0), ranks, ranks) == iota((square, ranks), 1)).astype(F32)
    by_c = (block_of(iota((ranks, mid), 1), inner, ranks) == iota((ranks, mid), 0)).astype(F32)
    column = iota((inner, mid), 1)
    by_j = (column - inner * block_of(column, inner, ranks) == iota((inner, mid), 0)).astype(F32)
    column = iota((outer, width), 1)
    by_b = (column - outer * block_of(column, outer, ranks) == iota((outer, width), 0)).astype(F32)
    line = iota((square, width), 0)
    own_block = (
        line - ranks * block_of(line, ranks, ranks) == block_of(iota((square, width), 1), outer, ranks)
    ).astype(F32)
    return spread, by_c, by_j, by_b, own_block


def moved_row(rows):
    half = lax.axis_size("seq") // 2
    return jnp.where(lax.axis_index("seq") < half, 0, rows - 1)


def normed(x, gain):
    x = x.astype(F32)
    return (x * inverse_rms(x) * gain[...][None, :]).astype(BF16)


def project(x, weight, target, at):
    pairs, _, lanes = target.shape
    count = x.shape[0]
    for t in range(pairs // 2):
        result = dot(x, weight[:, 2 * t * lanes : (2 * t + 2) * lanes]).astype(BF16)
        target[2 * t, at : at + count, :] = result[:, :lanes]
        target[2 * t + 1, at : at + count, :] = result[:, lanes:]


def local_kernel(own, sib, wq, wk, wv, gain, k_loc, v_loc, q_loc):
    shard = q_loc.shape[1] // 2
    blocks = [normed(x, gain) for x in (own[0, :shard], sib[0, :shard], own[1, :shard], sib[1, :shard])]
    x = jnp.concatenate(blocks, 0)
    project(x, wk, k_loc, 0)
    project(x, wv, v_loc, 0)
    project(jnp.concatenate([blocks[0], blocks[2]], 0), wq, q_loc, 0)


def segment_features(blocks, shard, lanes):
    lane = iota((shard, lanes), 1)
    keys, queries = [], []
    for block in blocks:
        line = block[shard : shard + 1, 0:shard].astype(F32)
        same = lane.astype(F32) == jnp.transpose(jnp.broadcast_to(line, (lanes, shard)))
        keys.append(same.astype(F32).astype(BF16))
        queries.append(jnp.where((lane < 3) & jnp.logical_not(same), masked, 0.0).astype(BF16))
    return jnp.concatenate(keys, 0), queries


def halves(lanes):
    low = iota((1, lanes), 1) < lanes // 2
    low_lane = low.astype(F32).astype(BF16)
    return low, low_lane, 1.0 - low_lane


def attention_kernel(
    is_moved, own, sib, far, far_sib, k_loc, v_loc, q_loc, tiles,
    wq, wk, wv, wo, gain, *rest,
):
    pairs, _, lanes = k_loc.shape
    shard = q_loc.shape[1] // 2
    if is_moved:
        win_far, k_rem, v_rem, q_rem, e, ctx, rinv, hid, win, sems = rest
        fetches = start_copies([(win_far, win)], sems)
        first, queries = 0, [0, 2]
    else:
        k_rem, v_rem, e, ctx, rinv, hid = rest
        fetches = []
        first, queries = 1, [0]
    place = lax.axis_index("seq")
    parts = lax.axis_size("seq")
    far_low = normed(far[0, :shard], gain)
    x = jnp.concatenate([far_low, normed(far_sib[0, :shard], gain)], 0)
    project(x, wk, k_rem, 0)
    project(x, wv, v_rem, 0)
    if is_moved:
        project(far_low, wq, q_rem, 0)
    key_feature, query_feature = segment_features(
        (own.at[first], sib.at[first], far.at[0], far_sib.at[0]), shard, lanes
    )
    local = slice(2 * first * shard, 2 * (first + 1) * shard)
    contexts = [[] for _ in queries]
    low, low_lane, high_lane = halves(lanes)
    for p in range(pairs):
        keys = jnp.concatenate([k_loc[p, local, :], k_rem[p]], 0)
        values = jnp.concatenate([v_loc[p, local, :], v_rem[p]], 0)
        lefts, biases = [], []
        for block in queries:
            q = q_rem[p] if block == 2 else q_loc[p, first * shard : (first + 1) * shard, :]
            feature = query_feature[block]
            lefts.append(jnp.concatenate([q * low_lane, feature], 1))
            lefts.append(jnp.concatenate([q * high_lane, feature], 1))
            at = jnp.bitwise_xor(place, block)
            biases.append(
                jnp.concatenate([tiles[jnp.bitwise_xor(place, k) - at + parts - 1, p] for k in range(parts)], 1)
            )
        scores = dot_nt(jnp.concatenate(lefts, 0), jnp.concatenate([keys, key_feature], 1))
        scores = scores + jnp.concatenate(biases, 0)
        weights = jnp.exp(scores - jnp.max(scores, 1, keepdims=True)).astype(BF16)
        both = dot(weights, jnp.concatenate([values, jnp.ones(values.shape, BF16)], 1))
        scale = 1.0 / both[:, lanes:]
        mixed = both[:, :lanes] * scale
        for b in range(len(queries)):
            one = slice(2 * b * shard, (2 * b + 1) * shard)
            two = slice((2 * b + 1) * shard, (2 * b + 2) * shard)
            span = slice(b * shard, (b + 1) * shard)
            e[b * pairs + p] = weights[2 * b * shard : 2 * (b + 1) * shard]
            kept = jnp.where(low, mixed[one], mixed[two])
            ctx[p, span, :] = kept
            rinv[p, span, :] = jnp.where(low, scale[one], scale[two])
            contexts[b].append(kept.astype(BF16))
    context = jnp.concatenate([jnp.concatenate(c, 1) for c in contexts], 0)
    x = jnp.concatenate([own[first, :shard]] + ([far[0, :shard]] if is_moved else []), 0).astype(F32)
    hid[...] = x + dot(context, wo[...])
    for one in fetches:
        one.wait()


def middle_kernel(
    ranks, hid_a, hid_b, cot, cot_far, win, wout, gain2, bd, bu, down_t, up, mix, side, left,
    out, out_send, hidden_grad, low_grad, pack, low, act, gslope, adapter_grad,
):
    rows, shard, width = cot.shape
    hidden = win.shape[1]
    state = jnp.concatenate([hid_a[...], hid_b[...]], 0)
    inv2 = inverse_rms(state)
    low[...] = (state * inv2 * gain2[...][None, :]).astype(BF16)
    chunk = width // 3
    for j in range(hidden // chunk):
        cols = slice(j * chunk, (j + 1) * chunk)
        g, slope = gelu_pair(dot(low[...], win[:, cols]))
        gslope[:, cols] = slope.astype(BF16)
        act[:, cols] = g.astype(BF16)
    branch = dot(act[...], wout[...])
    row = moved_row(rows)
    branch_low = branch.astype(BF16)
    g, slope = gelu_pair(dot_nt(branch_low, down_t[...]) + bd[...][None, :])
    g_low = g.astype(BF16)
    up_low = jnp.concatenate([cot[row], cot_far[0], cot[1]], 0)
    upstream = up_low.astype(F32)
    gb = dot_nt(up_low, up[...]) * slope
    gb_low = gb.astype(BF16)
    low[...] = (upstream + dot(gb_low, down_t[...])).astype(BF16)
    result = state + branch + dot(g_low, up[...]) + bu[...][None, :]
    for b in range(rows):
        out[b] = result[b * shard : (b + 1) * shard].astype(BF16)
    out_send[0] = result[shard : 2 * shard].astype(BF16)
    mid = g.shape[1]
    adapter_grad[:mid, :] = dot_tn(gb_low, branch_low)
    adapter_grad[mid:, :] = dot_tn(g_low, up_low)
    grad2 = jnp.zeros((rows * shard, width), F32)
    chunk = width
    for j in range(hidden // chunk):
        cols = slice(j * chunk, (j + 1) * chunk)
        pre = (dot_nt(low[...], wout[cols, :]) * gslope[:, cols].astype(F32)).astype(BF16)
        if j == 1:
            pack_small(ranks, adapter_grad, mix, side, left, pack)
        grad2 = grad2 + dot_nt(pre, win[:, cols])
    state = jnp.concatenate([hid_a[...], hid_b[...]], 0)
    inv2 = inverse_rms(state)
    hat2 = state * inv2
    c = grad2 * gain2[...][None, :]
    total = upstream + inv2 * (c - hat2 * jnp.mean(hat2 * c, -1, keepdims=True))
    hidden_grad[...] = total
    low_grad[...] = total.astype(BF16)
    pack[1:2, :] = jnp.sum(grad2 * hat2, 0, keepdims=True)
    pack[2:3, :] = jnp.sum(upstream, 0, keepdims=True)
    pack[3:4, 0:mid] = jnp.sum(gb, 0, keepdims=True)


def backward_kernel(
    is_moved, own, sib, far, far_sib, ctx, rinv, e, k_loc, v_loc, q_loc, k_rem, v_rem, *rest,
):
    pairs, _, lanes = k_loc.shape
    shard, width = q_loc.shape[1] // 2, pairs * lanes
    if is_moved:
        q_rem, wq, wk, wv, wo, low_grad, pack_in, own_part, sib_part, pack, dctx_b, dkt, dvt, dctx = rest
        first, blocks = 0, 2
        for t in range(pairs // 2):
            part = dot_nt(low_grad[...], wo[2 * t * lanes : (2 * t + 2) * lanes, :]).astype(BF16)
            for k in range(2):
                dctx[2 * t + k] = part[: 2 * shard, k * lanes : (k + 1) * lanes]
                dctx_b[2 * t + k] = part[2 * shard :, k * lanes : (k + 1) * lanes]
    else:
        wq, wk, wv, dctx, pack_in, own_part, far_part, sib_part, pack, dkt, dvt = rest
        first, blocks = 1, 1
    low, low_lane, high_lane = halves(lanes)
    low_row = (iota((lanes, 1), 0) < lanes // 2).astype(F32).astype(BF16)
    high_row = 1.0 - low_row
    local = slice(2 * first * shard, 2 * (first + 1) * shard)
    query_grads = [[] for _ in range(blocks)]

    def prepare(p):
        lefts, deltas, turned_q, turned_s = [], [], [], []
        for b in range(blocks):
            span = slice(b * shard, (b + 1) * shard)
            scaled = dctx[p, span, :].astype(F32) * rinv[p, span, :]
            product = scaled * ctx[p, span, :]
            deltas.append(jnp.sum(jnp.where(low, product, 0.0), 1, keepdims=True))
            deltas.append(jnp.sum(jnp.where(low, 0.0, product), 1, keepdims=True))
            scaled = scaled.astype(BF16)
            lefts += [scaled * low_lane, scaled * high_lane]
            q = q_rem[p] if b == 1 else q_loc[p, first * shard : (first + 1) * shard, :]
            q_t, s_t = jnp.transpose(q), jnp.transpose(scaled)
            turned_q += [q_t * low_row, q_t * high_row]
            turned_s += [s_t * low_row, s_t * high_row]
        weights = jnp.concatenate([e[b * pairs + p] for b in range(blocks)], 0)
        values = jnp.concatenate([v_loc[p, local, :], v_rem[p]], 0)
        slopes = dot_nt(jnp.concatenate(lefts, 0), values) - jnp.concatenate(deltas, 0)
        steep = weights * slopes.astype(BF16)
        return jnp.concatenate(turned_q, 1), jnp.concatenate(turned_s, 1), weights, steep

    prepared = [prepare(p) for p in range(pairs)]
    for p, (turned_q, turned_s, weights, steep) in enumerate(prepared):
        keys = jnp.concatenate([k_loc[p, local, :], k_rem[p]], 0)
        grad_q = dot(steep, keys)
        for b in range(blocks):
            one = grad_q[2 * b * shard : (2 * b + 1) * shard]
            two = grad_q[(2 * b + 1) * shard : (2 * b + 2) * shard]
            query_grads[b].append(jnp.where(low, one, two).astype(BF16))
        dkt[p] = dot(turned_q, steep).astype(BF16)
        dvt[p] = dot(turned_s, weights).astype(BF16)
    keys = dkt.shape[2]
    key_t = dkt[...].reshape(width, keys)
    value_t = dvt[...].reshape(width, keys)
    part = jnp.transpose(dot(wk[...], key_t) + dot(wv[...], value_t))
    from_q = dot_nt(jnp.concatenate([jnp.concatenate(g, 1) for g in query_grads], 0), wq[...])
    pieces = [part[k * shard : (k + 1) * shard] for k in range(4)]
    pieces[0] = pieces[0] + from_q[:shard]
    if is_moved:
        pieces[2] = pieces[2] + from_q[shard:]
    gain = jnp.zeros((1, width), F32)
    for piece, x in zip(pieces, (own[first], sib[first], far[0], far_sib[0])):
        x = x[:shard].astype(F32)
        gain = gain + jnp.sum(piece * (x * inverse_rms(x)), 0, keepdims=True)
    pack[...] = pack_in[...]
    pack[0:1, :] = pack_in[0:1, :] + gain
    if is_moved:
        own_part[0] = pieces[0]
        own_part[1] = pieces[2]
    else:
        own_part[0] = pieces[0]
        far_part[0] = pieces[2].astype(BF16)
    sib_part[0, :shard] = pieces[1].astype(BF16)
    sib_part[1, :shard] = pieces[3].astype(BF16)


def pack_small(ranks, grads, mix, side, left, pack):
    mid, width = grads.shape[0] // 2, grads.shape[1]
    inner, outer, square = mid // ranks, width // ranks, ranks * ranks
    line = iota((2 * square, width), 0)
    line = line - ranks * block_of(line, ranks, 2 * ranks)
    own_block = (line == block_of(iota((2 * square, width), 1), outer, ranks)).astype(F32)
    factor = block_of(iota((2 * ranks, 2 * square), 1), ranks, 2 * ranks)
    spread = (factor == iota((2 * ranks, 2 * square), 0)).astype(F32)
    column = iota((outer, width), 1)
    by_b = (column - outer * block_of(column, outer, ranks) == iota((outer, width), 0)).astype(F32)
    group = block_of(iota((2 * ranks, 2 * mid), 1), inner, 2 * ranks)
    by_c = (group == iota((2 * ranks, 2 * mid), 0)).astype(F32)
    column = iota((2 * inner, 2 * mid), 1)
    place = column - inner * block_of(column, inner, 2 * ranks) + inner * (column >= mid).astype(jnp.int32)
    by_j = (place == iota((2 * inner, 2 * mid), 0)).astype(F32)
    column = iota((2 * ranks, square), 1)
    major = block_of(column, ranks, ranks)
    minor = column - ranks * major
    row = iota((2 * ranks, square), 0)
    widen = jnp.where(row < ranks, (row == minor).astype(F32), (row - ranks == major).astype(F32))
    column = iota((2 * square, square), 1)
    major = block_of(column, ranks, ranks)
    minor = column - ranks * major
    row = iota((2 * square, square), 0)
    inside = row - ranks * block_of(row, ranks, 2 * ranks)
    keep = jnp.where(row < square, (inside == major).astype(F32), (inside == minor).astype(F32))
    grads = grads[...]
    product = dot_nt(left[...], grads)
    ends = dot_nt(dot(spread, dot(mix[...] * side[...], grads) * own_block), by_b)
    sides = dot_nt(dot(spread, product * mix[...]), by_j)
    core = dot(spread, dot(dot_nt(product * side[...], by_c), widen) * keep)
    pack[...] = jnp.zeros(pack.shape, F32)
    pack[4:8, 0:outer] = ends[:ranks]
    pack[4:8, 256 : 256 + outer] = ends[ranks:]
    pack[4:8, 512 : 512 + inner] = sides[:ranks, :inner]
    pack[4:8, 640 : 640 + inner] = sides[ranks:, inner:]
    pack[4:8, 704 : 704 + square] = core[:ranks] + core[ranks:]


def norm_back(x, grad, hidden_grad, gain):
    x = x.astype(F32)
    inv = inverse_rms(x)
    hat = x * inv
    c = grad * gain[...][None, :]
    return hidden_grad + inv * (c - hat * jnp.mean(hat * c, -1, keepdims=True))


def return_kernel(far, own_part, from_sib, far_part, from_sib_b, hidden_grad, gain, back):
    shard = back.shape[1]
    back[0] = (far_part[0].astype(F32) + from_sib_b[1, :shard].astype(F32)).astype(BF16)
    grad = own_part[1] + from_sib[1].astype(F32)
    back[1] = norm_back(far[0, :shard], grad, hidden_grad[shard : 2 * shard, :], gain).astype(BF16)


def own_rows_kernel(own, part_a, sib_a, hidden_grad, gain, out, output, grad_input, mark):
    mark[...] = jnp.zeros(mark.shape, F32)
    rows, shard, width = out.shape
    row = moved_row(rows)
    output[row] = out[0]
    output[1] = out[2]
    grad = part_a[0] + sib_a[0].astype(F32)
    grad_input[row] = norm_back(own[0, :shard], grad, hidden_grad[0:shard, :], gain).astype(BF16)


def last_kernel(own, part_b, sib_b, hidden_grad, gain, out_far, back, _, __, output, grad_input, grad_b, sems):
    rows, shard, width = output.shape
    other = rows - 1 - moved_row(rows)
    started = start_copies([(out_far.at[0], output.at[other]), (back.at[1], grad_input.at[other])], sems)
    grad = part_b[0] + sib_b[0].astype(F32) + back[0].astype(F32)
    grad_b[...] = norm_back(own[1, :shard], grad, hidden_grad[2 * shard :, :], gain).astype(BF16)
    own_copy = pltpu.make_async_copy(grad_b, grad_input.at[1], sems.at[2])
    own_copy.start()
    for one in (*started, own_copy):
        one.wait()


def unpack_kernel(ranks, mid, near_pack, far_pack, _, g1, g2, shared, dl, dr, ul, ur, bd, bu):
    width = near_pack.shape[1]
    pack = near_pack[...] + far_pack[...]
    inner, outer = mid // ranks, width // ranks
    g1[...] = pack[0]
    g2[...] = pack[1]
    bu[...] = pack[2]
    bd[...] = pack[3, 0:mid]
    dl[...] = pack[4:8, 0:outer]
    ur[...] = pack[4:8, 256 : 256 + outer]
    dr[...] = pack[4:8, 512 : 512 + inner]
    ul[...] = pack[4:8, 640 : 640 + inner]
    for k in range(ranks):
        shared[:, k, :] = pack[4:8, 704 + k * ranks : 704 + (k + 1) * ranks]


def add_kernel(a, b, c):
    c[...] = a[...] + b[...]


def exchange(value, axis, bit):
    count = lax.axis_size(axis)
    return lax.ppermute(value, axis, [(k, k ^ bit) for k in range(count)])


def shards(
    inputs, cotangent, segment_ids, bucket_table, position_bias, query_weight, key_weight, value_weight, out_weight,
    hidden_in, hidden_out, gain_first, gain_second, shared, down_left, down_right, up_left_vectors, up_right,
    bias_down, bias_up,
):
    rows, shard, width = inputs.shape
    heads = position_bias.shape[1]
    hidden = hidden_in.shape[1]
    parts = lax.axis_size("seq")
    ranks, mid = shared.shape[0], bias_down.shape[0]
    pairs, tokens, keys = heads // 2, rows * shard, shard * parts
    lanes = width // pairs
    inner, outer, square = mid // ranks, width // ranks, ranks * ranks
    padded = shard + 8

    own, a_send, b_send, cot_send = call(
        pick_kernel,
        [((2, padded, width), BF16), ((1, padded, width), BF16), ((1, padded, width), BF16), ((1, shard, width), BF16)],
        (Far(inputs), Far(cotangent), Far(segment_ids)),
        8,
        1.0,
        [((rows, shard), jnp.int32)],
        6,
    )
    a_far = exchange(a_send, "seq", 2)
    b_far = exchange(b_send, "seq", 2)
    cot_far = exchange(cot_send, "seq", 2)
    sib = exchange(own, "seq", 1)

    small = (
        bucket_table, jnp.transpose(position_bias), shared, down_left, down_right, up_left_vectors, up_right,
        bias_down, bias_up, gain_first, gain_second,
    )
    large = (query_weight, key_weight, value_weight, out_weight, hidden_out)
    tiles, down_t, up, *expanded = call(
        functools.partial(setup_kernel, shard, parts),
        [((2 * parts - 1, pairs, 2 * shard, shard), F32), ((mid, width), BF16), ((mid, width), BF16)]
        + [((2 * square, 2 * mid), F32)] * 2 + [((2 * square, width), F32)]
        + [(x.shape, x.dtype) for x in small[7:] + large],
        [Far(x) for x in small + large],
        8,
        20.0,
        [((16, 2 * keys), F32), ((square, ranks), F32), ((square, ranks), F32)]
        + [(x.shape, x.dtype) for x in small[:7]],
        len(small) + len(large),
    )
    bd, bu, gain1, gain2, wq, wk, wv, wo, wout = expanded[3:]
    expanded = expanded[:3]
    k_loc, v_loc, q_loc = call(
        local_kernel,
        [((pairs, 4 * shard, lanes), BF16), ((pairs, 4 * shard, lanes), BF16), ((pairs, 2 * shard, lanes), BF16)],
        (own, sib, wq, wk, wv, gain1),
        8,
        20.0,
    )
    a_far, k_loc = lax.optimization_barrier((a_far, k_loc))
    a_far_sib = exchange(a_far, "seq", 1)
    a_far_sib, b_far = lax.optimization_barrier((a_far_sib, b_far))
    b_far_sib = exchange(b_far, "seq", 1)
    proj = ((pairs, 2 * shard, lanes), BF16)
    weights = (wq, wk, wv, wo, gain1)
    ka, va, qa, ea, ctx_a, rinv_a, hid_a, win = call(
        functools.partial(attention_kernel, True),
        [
            proj, proj, ((pairs, shard, lanes), BF16), ((2 * pairs, 2 * shard, keys), BF16),
            ((pairs, 2 * shard, lanes), F32), ((pairs, 2 * shard, lanes), F32), ((2 * shard, width), F32),
            (hidden_in.shape, BF16),
        ],
        (own, sib, a_far, a_far_sib, k_loc, v_loc, q_loc, tiles, *weights, Far(hidden_in)),
        12,
        3.0,
        copies=1,
    )
    kb, vb, eb, ctx_b, rinv_b, hid_b = call(
        functools.partial(attention_kernel, False),
        [
            proj, proj, ((pairs, 2 * shard, keys), BF16),
            ((pairs, shard, lanes), F32), ((pairs, shard, lanes), F32), ((shard, width), F32),
        ],
        (own, sib, b_far, b_far_sib, k_loc, v_loc, q_loc, tiles, *weights),
        12,
        3.0,
    )
    out, out_send, hidden_grad, low_grad, pack_m = call(
        functools.partial(middle_kernel, ranks),
        [
            ((rows, shard, width), BF16), ((1, shard, width), BF16), ((tokens, width), F32), ((tokens, width), BF16),
            ((8, width), F32),
        ],
        (
            hid_a, hid_b, cotangent, cot_far, win, wout, gain2, bd, bu, down_t, up, *expanded,
        ),
        20,
        12.0,
        [((tokens, width), BF16), ((tokens, hidden), BF16), ((tokens, hidden), BF16), ((2 * mid, width), F32)],
    )
    turned = [((pairs, lanes, keys), BF16)] * 2
    part_a, sib_part_a, pack_a, dctx_b = call(
        functools.partial(backward_kernel, True),
        [
            ((2, shard, width), F32), ((2, shard, width), BF16), ((8, width), F32), ((pairs, shard, lanes), BF16),
        ],
        (
            own, sib, a_far, a_far_sib, ctx_a, rinv_a, ea, k_loc, v_loc, q_loc, ka, va, qa,
            wq, wk, wv, wo, low_grad, pack_m,
        ),
        14,
        6.0,
        turned + [((pairs, 2 * shard, lanes), BF16)],
    )
    sib_a = exchange(sib_part_a, "seq", 1)
    part_b, far_part, sib_part_b, pack = call(
        functools.partial(backward_kernel, False),
        [((1, shard, width), F32), ((1, shard, width), BF16), ((2, shard, width), BF16), ((8, width), F32)],
        (
            own, sib, b_far, b_far_sib, ctx_b, rinv_b, eb, k_loc, v_loc, q_loc, kb, vb,
            wq, wk, wv, dctx_b, pack_a,
        ),
        14,
        3.6,
        turned,
    )
    sib_part_b, sib_a = lax.optimization_barrier((sib_part_b, sib_a))
    sib_b = exchange(sib_part_b, "seq", 1)
    (back,) = call(
        return_kernel,
        [((2, shard, width), BF16)],
        (a_far, part_a, sib_a, far_part, sib_b, hidden_grad, gain1),
        16,
        0.5,
    )
    back = exchange(back, "seq", 2)
    out_far = exchange(out_send, "seq", 2)
    (pack,) = call(add_kernel, [((8, width), F32)], (pack, exchange(pack, "seq", 2)), 4, 10.0)
    first, second, third = (exchange(pack, "batch", k) for k in (1, 2, 3))
    pack = (pack + first) + (second + third)
    bit = 4
    while 2 * bit < lax.axis_size("batch"):
        pack = pack + exchange(pack, "batch", bit)
        bit *= 2
    pack = pack + exchange(pack, "seq", 1)
    far_pack = exchange(pack, "batch", bit)
    rowed = ((rows, shard, width), BF16)
    output, grad_input, mark = call(
        own_rows_kernel, [rowed, rowed, ((8, 128), F32)], (own, part_a, sib_a, hidden_grad, gain1, out), 16, 0.0, last=True
    )
    output, grad_input = call(
        last_kernel,
        [rowed, rowed],
        (own, part_b, sib_b, hidden_grad, gain1, out_far, back, Far(output), Far(grad_input)),
        16,
        1.0,
        [((shard, width), BF16)],
        copies=3,
        last=True,
        aliases={7: 0, 8: 1},
    )
    grads = call(
        functools.partial(unpack_kernel, ranks, mid),
        [
            ((width,), F32), ((width,), F32), ((ranks, ranks, ranks), F32), ((ranks, outer), F32),
            ((ranks, inner), F32), ((ranks, inner), F32), ((ranks, outer), F32), ((mid,), F32), ((width,), F32),
        ],
        (pack, far_pack, mark),
        8,
        0.5,
        last=True,
    )
    return (output, grad_input, *grads)


def solution(mesh):
    rows = P("batch", "seq", None)
    in_specs = (rows, rows, P("batch", "seq")) + (P(),) * 17
    out_specs = (rows, rows) + (P(),) * 9
    return jax.shard_map(shards, mesh=mesh, in_specs=in_specs, out_specs=out_specs, check_vma=False)
```
